32 devices in a mesh: dp: 4 (over z), row: 4 (over y, x), col: 2 (over core).
Axes of the slice: x: 2, y: 2, z: 4, core: 2. Of those that a mesh axis runs over, the one named last changes fastest.
Arguments:
- tokens: bfloat16 [4096, 2048], P(('dp', 'row'), 'col'), may hold values from -6 to 6
- cotangent: bfloat16 [4096, 2048], P(('dp', 'row'), 'col'), may hold values from -6 to 6
- seq_lengths: int32 [4, 3], P('dp'), may hold values from 0 to 896, as said below
- gains: float32 [4, 2048], replicated, may hold values from 0.4 to 6.5
- gain_mean: float32 [4, 2048], replicated, may hold values from -40 to 40
- gain_square: float32 [4, 2048], replicated, may hold values from 204.8 to 1638.4
- entry_weight: float32 [3, 2048, 2048], P(None, ('col', 'dp'), 'row'), may hold values from -0.125 to 0.125
- entry_mean: float32 [3, 2048, 2048], P(None, ('col', 'dp'), 'row'), may hold values from -40 to 40
- entry_square: float32 [3, 2048, 2048], P(None, ('col', 'dp'), 'row'), may hold values from 204.8 to 1638.4
- mixer_weight: float32 [2048, 2048], P(('row', 'dp'), 'col'), may hold values from -0.125 to 0.125
- mixer_mean: float32 [2048, 2048], P(('row', 'dp'), 'col'), may hold values from -80 to 80
- mixer_square: float32 [2048, 2048], P(('row', 'dp'), 'col'), may hold values from 819.2 to 6553.6
- expand_weight: float32 [2, 2048, 8192], P(None, ('col', 'dp'), 'row'), may hold values from -0.125 to 0.125
- expand_mean: float32 [2, 2048, 8192], P(None, ('col', 'dp'), 'row'), may hold values from -20 to 20
- expand_square: float32 [2, 2048, 8192], P(None, ('col', 'dp'), 'row'), may hold values from 51.2 to 409.6
- reduce_weight: float32 [8192, 2048], P(('row', 'dp'), 'col'), may hold values from -0.0625 to 0.0625
- reduce_mean: float32 [8192, 2048], P(('row', 'dp'), 'col'), may hold values from -80 to 80
- reduce_square: float32 [8192, 2048], P(('row', 'dp'), 'col'), may hold values from 819.2 to 6553.6
Outputs:
- layer_output: float32 [4096, 2048], P(('dp', 'row'), 'col')
- input_grad: float32 [4096, 2048], P(('dp', 'row'), 'col')
- gain_grad: float32 [4, 2048], replicated
- gain_momentum: float32 [4, 2048], replicated
- gain_variance: float32 [4, 2048], replicated
- gain_updated: float32 [4, 2048], replicated
- entry_grad: float32 [3, 2048, 2048], P(None, ('col', 'dp'), 'row')
- entry_momentum: float32 [3, 2048, 2048], P(None, ('col', 'dp'), 'row')
- entry_variance: float32 [3, 2048, 2048], P(None, ('col', 'dp'), 'row')
- entry_updated: float32 [3, 2048, 2048], P(None, ('col', 'dp'), 'row')
- mixer_grad: float32 [2048, 2048], P(('row', 'dp'), 'col')
- mixer_momentum: float32 [2048, 2048], P(('row', 'dp'), 'col')
- mixer_variance: float32 [2048, 2048], P(('row', 'dp'), 'col')
- mixer_updated: float32 [2048, 2048], P(('row', 'dp'), 'col')
- expand_grad: float32 [2, 2048, 8192], P(None, ('col', 'dp'), 'row')
- expand_momentum: float32 [2, 2048, 8192], P(None, ('col', 'dp'), 'row')
- expand_variance: float32 [2, 2048, 8192], P(None, ('col', 'dp'), 'row')
- expand_updated: float32 [2, 2048, 8192], P(None, ('col', 'dp'), 'row')
- reduce_grad: float32 [8192, 2048], P(('row', 'dp'), 'col')
- reduce_momentum: float32 [8192, 2048], P(('row', 'dp'), 'col')
- reduce_variance: float32 [8192, 2048], P(('row', 'dp'), 'col')
- reduce_updated: float32 [8192, 2048], P(('row', 'dp'), 'col')
The draws below stay inside these ranges and needn't reach their ends.
Inputs may be any that keep to these rules, and one draw needn't show every extreme that they name: `seq_lengths`: each group's 3 lengths sum to at most 1024; one of them, in a slot drawn from the seed, lies between 769 and 896, and equals 896 in some group; the others may be zero.
All inputs are finite; a program needn't handle non-finite values.
Results may differ from the reference program's by a relative error of at most 0.03.
Values may be sent and summed in bfloat16 or wider, within the bound.
No kernel may reach another device: no remote copies, remote signals or barrier semaphores. Data moves between devices by JAX's collectives and lax.ppermute only.
A program may use at most 192 MiB of HBM per device.

```python
import math
import jax
import jax.numpy as jnp
from jax import lax

D = 2048
H = 16
HD = 128
FF = 8192
TOK_GRP = 1024
SEQ_GRP = 3
STEP = 10
TOKENS = 4096
N_DP = 4


def draw_seq_lengths(key, part):
    key = jax.random.fold_in(key, 11)
    keys = jax.random.split(key, 5)
    eighth = TOK_GRP // 8
    longest = 6 * eighth + jax.random.randint(keys[0], (N_DP,), 1, eighth + 1)
    chosen = jax.random.randint(keys[1], (), 0, N_DP)
    longest = jnp.where(jnp.arange(N_DP) == chosen, 7 * eighth, longest)
    spare = TOK_GRP - longest
    first_other = jax.random.randint(keys[2], (N_DP,), 0, spare + 1)
    second_other = jax.random.randint(keys[3], (N_DP,), 0, spare - first_other + 1)
    placed = jax.random.randint(keys[4], (N_DP,), 0, 3)
    columns = jnp.arange(3)[None, :]
    others = columns - (columns > placed[:, None]).astype(jnp.int32)
    filler = jnp.where(others == 0, first_other[:, None], second_other[:, None])
    return jnp.where(columns == placed[:, None], longest[:, None], filler).astype(jnp.int32)


def draw_gains(key, part):
    key = jax.random.fold_in(key, 5)
    ramp = jnp.arange(D, dtype=jnp.float32) / (D - 1)
    wobble = jax.random.uniform(key, (4, D), jnp.float32, 0.8, 1.2)
    rising = 1.0 + 2.0 * ramp
    heads_part = 0.5 + ramp
    stacked = jnp.concatenate([jnp.broadcast_to(rising, (2, D)), jnp.broadcast_to(heads_part, (2, D))], 0)
    return stacked * wobble


def steps_of(stream_key, shape, cuts, least, high):
    def one(position, blocks):
        heights = jax.random.uniform(jax.random.fold_in(jax.random.fold_in(stream_key, 6), position), (blocks,), jnp.float32, least / len(cuts), high / len(cuts))
        return jnp.repeat(jnp.exp(heights), shape[position] // blocks).reshape((-1,) + (1,) * (len(shape) - position - 1))

    loudness = one(*cuts[0])
    for cut in cuts[1:]:
        loudness = loudness * one(*cut)
    return loudness


def scatter_about(stream_key, shape, scale, reach, shards=(), kind=jnp.bfloat16):
    drawn = scale * jax.random.normal(stream_key, shape, jnp.float32)
    if shards:
        drawn = drawn * steps_of(stream_key, shape, shards, -0.22, 0.18)
    return jnp.clip(drawn, -reach, reach).astype(kind)


def setup_inputs(seed: int = 0) -> dict:
    seeds = jax.random.split(jax.random.key(seed), 19)
    tokens = scatter_about(seeds[0], (TOKENS, D), 1.0, 6.0, ((0, 16), (1, 2)))
    cotangent = scatter_about(seeds[1], (TOKENS, D), 1.0, 6.0, ((0, 16), (1, 2)))
    seq_lengths = draw_seq_lengths(jax.random.fold_in(seeds[18], 71), 0)
    gains = draw_gains(jax.random.fold_in(seeds[18], 71), 0)
    gain_mean = scatter_about(seeds[4], (4, D), (0.11 * (TOK_GRP * N_DP) ** 0.5), 40.0, (), jnp.float32)
    gain_square = jnp.clip(jnp.exp(jax.random.uniform(seeds[5], (4, D), jnp.float32, math.log(204.8), math.log(1638.4))), 204.8, 1638.4)
    entry_weight = scatter_about(seeds[6], (3, D, D), D ** -0.5, 0.125, ((1, 8), (2, 4)), jnp.float32)
    entry_mean = scatter_about(seeds[7], (3, D, D), (0.11 * (TOK_GRP * N_DP) ** 0.5), 40.0, ((1, 8), (2, 4)), jnp.float32)
    entry_square = jnp.clip(jnp.exp(math.log(1638.4) - 2.0794415 * jax.random.uniform(seeds[8], (3, D, D), jnp.float32) ** steps_of(seeds[8], (3, D, D), ((1, 8), (2, 4)), -0.2, 0.2)), 204.8, 1638.4)
    mixer_weight = scatter_about(seeds[9], (D, D), D ** -0.5, 0.125, ((0, 16), (1, 2)), jnp.float32)
    mixer_mean = scatter_about(seeds[10], (D, D), (0.22 * (TOK_GRP * N_DP) ** 0.5), 80.0, ((0, 16), (1, 2)), jnp.float32)
    mixer_square = jnp.clip(jnp.exp(math.log(6553.6) - 2.0794415 * jax.random.uniform(seeds[11], (D, D), jnp.float32) ** steps_of(seeds[11], (D, D), ((0, 16), (1, 2)), -0.2, 0.2)), 819.2, 6553.6)
    expand_weight = scatter_about(seeds[12], (2, D, FF), D ** -0.5, 0.125, ((1, 8), (2, 4)), jnp.float32)
    expand_mean = scatter_about(seeds[13], (2, D, FF), (0.055 * (TOK_GRP * N_DP) ** 0.5), 20.0, ((1, 8), (2, 4)), jnp.float32)
    expand_square = jnp.clip(jnp.exp(math.log(409.6) - 2.0794415 * jax.random.uniform(seeds[14], (2, D, FF), jnp.float32) ** steps_of(seeds[14], (2, D, FF), ((1, 8), (2, 4)), -0.2, 0.2)), 51.2, 409.6)
    reduce_weight = scatter_about(seeds[15], (FF, D), FF ** -0.5, 0.0625, ((0, 16), (1, 2)), jnp.float32)
    reduce_mean = scatter_about(seeds[16], (FF, D), (0.22 * (TOK_GRP * N_DP) ** 0.5), 80.0, ((0, 16), (1, 2)), jnp.float32)
    reduce_square = jnp.clip(jnp.exp(math.log(6553.6) - 2.0794415 * jax.random.uniform(seeds[17], (FF, D), jnp.float32) ** steps_of(seeds[17], (FF, D), ((0, 16), (1, 2)), -0.2, 0.2)), 819.2, 6553.6)
    return dict(tokens=tokens, cotangent=cotangent, seq_lengths=seq_lengths, gains=gains, gain_mean=gain_mean, gain_square=gain_square, entry_weight=entry_weight, entry_mean=entry_mean, entry_square=entry_square, mixer_weight=mixer_weight, mixer_mean=mixer_mean, mixer_square=mixer_square, expand_weight=expand_weight, expand_mean=expand_mean, expand_square=expand_square, reduce_weight=reduce_weight, reduce_mean=reduce_mean, reduce_square=reduce_square)


@jax.custom_vjp
def low(v):
    return lax.optimization_barrier(v.astype(jnp.bfloat16)).astype(jnp.float32)

@jax.custom_vjp
def low_back(v):
    return v

def low_keep(v):
    return (low(v), None)

def low_pass(kept, grad):
    return (grad,)

def back_keep(v):
    return (v, None)

def back_low(kept, grad):
    return (low(grad),)
low.defvjp(low_keep, low_pass)
low_back.defvjp(back_keep, back_low)
NORM_EPSILON = 1e-06
ROPE_BASE = 500000.0
BETA_FIRST = 0.9
BETA_SECOND = 0.95
ADAM_EPSILON = 1e-08
WEIGHT_DECAY = 0.1
PRECISE = lax.Precision.HIGHEST

def matmul(left, right):
    return jnp.dot(left, right, precision=PRECISE)

def layout_info(lengths, extent):
    indices = jnp.arange(extent, dtype=jnp.int32)
    closing = jnp.cumsum(lengths).astype(jnp.int32)
    starts = closing - lengths.astype(jnp.int32)
    segment = lax.optimization_barrier(jnp.sum((indices[:, None] >= closing[None, :]).astype(jnp.int32), 1))
    member = segment[:, None] == jnp.arange(lengths.shape[0], dtype=jnp.int32)[None, :]
    anchor = lax.optimization_barrier(jnp.sum(jnp.where(member, starts[None, :], 0), 1))
    anchor = jnp.where(segment >= lengths.shape[0], closing[-1], anchor)
    return (segment, indices - anchor)

def rotary_tables(positions, width):
    half_width = width // 2
    freqs = ROPE_BASE ** (-jnp.arange(half_width, dtype=jnp.float32) * 2.0 / width)
    angles = positions.astype(jnp.float32)[:, None] * freqs[None, :]
    return (jnp.cos(angles), jnp.sin(angles))

def rotate(values, cosine, sine_table):
    half_width = values.shape[-1] // 2
    first = values[..., :half_width]
    second = values[..., half_width:]
    cos_wide = cosine[:, None, :]
    sin_wide = sine_table[:, None, :]
    return jnp.concatenate([first * cos_wide - second * sin_wide, second * cos_wide + first * sin_wide], -1)

def rms_scale(values):
    return lax.rsqrt(lax.optimization_barrier(jnp.mean(values * values, -1, keepdims=True)) + NORM_EPSILON)

def group_forward(inputs, lengths, gains, entry_low, mixer_low, expand_low, reduce_low):
    extent = inputs.shape[0]
    segment, positions = layout_info(lengths, extent)
    cosine, sine_table = rotary_tables(positions, HD)
    queries = low_back(matmul(inputs, entry_low[0]))
    key_rows = low_back(matmul(inputs, entry_low[1]))
    value_rows = low(low_back(matmul(inputs, entry_low[2])))
    queries = queries * rms_scale(queries) * gains[2]
    key_rows = key_rows * rms_scale(key_rows) * gains[3]
    queries = low(rotate(queries.reshape(extent, H, HD), cosine, sine_table))
    key_rows = low(rotate(key_rows.reshape(extent, H, HD), cosine, sine_table))
    value_rows = value_rows.reshape(extent, H, HD)
    indices = jnp.arange(extent, dtype=jnp.int32)
    allowed = (segment[:, None] == segment[None, :]) & (indices[None, :] <= indices[:, None])

    def one_head(operands):
        head_query, head_key, head_value = operands
        scores = low_back(matmul(head_query, head_key.T) * HD ** (-0.5))
        masked = jnp.where(allowed, scores, -1e+30)
        shares = jax.nn.softmax(masked, -1)
        return matmul(low(shares), head_value)
    attended = lax.map(jax.checkpoint(one_head), (queries.transpose(1, 0, 2), key_rows.transpose(1, 0, 2), value_rows.transpose(1, 0, 2)))
    attended = low(low_back(attended.transpose(1, 0, 2).reshape(extent, D)))
    branch = low_back(matmul(attended, mixer_low))
    hidden = inputs + branch * rms_scale(branch) * gains[0]
    lowered = low(hidden)
    gating = low_back(matmul(lowered, expand_low[0]))
    upward = low_back(matmul(lowered, expand_low[1]))
    product = low(jax.nn.silu(gating) * upward)
    second = low_back(matmul(product, reduce_low))
    return hidden + second * rms_scale(second) * gains[1]

def adam_step(weight, gradient, moment, square, step_rate, decay_rate):
    moment_new = BETA_FIRST * moment + (1.0 - BETA_FIRST) * gradient
    square_new = BETA_SECOND * square + (1.0 - BETA_SECOND) * gradient * gradient
    ratio = moment_new / (1.0 - BETA_FIRST ** STEP) / (jnp.sqrt(square_new / (1.0 - BETA_SECOND ** STEP)) + ADAM_EPSILON)
    return (moment_new, square_new, weight - step_rate * (ratio + decay_rate * weight))

def reference(tokens, cotangent, seq_lengths, gains, gain_mean, gain_square, entry_weight, entry_mean, entry_square, mixer_weight, mixer_mean, mixer_square, expand_weight, expand_mean, expand_square, reduce_weight, reduce_mean, reduce_square):
    inputs = tokens.astype(jnp.float32).reshape(N_DP, TOK_GRP, D)

    def forward(inputs, gains, entry_weight, mixer_weight, expand_weight, reduce_weight):
        entry_low = low(entry_weight)
        mixer_low = low(mixer_weight)
        expand_low = low(expand_weight)
        reduce_low = low(reduce_weight)

        def one_group(operands):
            return group_forward(operands[0], operands[1], gains, entry_low, mixer_low, expand_low, reduce_low)
        return lax.map(jax.checkpoint(one_group), (inputs, seq_lengths))
    outputs, pullback = jax.vjp(forward, inputs, gains, entry_weight, mixer_weight, expand_weight, reduce_weight)
    segments = jax.vmap(lambda lengths: layout_info(lengths, TOK_GRP)[0])(seq_lengths)
    valid = (segments < SEQ_GRP).astype(jnp.float32)
    upstream = cotangent.astype(jnp.float32).reshape(N_DP, TOK_GRP, D) * valid[:, :, None]
    input_grad, gain_grad, entry_grad, mixer_grad, expand_grad, reduce_grad = pullback(upstream)
    gain_momentum, gain_variance, gain_updated = adam_step(gains, gain_grad, gain_mean, gain_square, 1.0, 0.0)
    entry_momentum, entry_variance, entry_updated = adam_step(entry_weight, entry_grad, entry_mean, entry_square, 2.0 * D ** (-0.5), WEIGHT_DECAY)
    mixer_momentum, mixer_variance, mixer_updated = adam_step(mixer_weight, mixer_grad, mixer_mean, mixer_square, 2.0 * D ** (-0.5), WEIGHT_DECAY)
    expand_momentum, expand_variance, expand_updated = adam_step(expand_weight, expand_grad, expand_mean, expand_square, 2.0 * D ** (-0.5), WEIGHT_DECAY)
    reduce_momentum, reduce_variance, reduce_updated = adam_step(reduce_weight, reduce_grad, reduce_mean, reduce_square, 2.0 * FF ** (-0.5), WEIGHT_DECAY)
    return (outputs.reshape(TOKENS, D), input_grad.reshape(TOKENS, D), gain_grad, gain_momentum, gain_variance, gain_updated, entry_grad, entry_momentum, entry_variance, entry_updated, mixer_grad, mixer_momentum, mixer_variance, mixer_updated, expand_grad, expand_momentum, expand_variance, expand_updated, reduce_grad, reduce_momentum, reduce_variance, reduce_updated)
```

```python
import jax
import jax.numpy as jnp
from jax import lax
from jax.sharding import PartitionSpec as P

D = 2048
HD = 128
FF = 8192
STEP = 10


NORM_EPSILON = 1e-06
ROPE_BASE = 500000.0
BETA_FIRST = 0.9
BETA_SECOND = 0.95
ADAM_EPSILON = 1e-08
WEIGHT_DECAY = 0.1


def layout_info(lengths, indices):
    closing = jnp.cumsum(lengths)
    starts = closing - lengths
    segment = jnp.sum((indices[:, None] >= closing[None, :]).astype(jnp.int32), 1)
    member = segment[:, None] == jnp.arange(lengths.shape[0], dtype=jnp.int32)[None, :]
    anchor = jnp.sum(jnp.where(member, starts[None, :], 0), 1)
    anchor = jnp.where(segment >= lengths.shape[0], closing[-1], anchor)
    return (segment, indices - anchor)


def rotary_tables(positions, width):
    half_width = width // 2
    freqs = ROPE_BASE ** (-jnp.arange(half_width, dtype=jnp.float32) * 2.0 / width)
    angles = positions.astype(jnp.float32)[:, None] * freqs[None, :]
    return (jnp.cos(angles), jnp.sin(angles))


def rotate(values, cosine, sine_table):
    half_width = values.shape[-1] // 2
    first = values[..., :half_width]
    second = values[..., half_width:]
    cos_wide = cosine[:, None, :]
    sin_wide = sine_table[:, None, :]
    return jnp.concatenate(
        [first * cos_wide - second * sin_wide, second * cos_wide + first * sin_wide], -1
    )


def rotate_back(values, cosine, sine_table):
    half_width = values.shape[-1] // 2
    first = values[..., :half_width]
    second = values[..., half_width:]
    cos_wide = cosine[:, None, :]
    sin_wide = sine_table[:, None, :]
    return jnp.concatenate(
        [first * cos_wide + second * sin_wide, second * cos_wide - first * sin_wide], -1
    )


def adam_step(weight, gradient, moment, square, step_rate, decay_rate):
    moment_new = BETA_FIRST * moment + (1.0 - BETA_FIRST) * gradient
    square_new = BETA_SECOND * square + (1.0 - BETA_SECOND) * gradient * gradient
    ratio = (
        moment_new
        / (1.0 - BETA_FIRST**STEP)
        / (jnp.sqrt(square_new / (1.0 - BETA_SECOND**STEP)) + ADAM_EPSILON)
    )
    return (moment_new, square_new, weight - step_rate * (ratio + decay_rate * weight))


def swap(values, axis, distance):
    return lax.ppermute(values, axis, [(i, i ^ distance) for i in range(lax.axis_size(axis))])


def swap_col(values):
    return swap(values, "col", 1)


def feature_total(values):
    return values + swap_col(values)


def grid_total(values):
    values = feature_total(values)
    count = lax.axis_size("row")
    blocks = values.reshape(values.shape[0], count, -1)
    total = blocks
    for k in range(1, count):
        part = swap(blocks, "row", k)
        total = total + jnp.stack([part[:, j ^ k] for j in range(count)], 1)
    return total.reshape(values.shape)


def mesh_total(values):
    for axis in ("col", "row", "dp"):
        distance = 1
        while distance < lax.axis_size(axis):
            values = values + swap(values, axis, distance)
            distance *= 2
    return values


def gather_rows(block):
    return jnp.concatenate(
        [block] + [swap(block, "row", k) for k in range(1, lax.axis_size("row"))], 0
    )


def scatter_rows(partial_value):
    count = lax.axis_size("row")
    parts = partial_value.reshape(count, partial_value.shape[0] // count, -1)
    low = parts.astype(jnp.bfloat16)
    total = parts[0]
    for k in range(1, count):
        total = total + swap(low[k], "row", k).astype(jnp.float32)
    return total


def join_halves(own, axis):
    half = own.shape[axis]
    place = lax.axis_index("col") * half
    shape = list(own.shape)
    shape[axis] = 2 * half
    whole = lax.dynamic_update_slice_in_dim(jnp.zeros(shape, own.dtype), own, place, axis)
    return lax.dynamic_update_slice_in_dim(whole, swap_col(own), half - place, axis)


def split_halves(block, axis):
    half = block.shape[axis] // 2
    place = lax.axis_index("col") * half
    own = lax.dynamic_slice_in_dim(block, place, half, axis)
    return (own, swap_col(lax.dynamic_slice_in_dim(block, half - place, half, axis)))


def dot(equation, left, right):
    return jnp.einsum(equation, left, right, preferred_element_type=jnp.float32)


def on_device(
    tokens,
    cotangent,
    seq_lengths,
    gains,
    gain_mean,
    gain_square,
    entry_weight,
    entry_mean,
    entry_square,
    mixer_weight,
    mixer_mean,
    mixer_square,
    expand_weight,
    expand_mean,
    expand_square,
    reduce_weight,
    reduce_mean,
    reduce_square,
):
    entry_block, mixer_block, expand_block, reduce_block = (
        lax.all_gather(entry_weight.astype(jnp.bfloat16), "dp", axis=1, tiled=True),
        lax.all_gather(mixer_weight.astype(jnp.bfloat16), "dp", axis=0, tiled=True),
        lax.all_gather(expand_weight.astype(jnp.bfloat16), "dp", axis=1, tiled=True),
        lax.all_gather(reduce_weight.astype(jnp.bfloat16), "dp", axis=0, tiled=True),
    )
    row_size = lax.axis_size("row")
    col_size = lax.axis_size("col")
    local_rows = tokens.shape[0]
    feature_local = tokens.shape[1]
    extent = local_rows * row_size
    row_index = lax.axis_index("row")
    blocks = row_index ^ jnp.arange(row_size, dtype=jnp.int32)
    indices = (
        blocks[:, None] * local_rows + jnp.arange(local_rows, dtype=jnp.int32)[None, :]
    ).reshape(extent)
    segment, positions = layout_info(seq_lengths[0], indices)
    local_valid = (segment[:local_rows] < seq_lengths.shape[1]).astype(jnp.float32)
    head_width = entry_block.shape[2] // col_size
    head_start = (row_index * col_size + lax.axis_index("col")) * head_width
    col_start = lax.axis_index("col") * feature_local
    post_gain = lax.dynamic_slice_in_dim(gains[0:2], col_start, feature_local, 1)
    head_gain = lax.dynamic_slice_in_dim(gains[2:4], head_start, head_width, 1)
    head_count = head_width // HD
    shrink = HD ** (-0.5)
    inputs = tokens.astype(jnp.float32)
    token_rows = gather_rows(tokens)
    token_other = swap_col(token_rows)
    entry_own, entry_far = split_halves(entry_block, 2)
    projected = dot("td,kdf->ktf", token_rows, entry_own) + dot(
        "td,kdf->ktf", token_other, entry_far
    )
    squares = grid_total(jnp.sum(projected[0:2] * projected[0:2], -1))
    query_scale = lax.rsqrt(squares[0] / D + NORM_EPSILON)[:, None]
    key_scale = lax.rsqrt(squares[1] / D + NORM_EPSILON)[:, None]
    query_hat = projected[0] * query_scale
    key_hat = projected[1] * key_scale
    cosine, sine_table = rotary_tables(positions, HD)
    query_rot = rotate(
        (query_hat * head_gain[0]).reshape(extent, head_count, HD), cosine, sine_table
    ).astype(jnp.bfloat16)
    key_rot = rotate(
        (key_hat * head_gain[1]).reshape(extent, head_count, HD), cosine, sine_table
    ).astype(jnp.bfloat16)
    value_rows = projected[2].astype(jnp.bfloat16).reshape(extent, head_count, HD)
    block_rows = min(512, extent)

    def block_scores(offset):
        query_block = query_rot[offset : offset + block_rows]
        scores = (
            jnp.einsum("qhd,khd->hqk", query_block, key_rot, preferred_element_type=jnp.float32)
            * shrink
        )
        rows_here = indices[offset : offset + block_rows]
        allowed = (segment[offset : offset + block_rows][:, None] == segment[None, :]) & (
            indices[None, :] <= rows_here[:, None]
        )
        return (query_block, jnp.where(allowed[None], scores, -1e30))

    outputs = []
    logsums = []
    for offset in range(0, extent, block_rows):
        query_block, masked = block_scores(offset)
        peak = jnp.max(masked, -1, keepdims=True)
        expo = jnp.exp(masked - peak)
        totals = jnp.sum(expo, -1, keepdims=True)
        shares = (expo / totals).astype(jnp.bfloat16)
        outputs.append(
            jnp.einsum("hqk,khd->qhd", shares, value_rows, preferred_element_type=jnp.float32)
        )
        logsums.append(peak + jnp.log(totals))
    attended = jnp.concatenate(outputs, 0).astype(jnp.bfloat16).reshape(extent, head_width)
    attended_cols = join_halves(attended, 1)
    branch = scatter_rows(dot("tf,fd->td", attended_cols, mixer_block))
    branch_scale = lax.rsqrt(feature_total(jnp.sum(branch * branch, -1)) / D + NORM_EPSILON)[
        :, None
    ]
    branch_hat = branch * branch_scale
    hidden = inputs + branch_hat * post_gain[0]
    hidden_rows = gather_rows(hidden.astype(jnp.bfloat16))
    hidden_other = swap_col(hidden_rows)
    expand_own, expand_far = split_halves(expand_block, 2)
    gated = dot("td,kdf->ktf", hidden_rows, expand_own) + dot(
        "td,kdf->ktf", hidden_other, expand_far
    )
    product = (jax.nn.silu(gated[0]) * gated[1]).astype(jnp.bfloat16)
    product_cols = join_halves(product, 1)
    second = scatter_rows(dot("tf,fd->td", product_cols, reduce_block))
    second_scale = lax.rsqrt(feature_total(jnp.sum(second * second, -1)) / D + NORM_EPSILON)[
        :, None
    ]
    second_hat = second * second_scale
    layer_output = hidden + second_hat * post_gain[1]
    upstream = cotangent.astype(jnp.float32) * local_valid[:, None]
    gain_second_post = jnp.sum(upstream * second_hat, 0)
    scaled = upstream * post_gain[1]
    inner_sum = feature_total(jnp.sum(scaled * second_hat, -1))
    second_grad = (second_scale * (scaled - second_hat * inner_sum[:, None] / D)).astype(
        jnp.bfloat16
    )
    second_rows = gather_rows(second_grad)
    second_other = swap_col(second_rows)
    reduce_sum = dot("tf,td->fd", product_cols, second_rows)
    reduce_own, reduce_far = split_halves(reduce_block, 0)
    product_grad = dot("td,fd->tf", second_rows, reduce_own) + dot(
        "td,fd->tf", second_other, reduce_far
    )
    sigmoid = jax.nn.sigmoid(gated[0])
    gate_grad = product_grad * gated[1] * sigmoid * (1.0 + gated[0] * (1.0 - sigmoid))
    up_grad = product_grad * jax.nn.silu(gated[0])
    gated_grad = join_halves(jnp.stack([gate_grad, up_grad]).astype(jnp.bfloat16), 2)
    hidden_back = scatter_rows(dot("ktw,kdw->td", gated_grad, expand_block))
    expand_sum = dot("td,ktw->kdw", hidden_rows, gated_grad)
    hidden_grad = upstream + hidden_back
    gain_first_post = jnp.sum(hidden_grad * branch_hat, 0)
    scaled = hidden_grad * post_gain[0]
    inner_sum = feature_total(jnp.sum(scaled * branch_hat, -1))
    branch_grad = (branch_scale * (scaled - branch_hat * inner_sum[:, None] / D)).astype(
        jnp.bfloat16
    )
    branch_rows = gather_rows(branch_grad)
    branch_other = swap_col(branch_rows)
    mixer_sum = dot("tf,td->fd", attended_cols, branch_rows)
    mixer_own, mixer_far = split_halves(mixer_block, 0)
    attended_grad = dot("td,fd->tf", branch_rows, mixer_own) + dot(
        "td,fd->tf", branch_other, mixer_far
    )
    attended_low = attended_grad.astype(jnp.bfloat16).reshape(extent, head_count, HD)
    query_parts = []
    key_accum = jnp.zeros((extent, head_count, HD), jnp.float32)
    value_accum = jnp.zeros((extent, head_count, HD), jnp.float32)
    for number, offset in enumerate(range(0, extent, block_rows)):
        query_block, masked = block_scores(offset)
        shares = jnp.exp(masked - logsums[number])
        grad_block = attended_low[offset : offset + block_rows]
        flow_grad = jnp.einsum(
            "qhd,khd->hqk", grad_block, value_rows, preferred_element_type=jnp.float32
        )
        row_delta = jnp.sum(shares * flow_grad, -1, keepdims=True)
        score_grad = (shares * (flow_grad - row_delta)).astype(jnp.bfloat16)
        query_parts.append(
            jnp.einsum("hqk,khd->qhd", score_grad, key_rot, preferred_element_type=jnp.float32)
            * shrink
        )
        key_accum = (
            key_accum
            + jnp.einsum(
                "hqk,qhd->khd", score_grad, query_block, preferred_element_type=jnp.float32
            )
            * shrink
        )
        value_accum = value_accum + jnp.einsum(
            "hqk,qhd->khd",
            shares.astype(jnp.bfloat16),
            grad_block,
            preferred_element_type=jnp.float32,
        )
    query_grad = rotate_back(jnp.concatenate(query_parts, 0), cosine, sine_table).reshape(
        extent, head_width
    )
    key_grad = rotate_back(key_accum, cosine, sine_table).reshape(extent, head_width)
    gain_query = jnp.sum(query_grad * query_hat, 0)
    gain_key = jnp.sum(key_grad * key_hat, 0)
    query_scaled = query_grad * head_gain[0]
    key_scaled = key_grad * head_gain[1]
    head_dots = grid_total(
        jnp.stack(
            [jnp.sum(query_scaled * query_hat, -1), jnp.sum(key_scaled * key_hat, -1)]
        )
    )
    query_raw = query_scale * (query_scaled - query_hat * head_dots[0][:, None] / D)
    key_raw = key_scale * (key_scaled - key_hat * head_dots[1][:, None] / D)
    value_grad = value_accum.reshape(extent, head_width)
    projected_grad = join_halves(
        jnp.stack([query_raw, key_raw, value_grad]).astype(jnp.bfloat16), 2
    )
    entry_back = scatter_rows(dot("ktw,kdw->td", projected_grad, entry_block))
    entry_sum = dot("td,ktw->kdw", token_rows, projected_grad)
    input_grad = hidden_grad + entry_back
    entry_grad, mixer_grad, expand_grad, reduce_grad = (
        lax.psum_scatter(
            entry_sum.astype(jnp.bfloat16), "dp", scatter_dimension=1, tiled=True
        ).astype(jnp.float32),
        lax.psum_scatter(
            mixer_sum.astype(jnp.bfloat16), "dp", scatter_dimension=0, tiled=True
        ).astype(jnp.float32),
        lax.psum_scatter(
            expand_sum.astype(jnp.bfloat16), "dp", scatter_dimension=1, tiled=True
        ).astype(jnp.float32),
        lax.psum_scatter(
            reduce_sum.astype(jnp.bfloat16), "dp", scatter_dimension=0, tiled=True
        ).astype(jnp.float32),
    )
    gain_local = jnp.zeros((4, D), jnp.float32)
    gain_local = lax.dynamic_update_slice(
        gain_local, jnp.stack([gain_first_post, gain_second_post]), (0, col_start)
    )
    gain_local = lax.dynamic_update_slice(
        gain_local, jnp.stack([gain_query, gain_key]), (2, head_start)
    )
    gain_grad = mesh_total(gain_local)
    gain_momentum, gain_variance, gain_updated = adam_step(
        gains, gain_grad, gain_mean, gain_square, 1.0, 0.0
    )
    entry_momentum, entry_variance, entry_updated = adam_step(
        entry_weight, entry_grad, entry_mean, entry_square, 2.0 * D ** (-0.5), WEIGHT_DECAY
    )
    mixer_momentum, mixer_variance, mixer_updated = adam_step(
        mixer_weight, mixer_grad, mixer_mean, mixer_square, 2.0 * D ** (-0.5), WEIGHT_DECAY
    )
    expand_momentum, expand_variance, expand_updated = adam_step(
        expand_weight, expand_grad, expand_mean, expand_square, 2.0 * D ** (-0.5), WEIGHT_DECAY
    )
    reduce_momentum, reduce_variance, reduce_updated = adam_step(
        reduce_weight, reduce_grad, reduce_mean, reduce_square, 2.0 * FF ** (-0.5), WEIGHT_DECAY
    )
    return (
        layer_output,
        input_grad,
        gain_grad,
        gain_momentum,
        gain_variance,
        gain_updated,
        entry_grad,
        entry_momentum,
        entry_variance,
        entry_updated,
        mixer_grad,
        mixer_momentum,
        mixer_variance,
        mixer_updated,
        expand_grad,
        expand_momentum,
        expand_variance,
        expand_updated,
        reduce_grad,
        reduce_momentum,
        reduce_variance,
        reduce_updated,
    )


def solution(mesh):
    placed = (
        P(("dp", "row"), "col"),
        P(("dp", "row"), "col"),
        P("dp", None),
        P(),
        P(),
        P(),
        P(None, ("col", "dp"), "row"),
        P(None, ("col", "dp"), "row"),
        P(None, ("col", "dp"), "row"),
        P(("row", "dp"), "col"),
        P(("row", "dp"), "col"),
        P(("row", "dp"), "col"),
        P(None, ("col", "dp"), "row"),
        P(None, ("col", "dp"), "row"),
        P(None, ("col", "dp"), "row"),
        P(("row", "dp"), "col"),
        P(("row", "dp"), "col"),
        P(("row", "dp"), "col"),
    )
    return jax.shard_map(
        on_device,
        mesh=mesh,
        in_specs=placed,
        out_specs=(
            P(("dp", "row"), "col"),
            P(("dp", "row"), "col"),
            P(),
            P(),
            P(),
            P(),
            P(None, ("col", "dp"), "row"),
            P(None, ("col", "dp"), "row"),
            P(None, ("col", "dp"), "row"),
            P(None, ("col", "dp"), "row"),
            P(("row", "dp"), "col"),
            P(("row", "dp"), "col"),
            P(("row", "dp"), "col"),
            P(("row", "dp"), "col"),
            P(None, ("col", "dp"), "row"),
            P(None, ("col", "dp"), "row"),
            P(None, ("col", "dp"), "row"),
            P(None, ("col", "dp"), "row"),
            P(("row", "dp"), "col"),
            P(("row", "dp"), "col"),
            P(("row", "dp"), "col"),
            P(("row", "dp"), "col"),
        ),
        check_vma=False,
    )
```

```python
import jax
import jax.numpy as jnp
from jax import lax
from jax.experimental import pallas as pl
from jax.experimental.pallas import tpu as pltpu
from jax.sharding import PartitionSpec as P

D = 2048
HD = 128
FF = 8192
STEP = 10


NORM_EPSILON = 1e-06
ROPE_BASE = 500000.0
BETA_FIRST = 0.9
BETA_SECOND = 0.95
ADAM_EPSILON = 1e-08
WEIGHT_DECAY = 0.1


def layout_info(lengths, indices):
    closing = jnp.cumsum(lengths)
    starts = closing - lengths
    segment = jnp.sum((indices[:, None] >= closing[None, :]).astype(jnp.int32), 1)
    member = segment[:, None] == jnp.arange(lengths.shape[0], dtype=jnp.int32)[None, :]
    anchor = jnp.sum(jnp.where(member, starts[None, :], 0), 1)
    anchor = jnp.where(segment >= lengths.shape[0], closing[-1], anchor)
    return (segment, indices - anchor)


def rotary_tables(positions, width):
    half_width = width // 2
    freqs = ROPE_BASE ** (-jnp.arange(half_width, dtype=jnp.float32) * 2.0 / width)
    angles = positions.astype(jnp.float32)[:, None] * freqs[None, :]
    return (jnp.cos(angles), jnp.sin(angles))


def rotate(values, cosine, sine_table):
    half_width = values.shape[-1] // 2
    first = values[..., :half_width]
    second = values[..., half_width:]
    cos_wide = cosine[:, None, :]
    sin_wide = sine_table[:, None, :]
    return jnp.concatenate(
        [first * cos_wide - second * sin_wide, second * cos_wide + first * sin_wide], -1
    )


def rotate_back(values, cosine, sine_table):
    half_width = values.shape[-1] // 2
    first = values[..., :half_width]
    second = values[..., half_width:]
    cos_wide = cosine[:, None, :]
    sin_wide = sine_table[:, None, :]
    return jnp.concatenate(
        [first * cos_wide + second * sin_wide, second * cos_wide - first * sin_wide], -1
    )


def adam_step(weight, gradient, moment, square, step_rate, decay_rate):
    moment_new = BETA_FIRST * moment + (1.0 - BETA_FIRST) * gradient
    square_new = BETA_SECOND * square + (1.0 - BETA_SECOND) * gradient * gradient
    ratio = (
        moment_new
        / (1.0 - BETA_FIRST**STEP)
        / (jnp.sqrt(square_new / (1.0 - BETA_SECOND**STEP)) + ADAM_EPSILON)
    )
    return (moment_new, square_new, weight - step_rate * (ratio + decay_rate * weight))


def swap(values, axis, distance):
    return lax.ppermute(values, axis, [(i, i ^ distance) for i in range(lax.axis_size(axis))])


def swap_col(values):
    return swap(values, "col", 1)


def feature_total(values):
    return values + swap_col(values)


def grid_total(values):
    values = feature_total(values)
    count = lax.axis_size("row")
    blocks = values.reshape(values.shape[0], count, -1)
    total = blocks
    for k in range(1, count):
        part = swap(blocks, "row", k)
        total = total + jnp.stack([part[:, j ^ k] for j in range(count)], 1)
    return total.reshape(values.shape)


def mesh_total(values):
    for axis in ("col", "row", "dp"):
        distance = 1
        while distance < lax.axis_size(axis):
            values = values + swap(values, axis, distance)
            distance *= 2
    return values


def gather_rows(block):
    return jnp.concatenate(
        [block] + [swap(block, "row", k) for k in range(1, lax.axis_size("row"))], 0
    )


def scatter_rows(own, low):
    for k in range(1, lax.axis_size("row")):
        own = own + swap(low[k - 1], "row", k).astype(jnp.float32)
    return own


VMEM = 48 * 1024 * 1024
TILE = 256
NN = (((1,), (0,)), ((), ()))
NT = (((1,), (1,)), ((), ()))
TN = (((0,), (0,)), ((), ()))


def mm(left, right, dims=NN):
    return lax.dot_general(left, right, dims, preferred_element_type=jnp.float32)


def run(body, grid, ins, outs):
    place = lax.axis_index("col").astype(jnp.int32).reshape(1)
    return pl.pallas_call(
        body,
        grid_spec=pltpu.PrefetchScalarGridSpec(
            num_scalar_prefetch=1,
            grid=grid,
            in_specs=[pl.BlockSpec(block, where) for _, block, where in ins],
            out_specs=[pl.BlockSpec(block, where) for _, _, block, where in outs],
        ),
        out_shape=[jax.ShapeDtypeStruct(shape, kind) for shape, kind, _, _ in outs],
        compiler_params=pltpu.CompilerParams(vmem_limit_bytes=VMEM),
        cost_estimate=pl.CostEstimate(flops=1, bytes_accessed=1, transcendentals=0),
    )(place, *[array for array, _, _ in ins])


def whole(array):
    zeros = (0,) * array.ndim
    return (array, array.shape, lambda *_: zeros)


def tie_body(value, *refs):
    pass


def tie(value, *earlier):
    return pl.pallas_call(
        tie_body,
        in_specs=[pl.BlockSpec(memory_space=pl.ANY)] * (1 + len(earlier)),
        out_specs=pl.BlockSpec(memory_space=pl.ANY),
        out_shape=jax.ShapeDtypeStruct(value.shape, value.dtype),
        input_output_aliases={0: 0},
        cost_estimate=pl.CostEstimate(flops=1, bytes_accessed=1, transcendentals=0),
    )(value, *earlier)


def row_outs(extent, columns, tile):
    count = lax.axis_size("row")
    rows = extent // count
    return [
        ((rows, columns), jnp.float32, (rows, tile), lambda n, c: (0, n)),
        (
            (count - 1, rows, columns),
            jnp.bfloat16,
            (count - 1, rows, tile),
            lambda n, c: (0, 0, n),
        ),
    ]


def put_rows(total, own, low):
    rows = own.shape[0]
    own[...] = total[:rows]
    low[...] = total[rows:].astype(jnp.bfloat16).reshape(low.shape)


def project(rows, block):
    n, _, d, width = block.shape
    half = width // 2
    extent = rows.shape[0]

    def body(c, x, mine, theirs, own, far):
        own[0] = mm(x[...], mine[...].reshape(n * d, half))
        far[0] = mm(x[...], theirs[...].reshape(n * d, half))

    return run(
        body,
        (3,),
        [
            whole(rows),
            (block, (n, 1, d, half), lambda k, c: (0, k, 0, c[0])),
            (block, (n, 1, d, half), lambda k, c: (0, k, 0, 1 - c[0])),
        ],
        [
            ((3, extent, half), jnp.float32, (1, extent, half), lambda k, c: (k, 0, 0)),
            ((3, extent, half), jnp.float32, (1, extent, half), lambda k, c: (k, 0, 0)),
        ],
    )


def mix(own, other, block):
    n, _, d, width = block.shape
    extent, half = own.shape

    def body(c, x, y, mine, theirs, out, low):
        parts = []
        a = mine[...].reshape(n // 2, 2, d // 2, width)
        b = theirs[...].reshape(n // 2, 2, d // 2, width)
        for h in range(2):
            parts.append(
                mm(x[...], a[:, h].reshape(half, width)) + mm(y[...], b[:, h].reshape(half, width))
            )
        put_rows(jnp.concatenate(parts, 1), out, low)

    return run(
        body,
        (1,),
        [
            whole(own),
            whole(other),
            (block, (n // 2, 1, d, width), lambda n, c: (c[0], 3, 0, 0)),
            (block, (n // 2, 1, d, width), lambda n, c: (1 - c[0], 3, 0, 0)),
        ],
        row_outs(extent, 2 * width, 2 * width),
    )


def mix_back(own, other, block, far):
    n, _, d, width = block.shape
    extent = own.shape[0]
    half = n * d // 4

    def body(c, x, y, mine, theirs, out):
        a = mine[...].reshape(n // 2, 2, d // 2, width)
        b = theirs[...].reshape(n // 2, 2, d // 2, width)
        total = None
        for h in range(2):
            cols = slice(h * width, (h + 1) * width)
            part = mm(x[:, cols], a[:, h].reshape(half, width), NT) + mm(
                y[:, cols], b[:, h].reshape(half, width), NT
            )
            total = part if total is None else total + part
        out[...] = total.astype(jnp.bfloat16)

    return run(
        body,
        (1,),
        [
            whole(own),
            whole(other),
            (block, (n // 2, 1, d, width), lambda n, c: (c[0], 3, 0, 0)),
            whole(far),
        ],
        [((extent, half), jnp.bfloat16, (extent, half), lambda n, c: (0, 0))],
    )[0]


def widen_send(rows, block, t):
    n, _, d, width = block.shape
    part = width // 4
    extent = rows.shape[0]

    def body(c, x, w, out):
        out[0] = mm(x[...], w[...].reshape(n * d, part)).astype(jnp.bfloat16)

    return run(
        body,
        (2,),
        [
            whole(rows),
            (block, (n, 1, d, part), lambda k, c: (0, k, 0, (1 - c[0]) * 2 + t)),
        ],
        [((2, extent, part), jnp.bfloat16, (1, extent, part), lambda k, c: (k, 0, 0))],
    )[0]


def widen(rows, block, arrived, t):
    n, _, d, width = block.shape
    part = width // 4
    extent = rows.shape[0]
    tiles = part // TILE

    def body(c, x, gate, up, far, kept, out):
        g = mm(x[...], gate[...].reshape(n * d, TILE)) + far[0].astype(jnp.float32)
        u = mm(x[...], up[...].reshape(n * d, TILE)) + far[1].astype(jnp.float32)
        kept[0] = g
        kept[1] = u
        out[...] = (g * jax.nn.sigmoid(g) * u).astype(jnp.bfloat16)

    return run(
        body,
        (tiles,),
        [
            whole(rows),
            (block, (n, 1, d, TILE), lambda i, c: (0, 0, 0, (c[0] * 2 + t) * tiles + i)),
            (block, (n, 1, d, TILE), lambda i, c: (0, 1, 0, (c[0] * 2 + t) * tiles + i)),
            (arrived, (2, extent, TILE), lambda i, c: (0, 0, i)),
        ],
        [
            ((2, extent, part), jnp.float32, (2, extent, TILE), lambda i, c: (0, 0, i)),
            ((extent, part), jnp.bfloat16, (extent, TILE), lambda i, c: (0, i)),
        ],
    )


def narrow(own, other, block):
    pieces = block.reshape(4, block.shape[0] // 4, block.shape[1])
    _, part, columns = pieces.shape
    extent = own[0].shape[0]

    def body(c, x0, x1, y0, y1, mine, theirs, out, low):
        total = mm(x0[...], mine[0]) + mm(x1[...], mine[1])
        total = total + mm(y0[...], theirs[0]) + mm(y1[...], theirs[1])
        put_rows(total, out, low)

    return run(
        body,
        (columns // TILE,),
        [whole(x) for x in own + other]
        + [
            (pieces, (2, part, TILE), lambda n, c: (c[0], 0, n)),
            (pieces, (2, part, TILE), lambda n, c: (1 - c[0], 0, n)),
        ],
        row_outs(extent, columns, TILE),
    )


def narrow_weight(own, other, grads):
    extent, part = own[0].shape
    columns = grads.shape[1]

    def body(c, x0, x1, y0, y1, g, out):
        for j, x in enumerate((x0, x1, y0, y1)):

            @pl.when(pl.program_id(0) == j)
            def _(x=x):
                out[...] = mm(x[...], g[...], TN).astype(jnp.bfloat16)

    def where(i, c):
        return (jnp.where(i < 2, c[0] * 2 + i, (1 - c[0]) * 2 + i - 2), 0)

    return run(
        body,
        (4,),
        [whole(x) for x in own + other] + [whole(grads)],
        [((4 * part, columns), jnp.bfloat16, (part, columns), where)],
    )[0]


def narrow_back(own, other, block, far, kept, t):
    pieces = block.reshape(4, block.shape[0] // 4, block.shape[1])
    _, part, columns = pieces.shape
    extent = own.shape[0]
    tiles = part // TILE

    def body(c, x, y, mine, theirs, saved, out):
        grad = mm(x[...], mine[0], NT) + mm(y[...], theirs[0], NT)
        gate = saved[0]
        sig = jax.nn.sigmoid(gate)
        out[0] = (grad * saved[1] * sig * (1.0 + gate * (1.0 - sig))).astype(jnp.bfloat16)
        out[1] = (grad * (gate * sig)).astype(jnp.bfloat16)

    return run(
        body,
        (tiles,),
        [
            whole(own),
            whole(other),
            (pieces, (1, TILE, columns), lambda i, c: (c[0] * 2 + t, i, 0)),
            (far, (1, TILE, columns), lambda i, c: (t, i, 0)),
            (kept, (2, extent, TILE), lambda i, c: (0, 0, i)),
        ],
        [((2, extent, part), jnp.bfloat16, (2, extent, TILE), lambda i, c: (0, 0, i))],
    )[0]


def widen_back(own, other, block):
    n, _, d, width = block.shape
    part = width // 4
    extent = own[0].shape[1]
    group = TILE // d

    def body(c, x0, x1, y0, y1, w0, w1, v0, v1, out, low):
        total = None
        for x, w in ((x0, w0), (x1, w1), (y0, v0), (y1, v1)):
            for k in range(2):
                piece = mm(x[k], w[:, k].reshape(TILE, part), NT)
                total = piece if total is None else total + piece
        put_rows(total, out, low)

    shape = (group, 2, d, part)
    return run(
        body,
        (n * d // TILE,),
        [whole(x) for x in own + other]
        + [
            (block, shape, lambda i, c: (i, 0, 0, c[0] * 2)),
            (block, shape, lambda i, c: (i, 0, 0, c[0] * 2 + 1)),
            (block, shape, lambda i, c: (i, 0, 0, 2 - c[0] * 2)),
            (block, shape, lambda i, c: (i, 0, 0, 3 - c[0] * 2)),
        ],
        row_outs(extent, n * d, TILE),
    )


def widen_weight(rows, own, other, shape):
    n, _, d, width = shape
    extent, features = rows.shape
    part = width // 4
    group = TILE // d

    def body(c, x, y0, y1, z0, z1, out):
        for j, y in enumerate((y0, y1, z0, z1)):

            @pl.when(pl.program_id(1) == j)
            def _(y=y):
                for k in range(2):
                    out[:, k] = (
                        mm(x[...], y[k], TN).astype(jnp.bfloat16).reshape(group, d, part)
                    )

    def where(i, j, c):
        return (i, 0, 0, jnp.where(j < 2, c[0] * 2 + j, (1 - c[0]) * 2 + j - 2))

    return run(
        body,
        (features // TILE, 4),
        [(rows, (extent, TILE), lambda i, j, c: (0, i))] + [whole(y) for y in own + other],
        [(shape, jnp.bfloat16, (group, 2, d, part), where)],
    )[0]


def project_back(own, other, block):
    n, _, d, width = block.shape
    half = width // 2
    extent = own.shape[1]
    group = TILE // d

    def body(c, x, y, mine, theirs, out, low):
        total = None
        for a, w in ((x, mine), (y, theirs)):
            for k in range(3):
                piece = mm(a[k], w[:, k].reshape(TILE, half), NT)
                total = piece if total is None else total + piece
        put_rows(total, out, low)

    return run(
        body,
        (n * d // TILE,),
        [
            whole(own),
            whole(other),
            (block, (group, 4, d, half), lambda i, c: (i, 0, 0, c[0])),
            (block, (group, 4, d, half), lambda i, c: (i, 0, 0, 1 - c[0])),
        ],
        row_outs(extent, n * d, TILE),
    )


def entry_mixer_weight(rows, own, other, heads, far_heads, grads, shape):
    n, _, d, width = shape
    half = width // 2
    extent, features = rows.shape
    group = TILE // d
    low = jnp.bfloat16
    fine = TILE // 2

    def body(c, x, y, z, a, b, g, out):
        for k in range(3):
            mine = mm(x[...], y[k], TN).astype(low).reshape(group, d, half)
            theirs = mm(x[...], z[k], TN).astype(low).reshape(group, d, half)
            for side in range(2):

                @pl.when(c[0] == side)
                def _():
                    out[:, k, :, side * half : (side + 1) * half] = mine
                    out[:, k, :, (1 - side) * half : (2 - side) * half] = theirs

        i = pl.program_id(0)
        for source, first in ((a, c[0] * 2), (b, (1 - c[0]) * 2)):
            for j in range(2):

                @pl.when(i == first + j)
                def _():
                    piece = mm(source[:, j * fine : (j + 1) * fine], g[...], TN).astype(low)
                    for h in range(2):
                        out[:, 3, h * (d // 2) : (h + 1) * (d // 2), :] = piece[
                            :, h * width : (h + 1) * width
                        ].reshape(group, d // 2, width)

    return run(
        body,
        (features // TILE,),
        [(rows, (extent, TILE), lambda i, c: (0, i))]
        + [whole(v) for v in (own, other, heads, far_heads, grads)],
        [(shape, low, (group, 4, d, width), lambda i, c: (i, 0, 0, 0))],
    )[0]


def take_half(block, axis, which):
    half = block.shape[axis] // 2
    return lax.dynamic_slice_in_dim(block, which * half, half, axis)


def gather_shards(shard):
    return lax.all_gather(shard, "dp", axis=0, tiled=True)


def scatter_shards(values):
    return lax.psum_scatter(values, "dp", scatter_dimension=0, tiled=True)


def on_device(
    tokens,
    cotangent,
    seq_lengths,
    gains,
    gain_mean,
    gain_square,
    entry_weight,
    entry_mean,
    entry_square,
    mixer_weight,
    mixer_mean,
    mixer_square,
    expand_weight,
    expand_mean,
    expand_square,
    reduce_weight,
    reduce_mean,
    reduce_square,
):
    low = jnp.bfloat16
    shards = lax.axis_size("dp")
    side = lax.axis_index("col")
    depth, grid_width = entry_weight.shape[1:]
    mixer_rows = mixer_weight.shape[0]
    entry_shard = jnp.concatenate(
        [
            entry_weight.astype(low).reshape(-1, grid_width),
            mixer_weight[:, :grid_width].astype(low),
            mixer_weight[:, grid_width:].astype(low),
        ],
        0,
    )
    entry_block = gather_shards(entry_shard).reshape(shards, 4, depth, grid_width)
    expand_shard = expand_weight.astype(low).reshape(-1, expand_weight.shape[2])
    expand_block = gather_shards(expand_shard).reshape((shards,) + expand_weight.shape)
    reduce_block = gather_shards(reduce_weight.astype(low))
    row_size = lax.axis_size("row")
    col_size = lax.axis_size("col")
    local_rows = tokens.shape[0]
    feature_local = tokens.shape[1]
    extent = local_rows * row_size
    row_index = lax.axis_index("row")
    blocks = row_index ^ jnp.arange(row_size, dtype=jnp.int32)
    indices = (
        blocks[:, None] * local_rows + jnp.arange(local_rows, dtype=jnp.int32)[None, :]
    ).reshape(extent)
    segment, positions = layout_info(seq_lengths[0], indices)
    local_valid = (segment[:local_rows] < seq_lengths.shape[1]).astype(jnp.float32)
    head_width = grid_width // col_size
    head_start = (row_index * col_size + lax.axis_index("col")) * head_width
    col_start = lax.axis_index("col") * feature_local
    post_gain = lax.dynamic_slice_in_dim(gains[0:2], col_start, feature_local, 1)
    head_gain = lax.dynamic_slice_in_dim(gains[2:4], head_start, head_width, 1)
    head_count = head_width // HD
    shrink = HD ** (-0.5)
    inputs = tokens.astype(jnp.float32)
    token_rows = gather_rows(tokens)
    projected, projected_far = project(token_rows, entry_block)
    projected = projected + swap_col(projected_far)
    squares = grid_total(jnp.sum(projected[0:2] * projected[0:2], -1))
    query_scale = lax.rsqrt(squares[0] / D + NORM_EPSILON)[:, None]
    key_scale = lax.rsqrt(squares[1] / D + NORM_EPSILON)[:, None]
    query_hat = projected[0] * query_scale
    key_hat = projected[1] * key_scale
    cosine, sine_table = rotary_tables(positions, HD)
    query_rot = rotate(
        (query_hat * head_gain[0]).reshape(extent, head_count, HD), cosine, sine_table
    ).astype(jnp.bfloat16)
    key_rot = rotate(
        (key_hat * head_gain[1]).reshape(extent, head_count, HD), cosine, sine_table
    ).astype(jnp.bfloat16)
    value_rows = projected[2].astype(jnp.bfloat16).reshape(extent, head_count, HD)
    block_rows = min(512, extent)

    def block_scores(offset):
        query_block = query_rot[offset : offset + block_rows]
        scores = (
            jnp.einsum("qhd,khd->hqk", query_block, key_rot, preferred_element_type=jnp.float32)
            * shrink
        )
        rows_here = indices[offset : offset + block_rows]
        allowed = (segment[offset : offset + block_rows][:, None] == segment[None, :]) & (
            indices[None, :] <= rows_here[:, None]
        )
        return (query_block, jnp.where(allowed[None], scores, -1e30))

    outputs = []
    logsums = []
    for offset in range(0, extent, block_rows):
        query_block, masked = block_scores(offset)
        peak = jnp.max(masked, -1, keepdims=True)
        expo = jnp.exp(masked - peak)
        totals = jnp.sum(expo, -1, keepdims=True)
        shares = (expo / totals).astype(jnp.bfloat16)
        outputs.append(
            jnp.einsum("hqk,khd->qhd", shares, value_rows, preferred_element_type=jnp.float32)
        )
        logsums.append(peak + jnp.log(totals))
    attended = jnp.concatenate(outputs, 0).astype(jnp.bfloat16).reshape(extent, head_width)
    attended_other = swap_col(attended)
    branch = scatter_rows(*mix(attended, attended_other, entry_block))
    branch_scale = lax.rsqrt(feature_total(jnp.sum(branch * branch, -1)) / D + NORM_EPSILON)[
        :, None
    ]
    branch_hat = branch * branch_scale
    hidden = inputs + branch_hat * post_gain[0]
    hidden_rows = gather_rows(hidden.astype(jnp.bfloat16))
    sent = [widen_send(hidden_rows, expand_block, t) for t in range(2)]
    kept, product = zip(
        *[widen(hidden_rows, expand_block, swap_col(sent[t]), t) for t in range(2)]
    )
    product = list(product)
    product_other = [swap_col(value) for value in product]
    second = scatter_rows(*narrow(product, product_other, reduce_block))
    second_scale = lax.rsqrt(feature_total(jnp.sum(second * second, -1)) / D + NORM_EPSILON)[
        :, None
    ]
    second_hat = second * second_scale
    layer_output = hidden + second_hat * post_gain[1]
    upstream = cotangent.astype(jnp.float32) * local_valid[:, None]
    gain_second_post = jnp.sum(upstream * second_hat, 0)
    scaled = upstream * post_gain[1]
    inner_sum = feature_total(jnp.sum(scaled * second_hat, -1))
    second_grad = (second_scale * (scaled - second_hat * inner_sum[:, None] / D)).astype(
        jnp.bfloat16
    )
    second_rows = gather_rows(second_grad)
    reduce_sum = narrow_weight(product, product_other, second_rows)
    reduce_grad = scatter_shards(reduce_sum)
    second_other = swap_col(second_rows)
    reduce_pieces = reduce_block.reshape(4, -1, reduce_block.shape[1])
    reduce_far = swap_col(take_half(reduce_pieces, 0, 1 - side))
    gated_grad = [
        narrow_back(tie(second_rows, reduce_sum), second_other, reduce_block, reduce_far, kept[t], t)
        for t in range(2)
    ]
    gated_other = [swap_col(value) for value in gated_grad]
    hidden_back = scatter_rows(*widen_back(gated_grad, gated_other, expand_block))
    expand_sum = widen_weight(hidden_rows, gated_grad, gated_other, expand_block.shape)
    expand_grad = scatter_shards(
        tie(expand_sum, reduce_grad).reshape(-1, expand_block.shape[3])
    ).reshape(expand_weight.shape)
    hidden_back = tie(hidden_back, expand_sum)
    hidden_grad = upstream + hidden_back
    gain_first_post = jnp.sum(hidden_grad * branch_hat, 0)
    scaled = hidden_grad * post_gain[0]
    inner_sum = feature_total(jnp.sum(scaled * branch_hat, -1))
    branch_grad = (branch_scale * (scaled - branch_hat * inner_sum[:, None] / D)).astype(
        jnp.bfloat16
    )
    branch_rows = gather_rows(branch_grad)
    branch_other = swap_col(branch_rows)
    mixer_far = swap_col(take_half(entry_block[:, 3:], 0, 1 - side))
    attended_low = mix_back(branch_rows, branch_other, entry_block, mixer_far).reshape(
        extent, head_count, HD
    )
    query_parts = []
    key_accum = jnp.zeros((extent, head_count, HD), jnp.float32)
    value_accum = jnp.zeros((extent, head_count, HD), jnp.float32)
    for number, offset in enumerate(range(0, extent, block_rows)):
        query_block, masked = block_scores(offset)
        shares = jnp.exp(masked - logsums[number])
        grad_block = attended_low[offset : offset + block_rows]
        flow_grad = jnp.einsum(
            "qhd,khd->hqk", grad_block, value_rows, preferred_element_type=jnp.float32
        )
        row_delta = jnp.sum(shares * flow_grad, -1, keepdims=True)
        score_grad = (shares * (flow_grad - row_delta)).astype(jnp.bfloat16)
        query_parts.append(
            jnp.einsum("hqk,khd->qhd", score_grad, key_rot, preferred_element_type=jnp.float32)
            * shrink
        )
        key_accum = (
            key_accum
            + jnp.einsum(
                "hqk,qhd->khd", score_grad, query_block, preferred_element_type=jnp.float32
            )
            * shrink
        )
        value_accum = value_accum + jnp.einsum(
            "hqk,qhd->khd",
            shares.astype(jnp.bfloat16),
            grad_block,
            preferred_element_type=jnp.float32,
        )
    query_grad = rotate_back(jnp.concatenate(query_parts, 0), cosine, sine_table).reshape(
        extent, head_width
    )
    key_grad = rotate_back(key_accum, cosine, sine_table).reshape(extent, head_width)
    gain_query = jnp.sum(query_grad * query_hat, 0)
    gain_key = jnp.sum(key_grad * key_hat, 0)
    query_scaled = query_grad * head_gain[0]
    key_scaled = key_grad * head_gain[1]
    head_dots = grid_total(
        jnp.stack(
            [jnp.sum(query_scaled * query_hat, -1), jnp.sum(key_scaled * key_hat, -1)]
        )
    )
    query_raw = query_scale * (query_scaled - query_hat * head_dots[0][:, None] / D)
    key_raw = key_scale * (key_scaled - key_hat * head_dots[1][:, None] / D)
    value_grad = value_accum.reshape(extent, head_width)
    projected_grad = jnp.stack([query_raw, key_raw, value_grad]).astype(low)
    projected_other = swap_col(projected_grad)
    entry_sum = entry_mixer_weight(
        token_rows,
        projected_grad,
        projected_other,
        attended,
        attended_other,
        branch_rows,
        entry_block.shape,
    )
    entry_out = scatter_shards(tie(entry_sum, expand_grad).reshape(-1, grid_width)).astype(
        jnp.float32
    )
    entry_back = scatter_rows(
        *project_back(tie(projected_grad, entry_sum), projected_other, entry_block)
    )
    input_grad = hidden_grad + entry_back
    entry_grad = entry_out[: 3 * depth].reshape(entry_weight.shape)
    mixer_grad = jnp.concatenate(
        [entry_out[3 * depth : 3 * depth + mixer_rows], entry_out[3 * depth + mixer_rows :]], 1
    )
    expand_grad = expand_grad.astype(jnp.float32)
    reduce_grad = reduce_grad.astype(jnp.float32)
    gain_local = jnp.zeros((4, D), jnp.float32)
    gain_local = lax.dynamic_update_slice(
        gain_local, jnp.stack([gain_first_post, gain_second_post]), (0, col_start)
    )
    gain_local = lax.dynamic_update_slice(
        gain_local, jnp.stack([gain_query, gain_key]), (2, head_start)
    )
    gain_grad = mesh_total(gain_local)
    gain_momentum, gain_variance, gain_updated = adam_step(
        gains, gain_grad, gain_mean, gain_square, 1.0, 0.0
    )
    entry_momentum, entry_variance, entry_updated = adam_step(
        entry_weight, entry_grad, entry_mean, entry_square, 2.0 * D ** (-0.5), WEIGHT_DECAY
    )
    mixer_momentum, mixer_variance, mixer_updated = adam_step(
        mixer_weight, mixer_grad, mixer_mean, mixer_square, 2.0 * D ** (-0.5), WEIGHT_DECAY
    )
    expand_momentum, expand_variance, expand_updated = adam_step(
        expand_weight, expand_grad, expand_mean, expand_square, 2.0 * D ** (-0.5), WEIGHT_DECAY
    )
    reduce_momentum, reduce_variance, reduce_updated = adam_step(
        reduce_weight, reduce_grad, reduce_mean, reduce_square, 2.0 * FF ** (-0.5), WEIGHT_DECAY
    )
    return (
        layer_output,
        input_grad,
        gain_grad,
        gain_momentum,
        gain_variance,
        gain_updated,
        entry_grad,
        entry_momentum,
        entry_variance,
        entry_updated,
        mixer_grad,
        mixer_momentum,
        mixer_variance,
        mixer_updated,
        expand_grad,
        expand_momentum,
        expand_variance,
        expand_updated,
        reduce_grad,
        reduce_momentum,
        reduce_variance,
        reduce_updated,
    )


def solution(mesh):
    placed = (
        P(("dp", "row"), "col"),
        P(("dp", "row"), "col"),
        P("dp", None),
        P(),
        P(),
        P(),
        P(None, ("col", "dp"), "row"),
        P(None, ("col", "dp"), "row"),
        P(None, ("col", "dp"), "row"),
        P(("row", "dp"), "col"),
        P(("row", "dp"), "col"),
        P(("row", "dp"), "col"),
        P(None, ("col", "dp"), "row"),
        P(None, ("col", "dp"), "row"),
        P(None, ("col", "dp"), "row"),
        P(("row", "dp"), "col"),
        P(("row", "dp"), "col"),
        P(("row", "dp"), "col"),
    )
    return jax.shard_map(
        on_device,
        mesh=mesh,
        in_specs=placed,
        out_specs=(
            P(("dp", "row"), "col"),
            P(("dp", "row"), "col"),
            P(),
            P(),
            P(),
            P(),
            P(None, ("col", "dp"), "row"),
            P(None, ("col", "dp"), "row"),
            P(None, ("col", "dp"), "row"),
            P(None, ("col", "dp"), "row"),
            P(("row", "dp"), "col"),
            P(("row", "dp"), "col"),
            P(("row", "dp"), "col"),
            P(("row", "dp"), "col"),
            P(None, ("col", "dp"), "row"),
            P(None, ("col", "dp"), "row"),
            P(None, ("col", "dp"), "row"),
            P(None, ("col", "dp"), "row"),
            P(("row", "dp"), "col"),
            P(("row", "dp"), "col"),
            P(("row", "dp"), "col"),
            P(("row", "dp"), "col"),
        ),
        check_vma=False,
    )
```

```python
import jax
import jax.numpy as jnp
from jax import lax
from jax.experimental import pallas as pl
from jax.experimental.pallas import tpu as pltpu
from jax.sharding import PartitionSpec as P

D = 2048
HD = 128
FF = 8192
STEP = 10


NORM_EPSILON = 1e-06
ROPE_BASE = 500000.0
BETA_FIRST = 0.9
BETA_SECOND = 0.95
ADAM_EPSILON = 1e-08
WEIGHT_DECAY = 0.1


def layout_info(lengths, indices):
    closing = jnp.cumsum(lengths)
    starts = closing - lengths
    segment = jnp.sum((indices[:, None] >= closing[None, :]).astype(jnp.int32), 1)
    member = segment[:, None] == jnp.arange(lengths.shape[0], dtype=jnp.int32)[None, :]
    anchor = jnp.sum(jnp.where(member, starts[None, :], 0), 1)
    anchor = jnp.where(segment >= lengths.shape[0], closing[-1], anchor)
    return (segment, indices - anchor)


def rotary_tables(positions, width):
    half_width = width // 2
    freqs = ROPE_BASE ** (-jnp.arange(half_width, dtype=jnp.float32) * 2.0 / width)
    angles = positions.astype(jnp.float32)[:, None] * freqs[None, :]
    return (jnp.cos(angles), jnp.sin(angles))


def rotate(values, cosine, sine_table):
    half_width = values.shape[-1] // 2
    first = values[..., :half_width]
    second = values[..., half_width:]
    cos_wide = cosine[:, None, :]
    sin_wide = sine_table[:, None, :]
    return jnp.concatenate(
        [first * cos_wide - second * sin_wide, second * cos_wide + first * sin_wide], -1
    )


def rotate_back(values, cosine, sine_table):
    half_width = values.shape[-1] // 2
    first = values[..., :half_width]
    second = values[..., half_width:]
    cos_wide = cosine[:, None, :]
    sin_wide = sine_table[:, None, :]
    return jnp.concatenate(
        [first * cos_wide + second * sin_wide, second * cos_wide - first * sin_wide], -1
    )


def adam_step(weight, gradient, moment, square, step_rate, decay_rate):
    moment_new = BETA_FIRST * moment + (1.0 - BETA_FIRST) * gradient
    square_new = BETA_SECOND * square + (1.0 - BETA_SECOND) * gradient * gradient
    ratio = (
        moment_new
        / (1.0 - BETA_FIRST**STEP)
        / (jnp.sqrt(square_new / (1.0 - BETA_SECOND**STEP)) + ADAM_EPSILON)
    )
    return (moment_new, square_new, weight - step_rate * (ratio + decay_rate * weight))


def swap(values, axis, distance):
    return lax.ppermute(values, axis, [(i, i ^ distance) for i in range(lax.axis_size(axis))])


def swap_col(values):
    return swap(values, "col", 1)


def feature_total(values):
    return values + swap_col(values)


def grid_total(values):
    values = feature_total(values)
    count = lax.axis_size("row")
    blocks = values.reshape(values.shape[0], count, -1)
    total = blocks
    for k in range(1, count):
        part = swap(blocks, "row", k)
        total = total + jnp.stack([part[:, j ^ k] for j in range(count)], 1)
    return total.reshape(values.shape)


def mesh_total(values):
    for axis in ("col", "row", "dp"):
        distance = 1
        while distance < lax.axis_size(axis):
            values = values + swap(values, axis, distance)
            distance *= 2
    return values


def gather_rows(block):
    count = lax.axis_size("row")
    if count != 4:
        return jnp.concatenate([block] + [swap(block, "row", k) for k in range(1, count)], 0)
    half = block.shape[0] // 2
    first = swap(block, "row", 1)
    second = swap(block, "row", 2)
    return jnp.concatenate(
        [block, first, second, swap(first[:half], "row", 2), swap(second[half:], "row", 1)], 0
    )


def scatter_rows(own, low):
    for k in range(1, lax.axis_size("row")):
        own = own + swap(low[k - 1], "row", k).astype(jnp.float32)
    return own


VMEM = 48 * 1024 * 1024
TILE = 256
PART = 512
NN = (((1,), (0,)), ((), ()))
NT = (((1,), (1,)), ((), ()))
TN = (((0,), (0,)), ((), ()))


def mm(left, right, dims=NN):
    return lax.dot_general(left, right, dims, preferred_element_type=jnp.float32)


def run(body, grid, ins, outs, earlier=()):
    place = lax.axis_index("col").astype(jnp.int32).reshape(1)

    def kernel(c, *refs):
        body(c, *refs[: len(ins)], *refs[len(ins) + len(earlier) :])

    return pl.pallas_call(
        kernel,
        grid_spec=pltpu.PrefetchScalarGridSpec(
            num_scalar_prefetch=1,
            grid=grid,
            in_specs=[pl.BlockSpec(block, where) for _, block, where in ins]
            + [pl.BlockSpec(memory_space=pl.ANY)] * len(earlier),
            out_specs=[pl.BlockSpec(block, where) for _, _, block, where in outs],
        ),
        out_shape=[jax.ShapeDtypeStruct(shape, kind) for shape, kind, _, _ in outs],
        compiler_params=pltpu.CompilerParams(vmem_limit_bytes=VMEM),
        cost_estimate=pl.CostEstimate(flops=1, bytes_accessed=1, transcendentals=0),
    )(place, *[array for array, _, _ in ins], *earlier)


def whole(array):
    zeros = (0,) * array.ndim
    return (array, array.shape, lambda *_: zeros)


def tie_body(value, *refs):
    pass


def tie(value, *earlier):
    return pl.pallas_call(
        tie_body,
        in_specs=[pl.BlockSpec(memory_space=pl.ANY)] * (1 + len(earlier)),
        out_specs=pl.BlockSpec(memory_space=pl.ANY),
        out_shape=jax.ShapeDtypeStruct(value.shape, value.dtype),
        input_output_aliases={0: 0},
        cost_estimate=pl.CostEstimate(flops=1, bytes_accessed=1, transcendentals=0),
    )(value, *earlier)


def ring_gather(shards):
    count = lax.axis_size("dp")
    rows = shards[0].shape[0]
    joined = jnp.zeros((count, len(shards)) + shards[0].shape, shards[0].dtype)
    pairs = [(i, (i - 1) % count) for i in range(count)]
    for step in range(count):
        spot = lax.rem(lax.axis_index("dp") + step, count)
        if step:
            shards = [lax.ppermute(shard, "dp", pairs) for shard in shards]
        for j, shard in enumerate(shards):
            joined = lax.dynamic_update_slice(joined, shard[None, None], (spot, j, 0, 0))
    return joined.reshape((count, len(shards) * rows) + joined.shape[3:])


def row_outs(extent, columns, tile):
    count = lax.axis_size("row")
    rows = extent // count
    return [
        ((rows, columns), jnp.float32, (rows, tile), lambda n, c: (0, n)),
        (
            (count - 1, rows, columns),
            jnp.bfloat16,
            (count - 1, rows, tile),
            lambda n, c: (0, 0, n),
        ),
    ]


def put_rows(total, own, low):
    rows = own.shape[0]
    own[...] = total[:rows]
    low[...] = total[rows:].astype(jnp.bfloat16).reshape(low.shape)


def project(rows, block):
    n, _, d, width = block.shape
    half = width // 2
    extent = rows.shape[0]

    def body(c, x, mine, theirs, own, far):
        own[0] = mm(x[...], mine[...].reshape(n * d, half))
        far[0] = mm(x[...], theirs[...].reshape(n * d, half))

    return run(
        body,
        (3,),
        [
            whole(rows),
            (block, (n, 1, d, half), lambda k, c: (0, k, 0, c[0])),
            (block, (n, 1, d, half), lambda k, c: (0, k, 0, 1 - c[0])),
        ],
        [
            ((3, extent, half), jnp.float32, (1, extent, half), lambda k, c: (k, 0, 0)),
            ((3, extent, half), jnp.float32, (1, extent, half), lambda k, c: (k, 0, 0)),
        ],
    )


def mix(own, other, block):
    n, _, d, width = block.shape
    extent, half = own.shape

    def body(c, x, y, mine, theirs, out, low):
        parts = []
        a = mine[...].reshape(n // 2, 2, d // 2, width)
        b = theirs[...].reshape(n // 2, 2, d // 2, width)
        for h in range(2):
            parts.append(
                mm(x[...], a[:, h].reshape(half, width)) + mm(y[...], b[:, h].reshape(half, width))
            )
        put_rows(jnp.concatenate(parts, 1), out, low)

    return run(
        body,
        (1,),
        [
            whole(own),
            whole(other),
            (block, (n // 2, 1, d, width), lambda n, c: (c[0], 3, 0, 0)),
            (block, (n // 2, 1, d, width), lambda n, c: (1 - c[0], 3, 0, 0)),
        ],
        row_outs(extent, 2 * width, 2 * width),
    )


def mix_back(own, other, block, far):
    n, _, d, width = block.shape
    extent = own.shape[0]
    half = n * d // 4

    def body(c, x, y, mine, theirs, out):
        a = mine[...].reshape(n // 2, 2, d // 2, width)
        b = theirs[...].reshape(n // 2, 2, d // 2, width)
        total = None
        for h in range(2):
            cols = slice(h * width, (h + 1) * width)
            part = mm(x[:, cols], a[:, h].reshape(half, width), NT) + mm(
                y[:, cols], b[:, h].reshape(half, width), NT
            )
            total = part if total is None else total + part
        out[...] = total.astype(jnp.bfloat16)

    return run(
        body,
        (1,),
        [
            whole(own),
            whole(other),
            (block, (n // 2, 1, d, width), lambda n, c: (c[0], 3, 0, 0)),
            whole(far),
        ],
        [((extent, half), jnp.bfloat16, (extent, half), lambda n, c: (0, 0))],
    )[0]


def piece_order(pieces):
    half = pieces // 2
    return lambda j, c: jnp.where(j < half, c[0] * half + j, (1 - c[0]) * half + j - half)


def widen_send(rows, block, t):
    n, _, d, width = block.shape
    half = width // PART // 2
    extent = rows.shape[0]

    def body(c, x, w, out):
        out[0] = mm(x[...], w[...].reshape(n * d, PART)).astype(jnp.bfloat16)

    return run(
        body,
        (2,),
        [
            whole(rows),
            (block, (n, 1, d, PART), lambda k, c: (0, k, 0, (1 - c[0]) * half + t)),
        ],
        [((2, extent, PART), jnp.bfloat16, (1, extent, PART), lambda k, c: (k, 0, 0))],
    )[0]


def widen(rows, block, arrived, t):
    n, _, d, width = block.shape
    half = width // PART // 2
    extent = rows.shape[0]
    tiles = PART // TILE

    def body(c, x, gate, up, far, kept, out):
        g = mm(x[...], gate[...].reshape(n * d, TILE)) + far[0].astype(jnp.float32)
        u = mm(x[...], up[...].reshape(n * d, TILE)) + far[1].astype(jnp.float32)
        kept[0] = g
        kept[1] = u
        out[...] = (g * jax.nn.sigmoid(g) * u).astype(jnp.bfloat16)

    return run(
        body,
        (tiles,),
        [
            whole(rows),
            (block, (n, 1, d, TILE), lambda i, c: (0, 0, 0, (c[0] * half + t) * tiles + i)),
            (block, (n, 1, d, TILE), lambda i, c: (0, 1, 0, (c[0] * half + t) * tiles + i)),
            (arrived, (2, extent, TILE), lambda i, c: (0, 0, i)),
        ],
        [
            ((2, extent, PART), jnp.float32, (2, extent, TILE), lambda i, c: (0, 0, i)),
            ((extent, PART), jnp.bfloat16, (extent, TILE), lambda i, c: (0, i)),
        ],
    )


def narrow(own, other, pieces, earlier=()):
    count, part, columns = pieces.shape
    half = count // 2
    extent = own[0].shape[0]

    def body(c, *refs):
        xs = refs[:count]
        mine, theirs, out, low = refs[count:]
        total = None
        for j, x in enumerate(xs):
            piece = mm(x[...], (mine if j < half else theirs)[j % half])
            total = piece if total is None else total + piece
        put_rows(total, out, low)

    return run(
        body,
        (columns // TILE,),
        [whole(x) for x in own + other]
        + [
            (pieces, (half, part, TILE), lambda n, c: (c[0], 0, n)),
            (pieces, (half, part, TILE), lambda n, c: (1 - c[0], 0, n)),
        ],
        row_outs(extent, columns, TILE),
        earlier,
    )


def narrow_weight(own, other, grads, earlier=()):
    groups = len(grads)
    half = len(own[0])
    extent, part = own[0][0].shape
    columns = grads[0].shape[1]
    order = piece_order(2 * half)
    flat = [x for j in range(2 * half) for x in ([g[j] for g in own] if j < half else [g[j - half] for g in other])]

    def body(c, *refs):
        gs = refs[len(flat) : len(flat) + groups]
        out = refs[-1]
        for j in range(2 * half):

            @pl.when(pl.program_id(0) == j)
            def _(j=j):
                total = None
                for g in range(groups):
                    piece = mm(refs[j * groups + g][...], gs[g][...], TN)
                    total = piece if total is None else total + piece
                out[0] = total.astype(jnp.bfloat16)

    return run(
        body,
        (2 * half,),
        [whole(x) for x in flat] + [whole(g) for g in grads],
        [
            (
                (2 * half, part, columns),
                jnp.bfloat16,
                (1, part, columns),
                lambda i, c: (order(i, c), 0, 0),
            )
        ],
        earlier,
    )[0]


def narrow_back(own, other, pieces, far, kept, t, earlier=()):
    count, part, columns = pieces.shape
    half = count // 2
    extent = own.shape[0]
    tiles = part // TILE

    def body(c, x, y, mine, theirs, saved, out):
        grad = mm(x[...], mine[0], NT) + mm(y[...], theirs[0], NT)
        gate = saved[0]
        sig = jax.nn.sigmoid(gate)
        out[0] = (grad * saved[1] * sig * (1.0 + gate * (1.0 - sig))).astype(jnp.bfloat16)
        out[1] = (grad * (gate * sig)).astype(jnp.bfloat16)

    return run(
        body,
        (tiles,),
        [
            whole(own),
            whole(other),
            (pieces, (1, TILE, columns), lambda i, c: (c[0] * half + t, i, 0)),
            (far, (1, TILE, columns), lambda i, c: (t, i, 0)),
            (kept, (2, extent, TILE), lambda i, c: (0, 0, i)),
        ],
        [((2, extent, part), jnp.bfloat16, (2, extent, TILE), lambda i, c: (0, 0, i))],
        earlier,
    )[0]


def widen_back(own, other, block, earlier=()):
    n, _, d, width = block.shape
    count = width // PART
    extent = own[0].shape[1]
    group = TILE // d
    order = piece_order(count)

    def body(c, *refs):
        out, low = refs[2 * count :]
        total = None
        for x, w in zip(refs[:count], refs[count : 2 * count]):
            for k in range(2):
                piece = mm(x[k], w[:, k].reshape(TILE, PART), NT)
                total = piece if total is None else total + piece
        put_rows(total, out, low)

    return run(
        body,
        (n * d // TILE,),
        [whole(x) for x in own + other]
        + [
            (block, (group, 2, d, PART), lambda i, c, j=j: (i, 0, 0, order(j, c)))
            for j in range(count)
        ],
        row_outs(extent, n * d, TILE),
        earlier,
    )


def widen_weight(rows, own, other, shape, earlier=()):
    n, _, d, width = shape
    groups = len(rows)
    half = len(own[0])
    extent, features = rows[0].shape
    group = TILE // d
    order = piece_order(2 * half)
    flat = [x for j in range(2 * half) for x in ([g[j] for g in own] if j < half else [g[j - half] for g in other])]

    def body(c, *refs):
        xs = refs[:groups]
        ys = refs[groups:-1]
        out = refs[-1]
        for j in range(2 * half):

            @pl.when(pl.program_id(1) == j)
            def _(j=j):
                for k in range(2):
                    total = None
                    for g in range(groups):
                        piece = mm(xs[g][...], ys[j * groups + g][k], TN)
                        total = piece if total is None else total + piece
                    out[:, k] = total.astype(jnp.bfloat16).reshape(group, d, PART)

    return run(
        body,
        (features // TILE, 2 * half),
        [(x, (extent, TILE), lambda i, j, c: (0, i)) for x in rows] + [whole(y) for y in flat],
        [
            (
                shape,
                jnp.bfloat16,
                (group, 2, d, PART),
                lambda i, j, c: (i, 0, 0, order(j, c)),
            )
        ],
        earlier,
    )[0]


def project_back(own, other, block, earlier):
    n, _, d, width = block.shape
    half = width // 2
    extent = own.shape[1]
    group = TILE // d

    def body(c, x, y, mine, theirs, out, low):
        total = None
        for a, w in ((x, mine), (y, theirs)):
            for k in range(3):
                piece = mm(a[k], w[:, k].reshape(TILE, half), NT)
                total = piece if total is None else total + piece
        put_rows(total, out, low)

    return run(
        body,
        (n * d // TILE,),
        [
            whole(own),
            whole(other),
            (block, (group, 4, d, half), lambda i, c: (i, 0, 0, c[0])),
            (block, (group, 4, d, half), lambda i, c: (i, 0, 0, 1 - c[0])),
        ],
        row_outs(extent, n * d, TILE),
        earlier,
    )


def entry_mixer_weight(rows, own, other, heads, far_heads, grads, shape):
    n, _, d, width = shape
    half = width // 2
    extent, features = rows.shape
    group = TILE // d
    low = jnp.bfloat16
    fine = TILE // 2

    def body(c, x, y, z, a, b, g, out):
        for k in range(3):
            mine = mm(x[...], y[k], TN).astype(low).reshape(group, d, half)
            theirs = mm(x[...], z[k], TN).astype(low).reshape(group, d, half)
            for side in range(2):

                @pl.when(c[0] == side)
                def _():
                    out[:, k, :, side * half : (side + 1) * half] = mine
                    out[:, k, :, (1 - side) * half : (2 - side) * half] = theirs

        i = pl.program_id(0)
        for source, first in ((a, c[0] * 2), (b, (1 - c[0]) * 2)):
            for j in range(2):

                @pl.when(i == first + j)
                def _():
                    piece = mm(source[:, j * fine : (j + 1) * fine], g[...], TN).astype(low)
                    for h in range(2):
                        out[:, 3, h * (d // 2) : (h + 1) * (d // 2), :] = piece[
                            :, h * width : (h + 1) * width
                        ].reshape(group, d // 2, width)

    return run(
        body,
        (features // TILE,),
        [(rows, (extent, TILE), lambda i, c: (0, i))]
        + [whole(v) for v in (own, other, heads, far_heads, grads)],
        [(shape, low, (group, 4, d, width), lambda i, c: (i, 0, 0, 0))],
    )[0]


def take_half(block, axis, which):
    half = block.shape[axis] // 2
    return lax.dynamic_slice_in_dim(block, which * half, half, axis)


def gather_shards(shard):
    return lax.all_gather(shard, "dp", axis=0, tiled=True)


def scatter_shards(values):
    return lax.psum_scatter(values, "dp", scatter_dimension=0, tiled=True)


def adam_values(weight, gradient, moment, square, step_rate):
    moment_new, square_new, updated = adam_step(
        weight, gradient, moment, square, step_rate, WEIGHT_DECAY
    )
    return (gradient, moment_new, square_new, updated)


def adam_call(body, grid, gradients, state, block, where):
    return run(
        body,
        grid,
        gradients + [(array, block, where) for array in state],
        [(state[0].shape, jnp.float32, block, where)] * 4,
    )


def adam_rows(gradient, first, blocks, state, step_rate):
    d = state[0].shape[-2] // (blocks if state[0].ndim == 2 else 1)
    width = state[0].shape[-1]
    lead = (1,) * (state[0].ndim - 2)

    def body(c, g, weight, moment, square, *outs):
        value = g[...].astype(jnp.float32).reshape(weight.shape)
        for out, result in zip(
            outs, adam_values(weight[...], value, moment[...], square[...], step_rate)
        ):
            out[...] = result

    return adam_call(
        body,
        (blocks,),
        [(gradient, (d, width), lambda k, c: (first + k, 0))],
        state,
        lead + (d, width),
        (lambda k, c: (k, 0, 0)) if lead else (lambda k, c: (k, 0)),
    )


def adam_halves(gradient, first, state, step_rate):
    rows, width = state[0].shape
    block = (rows, width // 2)

    def body(c, g, weight, moment, square, *outs):
        value = g[...].astype(jnp.float32)
        for out, result in zip(
            outs, adam_values(weight[...], value, moment[...], square[...], step_rate)
        ):
            out[...] = result

    return adam_call(
        body,
        (2,),
        [(gradient, block, lambda k, c: (first + k, 0))],
        state,
        block,
        lambda k, c: (0, k),
    )


def on_device(
    tokens,
    cotangent,
    seq_lengths,
    gains,
    gain_mean,
    gain_square,
    entry_weight,
    entry_mean,
    entry_square,
    mixer_weight,
    mixer_mean,
    mixer_square,
    expand_weight,
    expand_mean,
    expand_square,
    reduce_weight,
    reduce_mean,
    reduce_square,
):
    low = jnp.bfloat16
    shards = lax.axis_size("dp")
    side = lax.axis_index("col")
    depth, grid_width = entry_weight.shape[1:]
    mixer_rows = mixer_weight.shape[0]
    entry_shard = jnp.concatenate(
        [
            entry_weight.astype(low).reshape(-1, grid_width),
            mixer_weight[:, :grid_width].astype(low),
            mixer_weight[:, grid_width:].astype(low),
        ],
        0,
    )
    if shards > 4:
        entry_block = gather_shards(entry_shard)
    else:
        entry_block = ring_gather([entry_shard[: 2 * depth], entry_shard[2 * depth :]])
    entry_block = entry_block.reshape(shards, 4, depth, grid_width)
    reduce_low = reduce_weight.astype(low)
    expand_low = expand_weight.astype(low)
    expand_block = gather_shards(
        tie(expand_low, entry_block).reshape(-1, expand_low.shape[2])
    ).reshape(
        (shards,) + expand_weight.shape
    )
    reduce_pieces = gather_shards(reduce_low).reshape(4, -1, reduce_low.shape[1])
    halves = range(2)

    row_size = lax.axis_size("row")
    col_size = lax.axis_size("col")
    local_rows = tokens.shape[0]
    feature_local = tokens.shape[1]
    extent = local_rows * row_size
    row_index = lax.axis_index("row")
    blocks = row_index ^ jnp.arange(row_size, dtype=jnp.int32)
    indices = (
        blocks[:, None] * local_rows + jnp.arange(local_rows, dtype=jnp.int32)[None, :]
    ).reshape(extent)
    segment, positions = layout_info(seq_lengths[0], indices)
    local_valid = (segment[:local_rows] < seq_lengths.shape[1]).astype(jnp.float32)
    head_width = grid_width // col_size
    head_start = (row_index * col_size + lax.axis_index("col")) * head_width
    col_start = lax.axis_index("col") * feature_local
    post_gain = lax.dynamic_slice_in_dim(gains[0:2], col_start, feature_local, 1)
    head_gain = lax.dynamic_slice_in_dim(gains[2:4], head_start, head_width, 1)
    head_count = head_width // HD
    shrink = HD ** (-0.5)
    inputs = tokens.astype(jnp.float32)
    token_rows = gather_rows(tokens)
    projected, projected_far = project(token_rows, entry_block)
    projected = projected + swap_col(projected_far)
    squares = grid_total(jnp.sum(projected[0:2] * projected[0:2], -1))
    query_scale = lax.rsqrt(squares[0] / D + NORM_EPSILON)[:, None]
    key_scale = lax.rsqrt(squares[1] / D + NORM_EPSILON)[:, None]
    query_hat = projected[0] * query_scale
    key_hat = projected[1] * key_scale
    cosine, sine_table = rotary_tables(positions, HD)
    query_rot = rotate(
        (query_hat * head_gain[0]).reshape(extent, head_count, HD), cosine, sine_table
    ).astype(jnp.bfloat16)
    key_rot = rotate(
        (key_hat * head_gain[1]).reshape(extent, head_count, HD), cosine, sine_table
    ).astype(jnp.bfloat16)
    value_rows = projected[2].astype(jnp.bfloat16).reshape(extent, head_count, HD)
    block_rows = min(512, extent)

    def block_scores(offset):
        query_block = query_rot[offset : offset + block_rows]
        scores = (
            jnp.einsum("qhd,khd->hqk", query_block, key_rot, preferred_element_type=jnp.float32)
            * shrink
        )
        rows_here = indices[offset : offset + block_rows]
        allowed = (segment[offset : offset + block_rows][:, None] == segment[None, :]) & (
            indices[None, :] <= rows_here[:, None]
        )
        return (query_block, jnp.where(allowed[None], scores, -1e30))

    outputs = []
    logsums = []
    for offset in range(0, extent, block_rows):
        query_block, masked = block_scores(offset)
        peak = jnp.max(masked, -1, keepdims=True)
        expo = jnp.exp(masked - peak)
        totals = jnp.sum(expo, -1, keepdims=True)
        shares = (expo / totals).astype(jnp.bfloat16)
        outputs.append(
            jnp.einsum("hqk,khd->qhd", shares, value_rows, preferred_element_type=jnp.float32)
        )
        logsums.append(peak + jnp.log(totals))
    attended = jnp.concatenate(outputs, 0).astype(jnp.bfloat16).reshape(extent, head_width)
    attended_other = swap_col(attended)
    branch = scatter_rows(*mix(attended, attended_other, entry_block))
    branch_scale = lax.rsqrt(feature_total(jnp.sum(branch * branch, -1)) / D + NORM_EPSILON)[
        :, None
    ]
    branch_hat = branch * branch_scale
    hidden = inputs + branch_hat * post_gain[0]
    hidden_rows = gather_rows(hidden.astype(jnp.bfloat16))
    sent = [swap_col(widen_send(hidden_rows, expand_block, t)) for t in halves]
    kept, product = zip(*[widen(hidden_rows, expand_block, sent[t], t) for t in halves])
    product = list(product)
    product_other = [swap_col(value) for value in product]
    second = scatter_rows(*narrow(product, product_other, reduce_pieces))
    upstream = cotangent.astype(jnp.float32) * local_valid[:, None]
    scaled = upstream * post_gain[1]
    totals = feature_total(
        jnp.stack([jnp.sum(second * second, -1), jnp.sum(scaled * second, -1)])
    )
    second_scale = lax.rsqrt(totals[0] / D + NORM_EPSILON)[:, None]
    second_hat = second * second_scale
    layer_output = hidden + second_hat * post_gain[1]
    gain_second_post = jnp.sum(upstream * second_hat, 0)
    inner_sum = totals[1][:, None] * second_scale
    second_grad = (second_scale * (scaled - second_hat * inner_sum / D)).astype(jnp.bfloat16)
    second_rows = gather_rows(second_grad)
    second_other = swap_col(second_rows)
    reduce_sum = narrow_weight([product], [product_other], [second_rows])
    reduce_far = swap_col(take_half(reduce_pieces, 0, 1 - side))
    gated_grad = [
        narrow_back(
            second_rows, second_other, reduce_pieces, reduce_far, kept[t], t, [reduce_sum]
        )
        for t in halves
    ]
    gated_other = [swap_col(value) for value in gated_grad]
    hidden_parts = widen_back(gated_grad, gated_other, expand_block)
    hidden_back = scatter_rows(*hidden_parts)
    expand_sum = widen_weight(
        [hidden_rows], [gated_grad], [gated_other], expand_block.shape, [hidden_parts[1]]
    )
    rate = 2.0 * D ** (-0.5)
    reduce_grad = scatter_shards(reduce_sum.reshape(-1, reduce_low.shape[1]))
    expand_grad = scatter_shards(
        tie(expand_sum, reduce_grad).reshape(-1, expand_low.shape[2])
    )
    reduce_outs = adam_rows(
        reduce_grad, 0, 2, [reduce_weight, reduce_mean, reduce_square], 2.0 * FF ** (-0.5)
    )
    expand_outs = adam_rows(
        expand_grad, 0, 2, [expand_weight, expand_mean, expand_square], rate
    )
    hidden_grad = upstream + hidden_back
    gain_first_post = jnp.sum(hidden_grad * branch_hat, 0)
    scaled = hidden_grad * post_gain[0]
    inner_sum = feature_total(jnp.sum(scaled * branch_hat, -1))
    branch_grad = (branch_scale * (scaled - branch_hat * inner_sum[:, None] / D)).astype(
        jnp.bfloat16
    )
    branch_rows = gather_rows(branch_grad)
    branch_other = swap_col(branch_rows)
    mixer_far = swap_col(take_half(entry_block[:, 3:], 0, 1 - side))
    attended_low = mix_back(branch_rows, branch_other, entry_block, mixer_far).reshape(
        extent, head_count, HD
    )
    query_parts = []
    key_accum = jnp.zeros((extent, head_count, HD), jnp.float32)
    value_accum = jnp.zeros((extent, head_count, HD), jnp.float32)
    for number, offset in enumerate(range(0, extent, block_rows)):
        query_block, masked = block_scores(offset)
        shares = jnp.exp(masked - logsums[number])
        grad_block = attended_low[offset : offset + block_rows]
        flow_grad = jnp.einsum(
            "qhd,khd->hqk", grad_block, value_rows, preferred_element_type=jnp.float32
        )
        row_delta = jnp.sum(shares * flow_grad, -1, keepdims=True)
        score_grad = (shares * (flow_grad - row_delta)).astype(jnp.bfloat16)
        query_parts.append(
            jnp.einsum("hqk,khd->qhd", score_grad, key_rot, preferred_element_type=jnp.float32)
            * shrink
        )
        key_accum = (
            key_accum
            + jnp.einsum(
                "hqk,qhd->khd", score_grad, query_block, preferred_element_type=jnp.float32
            )
            * shrink
        )
        value_accum = value_accum + jnp.einsum(
            "hqk,qhd->khd",
            shares.astype(jnp.bfloat16),
            grad_block,
            preferred_element_type=jnp.float32,
        )
    query_grad = rotate_back(jnp.concatenate(query_parts, 0), cosine, sine_table).reshape(
        extent, head_width
    )
    key_grad = rotate_back(key_accum, cosine, sine_table).reshape(extent, head_width)
    gain_query = jnp.sum(query_grad * query_hat, 0)
    gain_key = jnp.sum(key_grad * key_hat, 0)
    query_scaled = query_grad * head_gain[0]
    key_scaled = key_grad * head_gain[1]
    head_dots = grid_total(
        jnp.stack(
            [jnp.sum(query_scaled * query_hat, -1), jnp.sum(key_scaled * key_hat, -1)]
        )
    )
    query_raw = query_scale * (query_scaled - query_hat * head_dots[0][:, None] / D)
    key_raw = key_scale * (key_scaled - key_hat * head_dots[1][:, None] / D)
    value_grad = value_accum.reshape(extent, head_width)
    projected_grad = jnp.stack([query_raw, key_raw, value_grad]).astype(low)
    projected_other = swap_col(projected_grad)
    entry_sum = entry_mixer_weight(
        token_rows,
        projected_grad,
        projected_other,
        attended,
        attended_other,
        branch_rows,
        entry_block.shape,
    )
    entry_out = scatter_shards(tie(entry_sum, expand_grad).reshape(-1, grid_width))
    entry_outs = adam_rows(entry_out, 0, 3, [entry_weight, entry_mean, entry_square], rate)
    mixer_outs = adam_halves(
        entry_out,
        3 * depth // mixer_rows,
        [mixer_weight, mixer_mean, mixer_square],
        rate,
    )
    entry_back = scatter_rows(
        *project_back(projected_grad, projected_other, entry_block, [])
    )
    input_grad = hidden_grad + entry_back
    gain_local = jnp.zeros((4, D), jnp.float32)
    gain_local = lax.dynamic_update_slice(
        gain_local, jnp.stack([gain_first_post, gain_second_post]), (0, col_start)
    )
    gain_local = lax.dynamic_update_slice(
        gain_local, jnp.stack([gain_query, gain_key]), (2, head_start)
    )
    gain_grad = mesh_total(gain_local)
    gain_momentum, gain_variance, gain_updated = adam_step(
        gains, gain_grad, gain_mean, gain_square, 1.0, 0.0
    )
    return (
        layer_output,
        input_grad,
        gain_grad,
        gain_momentum,
        gain_variance,
        gain_updated,
        *entry_outs,
        *mixer_outs,
        *expand_outs,
        *reduce_outs,
    )


def solution(mesh):
    placed = (
        P(("dp", "row"), "col"),
        P(("dp", "row"), "col"),
        P("dp", None),
        P(),
        P(),
        P(),
        P(None, ("col", "dp"), "row"),
        P(None, ("col", "dp"), "row"),
        P(None, ("col", "dp"), "row"),
        P(("row", "dp"), "col"),
        P(("row", "dp"), "col"),
        P(("row", "dp"), "col"),
        P(None, ("col", "dp"), "row"),
        P(None, ("col", "dp"), "row"),
        P(None, ("col", "dp"), "row"),
        P(("row", "dp"), "col"),
        P(("row", "dp"), "col"),
        P(("row", "dp"), "col"),
    )
    return jax.shard_map(
        on_device,
        mesh=mesh,
        in_specs=placed,
        out_specs=(
            P(("dp", "row"), "col"),
            P(("dp", "row"), "col"),
            P(),
            P(),
            P(),
            P(),
            P(None, ("col", "dp"), "row"),
            P(None, ("col", "dp"), "row"),
            P(None, ("col", "dp"), "row"),
            P(None, ("col", "dp"), "row"),
            P(("row", "dp"), "col"),
            P(("row", "dp"), "col"),
            P(("row", "dp"), "col"),
            P(("row", "dp"), "col"),
            P(None, ("col", "dp"), "row"),
            P(None, ("col", "dp"), "row"),
            P(None, ("col", "dp"), "row"),
            P(None, ("col", "dp"), "row"),
            P(("row", "dp"), "col"),
            P(("row", "dp"), "col"),
            P(("row", "dp"), "col"),
            P(("row", "dp"), "col"),
        ),
        check_vma=False,
    )
```

```python
import jax
import jax.numpy as jnp
from jax import lax
from jax.experimental import pallas as pl
from jax.experimental.pallas import tpu as pltpu
from jax.sharding import PartitionSpec as P

D = 2048
HD = 128
FF = 8192
STEP = 10


NORM_EPSILON = 1e-06
ROPE_BASE = 500000.0
BETA_FIRST = 0.9
BETA_SECOND = 0.95
ADAM_EPSILON = 1e-08
WEIGHT_DECAY = 0.1


def layout_info(lengths, indices):
    closing = jnp.cumsum(lengths)
    starts = closing - lengths
    segment = jnp.sum((indices[:, None] >= closing[None, :]).astype(jnp.int32), 1)
    member = segment[:, None] == jnp.arange(lengths.shape[0], dtype=jnp.int32)[None, :]
    anchor = jnp.sum(jnp.where(member, starts[None, :], 0), 1)
    anchor = jnp.where(segment >= lengths.shape[0], closing[-1], anchor)
    return (segment, indices - anchor)


def rotary_tables(positions, width):
    half_width = width // 2
    freqs = ROPE_BASE ** (-jnp.arange(half_width, dtype=jnp.float32) * 2.0 / width)
    angles = positions.astype(jnp.float32)[:, None] * freqs[None, :]
    return (jnp.cos(angles), jnp.sin(angles))


def rotate(values, cosine, sine_table):
    half_width = values.shape[-1] // 2
    first = values[..., :half_width]
    second = values[..., half_width:]
    cos_wide = cosine[:, None, :]
    sin_wide = sine_table[:, None, :]
    return jnp.concatenate(
        [first * cos_wide - second * sin_wide, second * cos_wide + first * sin_wide], -1
    )


def rotate_back(values, cosine, sine_table):
    half_width = values.shape[-1] // 2
    first = values[..., :half_width]
    second = values[..., half_width:]
    cos_wide = cosine[:, None, :]
    sin_wide = sine_table[:, None, :]
    return jnp.concatenate(
        [first * cos_wide + second * sin_wide, second * cos_wide - first * sin_wide], -1
    )


def adam_step(weight, gradient, moment, square, step_rate, decay_rate):
    moment_new = BETA_FIRST * moment + (1.0 - BETA_FIRST) * gradient
    square_new = BETA_SECOND * square + (1.0 - BETA_SECOND) * gradient * gradient
    ratio = (
        moment_new
        / (1.0 - BETA_FIRST**STEP)
        / (jnp.sqrt(square_new / (1.0 - BETA_SECOND**STEP)) + ADAM_EPSILON)
    )
    return (moment_new, square_new, weight - step_rate * (ratio + decay_rate * weight))


def swap(values, axis, distance):
    return lax.ppermute(values, axis, [(i, i ^ distance) for i in range(lax.axis_size(axis))])


def swap_col(values):
    return swap(values, "col", 1)


def feature_total(values):
    return values + swap_col(values)


def grid_total(values):
    values = feature_total(values)
    count = lax.axis_size("row")
    blocks = values.reshape(values.shape[0], count, -1)
    total = blocks
    for k in range(1, count):
        part = swap(blocks, "row", k)
        total = total + jnp.stack([part[:, j ^ k] for j in range(count)], 1)
    return total.reshape(values.shape)


def axes_total(values, axes):
    for axis in axes:
        distance = 1
        while distance < lax.axis_size(axis):
            values = values + swap(values, axis, distance)
            distance *= 2
    return values


def gather_rows(block):
    count = lax.axis_size("row")
    if count != 4:
        return jnp.concatenate([block] + [swap(block, "row", k) for k in range(1, count)], 0)
    half = block.shape[0] // 2
    first = swap(block, "row", 1)
    second = swap(block, "row", 2)
    return jnp.concatenate(
        [block, first, second, swap(first[:half], "row", 2), swap(second[half:], "row", 1)], 0
    )


def scatter_rows(own, *lows):
    for k, low in enumerate(lows):
        own = own + swap(low, "row", k + 1).astype(jnp.float32)
    return own


VMEM = 48 * 1024 * 1024
TILE = 256
PART = 512
NN = (((1,), (0,)), ((), ()))
NT = (((1,), (1,)), ((), ()))
TN = (((0,), (0,)), ((), ()))


def mm(left, right, dims=NN):
    return lax.dot_general(left, right, dims, preferred_element_type=jnp.float32)


def run(body, grid, ins, outs, earlier=()):
    place = lax.axis_index("col").astype(jnp.int32).reshape(1)

    def kernel(c, *refs):
        body(c, *refs[: len(ins)], *refs[len(ins) + len(earlier) :])

    return pl.pallas_call(
        kernel,
        grid_spec=pltpu.PrefetchScalarGridSpec(
            num_scalar_prefetch=1,
            grid=grid,
            in_specs=[pl.BlockSpec(block, where) for _, block, where in ins]
            + [pl.BlockSpec(memory_space=pl.ANY)] * len(earlier),
            out_specs=[pl.BlockSpec(block, where) for _, _, block, where in outs],
        ),
        out_shape=[jax.ShapeDtypeStruct(shape, kind) for shape, kind, _, _ in outs],
        compiler_params=pltpu.CompilerParams(vmem_limit_bytes=VMEM),
        cost_estimate=pl.CostEstimate(flops=1, bytes_accessed=1, transcendentals=0),
    )(place, *[array for array, _, _ in ins], *earlier)


def whole(array):
    zeros = (0,) * array.ndim
    return (array, array.shape, lambda *_: zeros)


def tie_body(value, *refs):
    pass


def tie(value, *earlier):
    return pl.pallas_call(
        tie_body,
        in_specs=[pl.BlockSpec(memory_space=pl.ANY)] * (1 + len(earlier)),
        out_specs=pl.BlockSpec(memory_space=pl.ANY),
        out_shape=jax.ShapeDtypeStruct(value.shape, value.dtype),
        input_output_aliases={0: 0},
        cost_estimate=pl.CostEstimate(flops=1, bytes_accessed=1, transcendentals=0),
    )(value, *earlier)


def ring_gather(shards):
    count = lax.axis_size("dp")
    rows = shards[0].shape[0]
    joined = jnp.zeros((count, len(shards)) + shards[0].shape, shards[0].dtype)
    pairs = [(i, (i - 1) % count) for i in range(count)]
    for step in range(count):
        spot = lax.rem(lax.axis_index("dp") + step, count)
        if step:
            shards = [lax.ppermute(shard, "dp", pairs) for shard in shards]
        for j, shard in enumerate(shards):
            joined = lax.dynamic_update_slice(joined, shard[None, None], (spot, j, 0, 0))
    return joined.reshape((count, len(shards) * rows) + joined.shape[3:])


def ring_scatter(values, wait=None):
    count = lax.axis_size("dp")
    pairs = [(i, (i - 1) % count) for i in range(count)]

    def term(value, step):
        spot = lax.rem(lax.axis_index("dp") + step, count)
        return lax.dynamic_index_in_dim(value, spot, 0, keepdims=False)

    totals = [term(value, 1) for value in values]
    for step in range(1, count):
        arrived = [lax.ppermute(total, "dp", pairs) for total in totals]
        if step == 2 and wait is not None:
            arrived[0] = tie(arrived[0], wait)
        totals = [
            (term(value, step + 1).astype(jnp.float32) + part.astype(jnp.float32)).astype(
                value.dtype
            )
            for value, part in zip(values, arrived)
        ]
    return totals


def row_outs(extent, columns, tile):
    count = lax.axis_size("row")
    rows = extent // count
    return [
        ((rows, columns), kind, (rows, tile), lambda n, c: (0, n))
        for kind in [jnp.float32] + [jnp.bfloat16] * (count - 1)
    ]


def put_rows(total, outs):
    rows = outs[0].shape[0]
    for k, out in enumerate(outs):
        out[...] = total[k * rows : (k + 1) * rows].astype(out.dtype)


def project(rows, block):
    n, _, d, width = block.shape
    half = width // 2
    extent = rows.shape[0]

    def body(c, x, mine, theirs, own, far):
        own[0] = mm(x[...], mine[...].reshape(n * d, half))
        far[0] = mm(x[...], theirs[...].reshape(n * d, half))

    return run(
        body,
        (3,),
        [
            whole(rows),
            (block, (n, 1, d, half), lambda k, c: (0, k, 0, c[0])),
            (block, (n, 1, d, half), lambda k, c: (0, k, 0, 1 - c[0])),
        ],
        [
            ((3, extent, half), jnp.float32, (1, extent, half), lambda k, c: (k, 0, 0)),
            ((3, extent, half), jnp.float32, (1, extent, half), lambda k, c: (k, 0, 0)),
        ],
    )


def mix(own, other, block):
    n, _, d, width = block.shape
    extent, half = own.shape

    def body(c, x, y, mine, theirs, *outs):
        parts = []
        a = mine[...].reshape(n // 2, 2, d // 2, width)
        b = theirs[...].reshape(n // 2, 2, d // 2, width)
        for h in range(2):
            parts.append(
                mm(x[...], a[:, h].reshape(half, width)) + mm(y[...], b[:, h].reshape(half, width))
            )
        put_rows(jnp.concatenate(parts, 1), outs)

    return run(
        body,
        (1,),
        [
            whole(own),
            whole(other),
            (block, (n // 2, 1, d, width), lambda n, c: (c[0], 3, 0, 0)),
            (block, (n // 2, 1, d, width), lambda n, c: (1 - c[0], 3, 0, 0)),
        ],
        row_outs(extent, 2 * width, 2 * width),
    )


def mix_back(own, other, block, far):
    n, _, d, width = block.shape
    extent = own.shape[0]
    half = n * d // 4

    def body(c, x, y, mine, theirs, out):
        a = mine[...].reshape(n // 2, 2, d // 2, width)
        b = theirs[...].reshape(n // 2, 2, d // 2, width)
        total = None
        for h in range(2):
            cols = slice(h * width, (h + 1) * width)
            part = mm(x[:, cols], a[:, h].reshape(half, width), NT) + mm(
                y[:, cols], b[:, h].reshape(half, width), NT
            )
            total = part if total is None else total + part
        out[...] = total.astype(jnp.bfloat16)

    return run(
        body,
        (1,),
        [
            whole(own),
            whole(other),
            (block, (n // 2, 1, d, width), lambda n, c: (c[0], 3, 0, 0)),
            whole(far),
        ],
        [((extent, half), jnp.bfloat16, (extent, half), lambda n, c: (0, 0))],
    )[0]


def piece_order(pieces):
    half = pieces // 2
    return lambda j, c: jnp.where(j < half, c[0] * half + j, (1 - c[0]) * half + j - half)


def widen_send(rows, block, t):
    n, _, d, width = block.shape
    half = width // PART // 2
    extent = rows.shape[0]

    def body(c, x, w, out):
        out[0] = mm(x[...], w[...].reshape(n * d, PART)).astype(jnp.bfloat16)

    return run(
        body,
        (2,),
        [
            whole(rows),
            (block, (n, 1, d, PART), lambda k, c: (0, k, 0, (1 - c[0]) * half + t)),
        ],
        [((2, extent, PART), jnp.bfloat16, (1, extent, PART), lambda k, c: (k, 0, 0))],
    )[0]


def widen(rows, block, arrived, t):
    n, _, d, width = block.shape
    half = width // PART // 2
    extent = rows.shape[0]
    tiles = PART // TILE

    def body(c, x, gate, up, far, kept, out):
        g = mm(x[...], gate[...].reshape(n * d, TILE)) + far[0].astype(jnp.float32)
        u = mm(x[...], up[...].reshape(n * d, TILE)) + far[1].astype(jnp.float32)
        kept[0] = g
        kept[1] = u
        out[...] = (g * jax.nn.sigmoid(g) * u).astype(jnp.bfloat16)

    return run(
        body,
        (tiles,),
        [
            whole(rows),
            (block, (n, 1, d, TILE), lambda i, c: (0, 0, 0, (c[0] * half + t) * tiles + i)),
            (block, (n, 1, d, TILE), lambda i, c: (0, 1, 0, (c[0] * half + t) * tiles + i)),
            (arrived, (2, extent, TILE), lambda i, c: (0, 0, i)),
        ],
        [
            ((2, extent, PART), jnp.float32, (2, extent, TILE), lambda i, c: (0, 0, i)),
            ((extent, PART), jnp.bfloat16, (extent, TILE), lambda i, c: (0, i)),
        ],
    )


def narrow(own, other, pieces, earlier=()):
    count, part, columns = pieces.shape
    half = count // 2
    extent = own[0].shape[0]

    def body(c, *refs):
        xs = refs[:count]
        mine, theirs, *outs = refs[count:]
        total = None
        for j, x in enumerate(xs):
            piece = mm(x[...], (mine if j < half else theirs)[j % half])
            total = piece if total is None else total + piece
        put_rows(total, outs)

    return run(
        body,
        (columns // TILE,),
        [whole(x) for x in own + other]
        + [
            (pieces, (half, part, TILE), lambda n, c: (c[0], 0, n)),
            (pieces, (half, part, TILE), lambda n, c: (1 - c[0], 0, n)),
        ],
        row_outs(extent, columns, TILE),
        earlier,
    )


def narrow_weight(own, other, grads, earlier=()):
    groups = len(grads)
    half = len(own[0])
    extent, part = own[0][0].shape
    columns = grads[0].shape[1]
    order = piece_order(2 * half)
    flat = [x for j in range(2 * half) for x in ([g[j] for g in own] if j < half else [g[j - half] for g in other])]

    def body(c, *refs):
        gs = refs[len(flat) : len(flat) + groups]
        out = refs[-1]
        for j in range(2 * half):

            @pl.when(pl.program_id(0) == j)
            def _(j=j):
                total = None
                for g in range(groups):
                    piece = mm(refs[j * groups + g][...], gs[g][...], TN)
                    total = piece if total is None else total + piece
                out[0] = total.astype(jnp.bfloat16)

    return run(
        body,
        (2 * half,),
        [whole(x) for x in flat] + [whole(g) for g in grads],
        [
            (
                (2 * half, part, columns),
                jnp.bfloat16,
                (1, part, columns),
                lambda i, c: (order(i, c), 0, 0),
            )
        ],
        earlier,
    )[0]


def narrow_back(own, other, pieces, far, kept, t, earlier=()):
    count, part, columns = pieces.shape
    half = count // 2
    extent = own.shape[0]
    tiles = part // TILE

    def body(c, x, y, mine, theirs, saved, out):
        grad = mm(x[...], mine[0], NT) + mm(y[...], theirs[0], NT)
        gate = saved[0]
        sig = jax.nn.sigmoid(gate)
        out[0] = (grad * saved[1] * sig * (1.0 + gate * (1.0 - sig))).astype(jnp.bfloat16)
        out[1] = (grad * (gate * sig)).astype(jnp.bfloat16)

    return run(
        body,
        (tiles,),
        [
            whole(own),
            whole(other),
            (pieces, (1, TILE, columns), lambda i, c: (c[0] * half + t, i, 0)),
            (far, (1, TILE, columns), lambda i, c: (t, i, 0)),
            (kept, (2, extent, TILE), lambda i, c: (0, 0, i)),
        ],
        [((2, extent, part), jnp.bfloat16, (2, extent, TILE), lambda i, c: (0, 0, i))],
        earlier,
    )[0]


def widen_back(own, other, block, earlier=()):
    n, _, d, width = block.shape
    count = width // PART
    extent = own[0].shape[1]
    group = TILE // d
    order = piece_order(count)

    def body(c, *refs):
        outs = refs[2 * count :]
        total = None
        for x, w in zip(refs[:count], refs[count : 2 * count]):
            for k in range(2):
                piece = mm(x[k], w[:, k].reshape(TILE, PART), NT)
                total = piece if total is None else total + piece
        put_rows(total, outs)

    return run(
        body,
        (n * d // TILE,),
        [whole(x) for x in own + other]
        + [
            (block, (group, 2, d, PART), lambda i, c, j=j: (i, 0, 0, order(j, c)))
            for j in range(count)
        ],
        row_outs(extent, n * d, TILE),
        earlier,
    )


def widen_weight(rows, own, other, shape, earlier=()):
    n, _, d, width = shape
    groups = len(rows)
    half = len(own[0])
    extent, features = rows[0].shape
    group = TILE // d
    order = piece_order(2 * half)
    flat = [x for j in range(2 * half) for x in ([g[j] for g in own] if j < half else [g[j - half] for g in other])]

    def body(c, *refs):
        xs = refs[:groups]
        ys = refs[groups:-1]
        out = refs[-1]
        for j in range(2 * half):

            @pl.when(pl.program_id(1) == j)
            def _(j=j):
                for k in range(2):
                    total = None
                    for g in range(groups):
                        piece = mm(xs[g][...], ys[j * groups + g][k], TN)
                        total = piece if total is None else total + piece
                    out[:, k] = total.astype(jnp.bfloat16).reshape(group, d, PART)

    return run(
        body,
        (features // TILE, 2 * half),
        [(x, (extent, TILE), lambda i, j, c: (0, i)) for x in rows] + [whole(y) for y in flat],
        [
            (
                shape,
                jnp.bfloat16,
                (group, 2, d, PART),
                lambda i, j, c: (i, 0, 0, order(j, c)),
            )
        ],
        earlier,
    )[0]


def project_back(own, other, block, earlier):
    n, _, d, width = block.shape
    half = width // 2
    extent = own.shape[1]
    group = TILE // d

    def body(c, x, y, mine, theirs, *outs):
        total = None
        for a, w in ((x, mine), (y, theirs)):
            for k in range(3):
                piece = mm(a[k], w[:, k].reshape(TILE, half), NT)
                total = piece if total is None else total + piece
        put_rows(total, outs)

    return run(
        body,
        (n * d // TILE,),
        [
            whole(own),
            whole(other),
            (block, (group, 4, d, half), lambda i, c: (i, 0, 0, c[0])),
            (block, (group, 4, d, half), lambda i, c: (i, 0, 0, 1 - c[0])),
        ],
        row_outs(extent, n * d, TILE),
        earlier,
    )


def entry_mixer_weight(rows, own, other, heads, far_heads, grads, shape):
    n, _, d, width = shape
    half = width // 2
    extent, features = rows.shape
    group = TILE // d
    low = jnp.bfloat16
    fine = TILE // 2

    def body(c, x, y, z, a, b, g, first, second):
        for k in range(3):
            out = (first, second)[k // 2]
            mine = mm(x[...], y[k], TN).astype(low).reshape(group, d, half)
            theirs = mm(x[...], z[k], TN).astype(low).reshape(group, d, half)
            for side in range(2):

                @pl.when(c[0] == side)
                def _():
                    out[:, k % 2, :, side * half : (side + 1) * half] = mine
                    out[:, k % 2, :, (1 - side) * half : (2 - side) * half] = theirs

        i = pl.program_id(0)
        for source, first in ((a, c[0] * 2), (b, (1 - c[0]) * 2)):
            for j in range(2):

                @pl.when(i == first + j)
                def _():
                    piece = mm(source[:, j * fine : (j + 1) * fine], g[...], TN).astype(low)
                    for h in range(2):
                        second[:, 1, h * (d // 2) : (h + 1) * (d // 2), :] = piece[
                            :, h * width : (h + 1) * width
                        ].reshape(group, d // 2, width)

    return run(
        body,
        (features // TILE,),
        [(rows, (extent, TILE), lambda i, c: (0, i))]
        + [whole(v) for v in (own, other, heads, far_heads, grads)],
        [((n, 2, d, width), low, (group, 2, d, width), lambda i, c: (i, 0, 0, 0))] * 2,
    )


def take_half(block, axis, which):
    half = block.shape[axis] // 2
    return lax.dynamic_slice_in_dim(block, which * half, half, axis)


def gather_shards(shard):
    return lax.all_gather(shard, "dp", axis=0, tiled=True)


def scatter_shards(values):
    return lax.psum_scatter(values, "dp", scatter_dimension=0, tiled=True)


def adam_values(weight, gradient, moment, square, step_rate):
    moment_new, square_new, updated = adam_step(
        weight, gradient, moment, square, step_rate, WEIGHT_DECAY
    )
    return (gradient, moment_new, square_new, updated)


def adam_call(body, grid, gradients, state, block, where, earlier=()):
    return run(
        body,
        grid,
        gradients + [(array, block, where) for array in state],
        [(state[0].shape, jnp.float32, block, where)] * 4,
        earlier,
    )


def adam_rows(gradient, first, blocks, state, step_rate, earlier=()):
    d = state[0].shape[-2] // (blocks if state[0].ndim == 2 else 1)
    width = state[0].shape[-1]
    lead = (1,) * (state[0].ndim - 2)

    def body(c, g, weight, moment, square, *outs):
        value = g[...].astype(jnp.float32).reshape(weight.shape)
        for out, result in zip(
            outs, adam_values(weight[...], value, moment[...], square[...], step_rate)
        ):
            out[...] = result

    return adam_call(
        body,
        (blocks,),
        [(gradient, (d, width), lambda k, c: (first + k, 0))],
        state,
        lead + (d, width),
        (lambda k, c: (k, 0, 0)) if lead else (lambda k, c: (k, 0)),
        earlier,
    )


def adam_halves(gradient, first, state, step_rate):
    rows, width = state[0].shape
    block = (rows, width // 2)

    def body(c, g, weight, moment, square, *outs):
        value = g[...].astype(jnp.float32)
        for out, result in zip(
            outs, adam_values(weight[...], value, moment[...], square[...], step_rate)
        ):
            out[...] = result

    return adam_call(
        body,
        (2,),
        [(gradient, block, lambda k, c: (first + k, 0))],
        state,
        block,
        lambda k, c: (0, k),
    )


def on_device(
    tokens,
    cotangent,
    seq_lengths,
    gains,
    gain_mean,
    gain_square,
    entry_weight,
    entry_mean,
    entry_square,
    mixer_weight,
    mixer_mean,
    mixer_square,
    expand_weight,
    expand_mean,
    expand_square,
    reduce_weight,
    reduce_mean,
    reduce_square,
):
    low = jnp.bfloat16
    shards = lax.axis_size("dp")
    side = lax.axis_index("col")
    depth, grid_width = entry_weight.shape[1:]
    mixer_rows = mixer_weight.shape[0]
    entry_shard = jnp.concatenate(
        [
            entry_weight.astype(low).reshape(-1, grid_width),
            mixer_weight[:, :grid_width].astype(low),
            mixer_weight[:, grid_width:].astype(low),
        ],
        0,
    )
    if shards > 4:
        entry_block = gather_shards(entry_shard)
    else:
        entry_block = ring_gather([entry_shard[: 2 * depth], entry_shard[2 * depth :]])
    entry_block = entry_block.reshape(shards, 4, depth, grid_width)
    reduce_low = reduce_weight.astype(low)
    expand_low = expand_weight.astype(low)
    expand_block = gather_shards(
        tie(expand_low, entry_block).reshape(-1, expand_low.shape[2])
    )
    expand_block = expand_block.reshape((shards,) + expand_weight.shape)
    reduce_pieces = gather_shards(reduce_low).reshape(4, -1, reduce_low.shape[1])
    halves = range(2)

    row_size = lax.axis_size("row")
    col_size = lax.axis_size("col")
    local_rows = tokens.shape[0]
    feature_local = tokens.shape[1]
    extent = local_rows * row_size
    row_index = lax.axis_index("row")
    blocks = row_index ^ jnp.arange(row_size, dtype=jnp.int32)
    indices = (
        blocks[:, None] * local_rows + jnp.arange(local_rows, dtype=jnp.int32)[None, :]
    ).reshape(extent)
    segment, positions = layout_info(seq_lengths[0], indices)
    local_valid = (segment[:local_rows] < seq_lengths.shape[1]).astype(jnp.float32)
    head_width = grid_width // col_size
    head_start = (row_index * col_size + lax.axis_index("col")) * head_width
    col_start = lax.axis_index("col") * feature_local
    post_gain = lax.dynamic_slice_in_dim(gains[0:2], col_start, feature_local, 1)
    head_gain = lax.dynamic_slice_in_dim(gains[2:4], head_start, head_width, 1)
    head_count = head_width // HD
    shrink = HD ** (-0.5)
    inputs = tokens.astype(jnp.float32)
    token_rows = gather_rows(tokens)
    projected, projected_far = project(token_rows, entry_block)
    projected = projected + swap_col(projected_far)
    squares = grid_total(jnp.sum(projected[0:2] * projected[0:2], -1))
    query_scale = lax.rsqrt(squares[0] / D + NORM_EPSILON)[:, None]
    key_scale = lax.rsqrt(squares[1] / D + NORM_EPSILON)[:, None]
    query_hat = projected[0] * query_scale
    key_hat = projected[1] * key_scale
    cosine, sine_table = rotary_tables(positions, HD)
    query_rot = rotate(
        (query_hat * head_gain[0]).reshape(extent, head_count, HD), cosine, sine_table
    ).astype(jnp.bfloat16)
    key_rot = rotate(
        (key_hat * head_gain[1]).reshape(extent, head_count, HD), cosine, sine_table
    ).astype(jnp.bfloat16)
    value_rows = projected[2].astype(jnp.bfloat16).reshape(extent, head_count, HD)
    block_rows = min(512, extent)

    def block_scores(offset):
        query_block = query_rot[offset : offset + block_rows]
        scores = (
            jnp.einsum("qhd,khd->hqk", query_block, key_rot, preferred_element_type=jnp.float32)
            * shrink
        )
        rows_here = indices[offset : offset + block_rows]
        allowed = (segment[offset : offset + block_rows][:, None] == segment[None, :]) & (
            indices[None, :] <= rows_here[:, None]
        )
        return (query_block, jnp.where(allowed[None], scores, -1e30))

    outputs = []
    logsums = []
    for offset in range(0, extent, block_rows):
        query_block, masked = block_scores(offset)
        peak = jnp.max(masked, -1, keepdims=True)
        expo = jnp.exp(masked - peak)
        totals = jnp.sum(expo, -1, keepdims=True)
        shares = (expo / totals).astype(jnp.bfloat16)
        outputs.append(
            jnp.einsum("hqk,khd->qhd", shares, value_rows, preferred_element_type=jnp.float32)
        )
        logsums.append(peak + jnp.log(totals))
    attended = jnp.concatenate(outputs, 0).astype(jnp.bfloat16).reshape(extent, head_width)
    attended_other = swap_col(attended)
    branch = scatter_rows(*mix(attended, attended_other, entry_block))
    branch_scale = lax.rsqrt(feature_total(jnp.sum(branch * branch, -1)) / D + NORM_EPSILON)[
        :, None
    ]
    branch_hat = branch * branch_scale
    hidden = inputs + branch_hat * post_gain[0]
    hidden_rows = gather_rows(hidden.astype(jnp.bfloat16))
    sent = [swap_col(widen_send(hidden_rows, expand_block, t)) for t in halves]
    kept, product = zip(*[widen(hidden_rows, expand_block, sent[t], t) for t in halves])
    product = list(product)
    product_other = [swap_col(value) for value in product]
    second = scatter_rows(*narrow(product, product_other, reduce_pieces))
    upstream = cotangent.astype(jnp.float32) * local_valid[:, None]
    scaled = upstream * post_gain[1]
    totals = feature_total(
        jnp.stack([jnp.sum(second * second, -1), jnp.sum(scaled * second, -1)])
    )
    second_scale = lax.rsqrt(totals[0] / D + NORM_EPSILON)[:, None]
    second_hat = second * second_scale
    layer_output = hidden + second_hat * post_gain[1]
    gain_second_post = jnp.sum(upstream * second_hat, 0)
    inner_sum = totals[1][:, None] * second_scale
    second_grad = (second_scale * (scaled - second_hat * inner_sum / D)).astype(jnp.bfloat16)
    second_rows = gather_rows(second_grad)
    second_other = swap_col(second_rows)
    reduce_sum = narrow_weight([product], [product_other], [second_rows])
    reduce_far = swap_col(take_half(reduce_pieces, 0, 1 - side))
    gated_grad = [
        narrow_back(
            second_rows, second_other, reduce_pieces, reduce_far, kept[t], t, [reduce_sum]
        )
        for t in halves
    ]
    gated_other = [swap_col(value) for value in gated_grad]
    hidden_parts = widen_back(gated_grad, gated_other, expand_block)
    hidden_back = scatter_rows(*hidden_parts)
    expand_sum = widen_weight(
        [hidden_rows], [gated_grad], [gated_other], expand_block.shape, [hidden_parts[1]]
    )
    rate = 2.0 * D ** (-0.5)
    reduce_grad = scatter_shards(reduce_sum.reshape(-1, reduce_low.shape[1]))
    expand_grad = scatter_shards(
        tie(expand_sum, reduce_grad).reshape(-1, expand_low.shape[2])
    )
    reduce_outs = adam_rows(
        reduce_grad, 0, 2, [reduce_weight, reduce_mean, reduce_square], 2.0 * FF ** (-0.5)
    )
    hidden_grad = upstream + hidden_back
    gain_first_post = jnp.sum(hidden_grad * branch_hat, 0)
    scaled = hidden_grad * post_gain[0]
    inner_sum = feature_total(jnp.sum(scaled * branch_hat, -1))
    branch_grad = (branch_scale * (scaled - branch_hat * inner_sum[:, None] / D)).astype(
        jnp.bfloat16
    )
    branch_rows = gather_rows(branch_grad)
    branch_other = swap_col(branch_rows)
    mixer_far = swap_col(take_half(entry_block[:, 3:], 0, 1 - side))
    attended_low = mix_back(branch_rows, branch_other, entry_block, mixer_far).reshape(
        extent, head_count, HD
    )
    query_parts = []
    key_accum = jnp.zeros((extent, head_count, HD), jnp.float32)
    value_accum = jnp.zeros((extent, head_count, HD), jnp.float32)
    for number, offset in enumerate(range(0, extent, block_rows)):
        query_block, masked = block_scores(offset)
        shares = jnp.exp(masked - logsums[number])
        grad_block = attended_low[offset : offset + block_rows]
        flow_grad = jnp.einsum(
            "qhd,khd->hqk", grad_block, value_rows, preferred_element_type=jnp.float32
        )
        row_delta = jnp.sum(shares * flow_grad, -1, keepdims=True)
        score_grad = (shares * (flow_grad - row_delta)).astype(jnp.bfloat16)
        query_parts.append(
            jnp.einsum("hqk,khd->qhd", score_grad, key_rot, preferred_element_type=jnp.float32)
            * shrink
        )
        key_accum = (
            key_accum
            + jnp.einsum(
                "hqk,qhd->khd", score_grad, query_block, preferred_element_type=jnp.float32
            )
            * shrink
        )
        value_accum = value_accum + jnp.einsum(
            "hqk,qhd->khd",
            shares.astype(jnp.bfloat16),
            grad_block,
            preferred_element_type=jnp.float32,
        )
    query_grad = rotate_back(jnp.concatenate(query_parts, 0), cosine, sine_table).reshape(
        extent, head_width
    )
    key_grad = rotate_back(key_accum, cosine, sine_table).reshape(extent, head_width)
    gain_query = jnp.sum(query_grad * query_hat, 0)
    gain_key = jnp.sum(key_grad * key_hat, 0)
    query_scaled = query_grad * head_gain[0]
    key_scaled = key_grad * head_gain[1]
    head_dots = grid_total(
        jnp.stack(
            [jnp.sum(query_scaled * query_hat, -1), jnp.sum(key_scaled * key_hat, -1)]
        )
    )
    query_raw = query_scale * (query_scaled - query_hat * head_dots[0][:, None] / D)
    key_raw = key_scale * (key_scaled - key_hat * head_dots[1][:, None] / D)
    value_grad = value_accum.reshape(extent, head_width)
    projected_grad = jnp.stack([query_raw, key_raw, value_grad]).astype(low)
    projected_other = swap_col(projected_grad)
    gain_local = jnp.zeros((4, D), jnp.float32)
    gain_local = lax.dynamic_update_slice(
        gain_local, jnp.stack([gain_first_post, gain_second_post]), (0, col_start)
    )
    gain_local = lax.dynamic_update_slice(
        gain_local, jnp.stack([gain_query, gain_key]), (2, head_start)
    )
    gain_local = axes_total(gain_local, ("dp",))
    entry_sum = entry_mixer_weight(
        token_rows,
        projected_grad,
        projected_other,
        attended,
        attended_other,
        branch_rows,
        entry_block.shape,
    )
    expand_outs = adam_rows(
        expand_grad, 0, 2, [expand_weight, expand_mean, expand_square], rate
    )
    if shards > 4:
        joined = jnp.concatenate(entry_sum, 1)
        entry_out = scatter_shards(tie(joined, expand_grad).reshape(-1, grid_width))
    else:
        entry_out = jnp.concatenate(
            ring_scatter([tie(value, gain_local) for value in entry_sum], expand_outs[0]), 0
        ).reshape(-1, grid_width)
    entry_outs = adam_rows(entry_out, 0, 3, [entry_weight, entry_mean, entry_square], rate)
    mixer_outs = adam_halves(
        entry_out,
        3 * depth // mixer_rows,
        [mixer_weight, mixer_mean, mixer_square],
        rate,
    )
    entry_back = scatter_rows(
        *project_back(projected_grad, projected_other, entry_block, [])
    )
    input_grad = hidden_grad + entry_back
    gain_grad = axes_total(gain_local, ("col", "row"))
    gain_momentum, gain_variance, gain_updated = adam_step(
        gains, gain_grad, gain_mean, gain_square, 1.0, 0.0
    )
    return (
        layer_output,
        input_grad,
        gain_grad,
        gain_momentum,
        gain_variance,
        gain_updated,
        *entry_outs,
        *mixer_outs,
        *expand_outs,
        *reduce_outs,
    )


def solution(mesh):
    placed = (
        P(("dp", "row"), "col"),
        P(("dp", "row"), "col"),
        P("dp", None),
        P(),
        P(),
        P(),
        P(None, ("col", "dp"), "row"),
        P(None, ("col", "dp"), "row"),
        P(None, ("col", "dp"), "row"),
        P(("row", "dp"), "col"),
        P(("row", "dp"), "col"),
        P(("row", "dp"), "col"),
        P(None, ("col", "dp"), "row"),
        P(None, ("col", "dp"), "row"),
        P(None, ("col", "dp"), "row"),
        P(("row", "dp"), "col"),
        P(("row", "dp"), "col"),
        P(("row", "dp"), "col"),
    )
    return jax.shard_map(
        on_device,
        mesh=mesh,
        in_specs=placed,
        out_specs=(
            P(("dp", "row"), "col"),
            P(("dp", "row"), "col"),
            P(),
            P(),
            P(),
            P(),
            P(None, ("col", "dp"), "row"),
            P(None, ("col", "dp"), "row"),
            P(None, ("col", "dp"), "row"),
            P(None, ("col", "dp"), "row"),
            P(("row", "dp"), "col"),
            P(("row", "dp"), "col"),
            P(("row", "dp"), "col"),
            P(("row", "dp"), "col"),
            P(None, ("col", "dp"), "row"),
            P(None, ("col", "dp"), "row"),
            P(None, ("col", "dp"), "row"),
            P(None, ("col", "dp"), "row"),
            P(("row", "dp"), "col"),
            P(("row", "dp"), "col"),
            P(("row", "dp"), "col"),
            P(("row", "dp"), "col"),
        ),
        check_vma=False,
    )
```

```python
import jax
import jax.numpy as jnp
from jax import lax
from jax.experimental import pallas as pl
from jax.experimental.pallas import tpu as pltpu
from jax.sharding import PartitionSpec as P

D = 2048
HD = 128
FF = 8192
STEP = 10


NORM_EPSILON = 1e-06
ROPE_BASE = 500000.0
BETA_FIRST = 0.9
BETA_SECOND = 0.95
ADAM_EPSILON = 1e-08
WEIGHT_DECAY = 0.1


def layout_info(lengths, indices):
    closing = jnp.cumsum(lengths)
    starts = closing - lengths
    segment = jnp.sum((indices[:, None] >= closing[None, :]).astype(jnp.int32), 1)
    member = segment[:, None] == jnp.arange(lengths.shape[0], dtype=jnp.int32)[None, :]
    anchor = jnp.sum(jnp.where(member, starts[None, :], 0), 1)
    anchor = jnp.where(segment >= lengths.shape[0], closing[-1], anchor)
    return (segment, indices - anchor)


def rotary_tables(positions, width):
    half_width = width // 2
    freqs = ROPE_BASE ** (-jnp.arange(half_width, dtype=jnp.float32) * 2.0 / width)
    angles = positions.astype(jnp.float32)[:, None] * freqs[None, :]
    return (jnp.cos(angles), jnp.sin(angles))


def rotate(values, cosine, sine_table):
    half_width = values.shape[-1] // 2
    first = values[..., :half_width]
    second = values[..., half_width:]
    cos_wide = cosine[:, None, :]
    sin_wide = sine_table[:, None, :]
    return jnp.concatenate(
        [first * cos_wide - second * sin_wide, second * cos_wide + first * sin_wide], -1
    )


def rotate_back(values, cosine, sine_table):
    half_width = values.shape[-1] // 2
    first = values[..., :half_width]
    second = values[..., half_width:]
    cos_wide = cosine[:, None, :]
    sin_wide = sine_table[:, None, :]
    return jnp.concatenate(
        [first * cos_wide + second * sin_wide, second * cos_wide - first * sin_wide], -1
    )


def adam_step(weight, gradient, moment, square, step_rate, decay_rate):
    moment_new = BETA_FIRST * moment + (1.0 - BETA_FIRST) * gradient
    square_new = BETA_SECOND * square + (1.0 - BETA_SECOND) * gradient * gradient
    ratio = (
        moment_new
        / (1.0 - BETA_FIRST**STEP)
        / (jnp.sqrt(square_new / (1.0 - BETA_SECOND**STEP)) + ADAM_EPSILON)
    )
    return (moment_new, square_new, weight - step_rate * (ratio + decay_rate * weight))


def swap(values, axis, distance):
    return lax.ppermute(values, axis, [(i, i ^ distance) for i in range(lax.axis_size(axis))])


def swap_col(values):
    return swap(values, "col", 1)


def feature_total(values):
    return values + swap_col(values)


def grid_total(values):
    values = feature_total(values)
    count = lax.axis_size("row")
    blocks = values.reshape(values.shape[0], count, -1)
    total = blocks
    for k in range(1, count):
        part = swap(blocks, "row", k)
        total = total + jnp.stack([part[:, j ^ k] for j in range(count)], 1)
    return total.reshape(values.shape)


def axes_total(values, axes):
    for axis in axes:
        distance = 1
        while distance < lax.axis_size(axis):
            values = values + swap(values, axis, distance)
            distance *= 2
    return values


def gather_rows(block):
    count = lax.axis_size("row")
    if count != 4:
        return jnp.concatenate([block] + [swap(block, "row", k) for k in range(1, count)], 0)
    half = block.shape[0] // 2
    first = swap(block, "row", 1)
    second = swap(block, "row", 2)
    return jnp.concatenate(
        [block, first, second, swap(first[:half], "row", 2), swap(second[half:], "row", 1)], 0
    )


def scatter_rows(own, *lows):
    for k, low in enumerate(lows):
        own = own + swap(low, "row", k + 1).astype(jnp.float32)
    return own


VMEM = 48 * 1024 * 1024
TILE = 256
PART = 512
NN = (((1,), (0,)), ((), ()))
NT = (((1,), (1,)), ((), ()))
TN = (((0,), (0,)), ((), ()))


def mm(left, right, dims=NN):
    return lax.dot_general(left, right, dims, preferred_element_type=jnp.float32)


def run(body, grid, ins, outs, earlier=()):
    place = lax.axis_index("col").astype(jnp.int32).reshape(1)

    def kernel(c, *refs):
        body(c, *refs[: len(ins)], *refs[len(ins) + len(earlier) :])

    return pl.pallas_call(
        kernel,
        grid_spec=pltpu.PrefetchScalarGridSpec(
            num_scalar_prefetch=1,
            grid=grid,
            in_specs=[pl.BlockSpec(block, where) for _, block, where in ins]
            + [pl.BlockSpec(memory_space=pl.ANY)] * len(earlier),
            out_specs=[pl.BlockSpec(block, where) for _, _, block, where in outs],
        ),
        out_shape=[jax.ShapeDtypeStruct(shape, kind) for shape, kind, _, _ in outs],
        compiler_params=pltpu.CompilerParams(vmem_limit_bytes=VMEM),
        cost_estimate=pl.CostEstimate(flops=1, bytes_accessed=1, transcendentals=0),
    )(place, *[array for array, _, _ in ins], *earlier)


def whole(array):
    zeros = (0,) * array.ndim
    return (array, array.shape, lambda *_: zeros)


def tie_body(value, *refs):
    pass


def tie(value, *earlier):
    return pl.pallas_call(
        tie_body,
        in_specs=[pl.BlockSpec(memory_space=pl.ANY)] * (1 + len(earlier)),
        out_specs=pl.BlockSpec(memory_space=pl.ANY),
        out_shape=jax.ShapeDtypeStruct(value.shape, value.dtype),
        input_output_aliases={0: 0},
        cost_estimate=pl.CostEstimate(flops=1, bytes_accessed=1, transcendentals=0),
    )(value, *earlier)


def ring_gather(shards):
    count = lax.axis_size("dp")
    rows = shards[0].shape[0]
    joined = jnp.zeros((count, len(shards)) + shards[0].shape, shards[0].dtype)
    pairs = [(i, (i - 1) % count) for i in range(count)]
    for step in range(count):
        spot = lax.rem(lax.axis_index("dp") + step, count)
        if step:
            shards = [lax.ppermute(shard, "dp", pairs) for shard in shards]
        for j, shard in enumerate(shards):
            joined = lax.dynamic_update_slice(joined, shard[None, None], (spot, j, 0, 0))
    return joined.reshape((count, len(shards) * rows) + joined.shape[3:])


def ring_scatter(values, wait=None):
    count = lax.axis_size("dp")
    pairs = [(i, (i - 1) % count) for i in range(count)]

    def term(value, step):
        spot = lax.rem(lax.axis_index("dp") + step, count)
        return lax.dynamic_index_in_dim(value, spot, 0, keepdims=False)

    totals = [term(value, 1) for value in values]
    for step in range(1, count):
        arrived = [lax.ppermute(total, "dp", pairs) for total in totals]
        if step == 2 and wait is not None:
            arrived[0] = tie(arrived[0], wait)
        totals = [
            (term(value, step + 1).astype(jnp.float32) + part.astype(jnp.float32)).astype(
                value.dtype
            )
            for value, part in zip(values, arrived)
        ]
    return totals


def row_outs(extent, columns, tile):
    count = lax.axis_size("row")
    rows = extent // count
    return [
        ((rows, columns), kind, (rows, tile), lambda n, c: (0, n))
        for kind in [jnp.float32] + [jnp.bfloat16] * (count - 1)
    ]


def put_rows(total, outs):
    rows = outs[0].shape[0]
    for k, out in enumerate(outs):
        out[...] = total[k * rows : (k + 1) * rows].astype(out.dtype)


def project(rows, block):
    n, _, d, width = block.shape
    half = width // 2
    extent = rows.shape[0]

    def body(c, x, mine, theirs, own, far):
        own[0] = mm(x[...], mine[...].reshape(n * d, half))
        far[0] = mm(x[...], theirs[...].reshape(n * d, half))

    return run(
        body,
        (3,),
        [
            whole(rows),
            (block, (n, 1, d, half), lambda k, c: (0, k, 0, c[0])),
            (block, (n, 1, d, half), lambda k, c: (0, k, 0, 1 - c[0])),
        ],
        [
            ((3, extent, half), jnp.float32, (1, extent, half), lambda k, c: (k, 0, 0)),
            ((3, extent, half), jnp.float32, (1, extent, half), lambda k, c: (k, 0, 0)),
        ],
    )


def mix(own, other, block):
    n, _, d, width = block.shape
    extent, half = own.shape

    def body(c, x, y, mine, theirs, *outs):
        parts = []
        a = mine[...].reshape(n // 2, 2, d // 2, width)
        b = theirs[...].reshape(n // 2, 2, d // 2, width)
        for h in range(2):
            parts.append(
                mm(x[...], a[:, h].reshape(half, width)) + mm(y[...], b[:, h].reshape(half, width))
            )
        put_rows(jnp.concatenate(parts, 1), outs)

    return run(
        body,
        (1,),
        [
            whole(own),
            whole(other),
            (block, (n // 2, 1, d, width), lambda n, c: (c[0], 3, 0, 0)),
            (block, (n // 2, 1, d, width), lambda n, c: (1 - c[0], 3, 0, 0)),
        ],
        row_outs(extent, 2 * width, 2 * width),
    )


def mix_back(own, other, block, far):
    n, _, d, width = block.shape
    extent = own.shape[0]
    half = n * d // 4

    def body(c, x, y, mine, theirs, out):
        a = mine[...].reshape(n // 2, 2, d // 2, width)
        b = theirs[...].reshape(n // 2, 2, d // 2, width)
        total = None
        for h in range(2):
            cols = slice(h * width, (h + 1) * width)
            part = mm(x[:, cols], a[:, h].reshape(half, width), NT) + mm(
                y[:, cols], b[:, h].reshape(half, width), NT
            )
            total = part if total is None else total + part
        out[...] = total.astype(jnp.bfloat16)

    return run(
        body,
        (1,),
        [
            whole(own),
            whole(other),
            (block, (n // 2, 1, d, width), lambda n, c: (c[0], 3, 0, 0)),
            whole(far),
        ],
        [((extent, half), jnp.bfloat16, (extent, half), lambda n, c: (0, 0))],
    )[0]


def piece_order(pieces):
    half = pieces // 2
    return lambda j, c: jnp.where(j < half, c[0] * half + j, (1 - c[0]) * half + j - half)


def widen_send(rows, block, t):
    n, _, d, width = block.shape
    half = width // PART // 2
    extent = rows.shape[0]

    def body(c, x, w, out):
        out[0] = mm(x[...], w[...].reshape(n * d, PART)).astype(jnp.bfloat16)

    return run(
        body,
        (2,),
        [
            whole(rows),
            (block, (n, 1, d, PART), lambda k, c: (0, k, 0, (1 - c[0]) * half + t)),
        ],
        [((2, extent, PART), jnp.bfloat16, (1, extent, PART), lambda k, c: (k, 0, 0))],
    )[0]


def widen(rows, block, arrived, t):
    n, _, d, width = block.shape
    half = width // PART // 2
    extent = rows.shape[0]
    tiles = PART // TILE

    def body(c, x, gate, up, far, kept, out):
        g = mm(x[...], gate[...].reshape(n * d, TILE)) + far[0].astype(jnp.float32)
        u = mm(x[...], up[...].reshape(n * d, TILE)) + far[1].astype(jnp.float32)
        kept[0] = g
        kept[1] = u
        out[...] = (g * jax.nn.sigmoid(g) * u).astype(jnp.bfloat16)

    return run(
        body,
        (tiles,),
        [
            whole(rows),
            (block, (n, 1, d, TILE), lambda i, c: (0, 0, 0, (c[0] * half + t) * tiles + i)),
            (block, (n, 1, d, TILE), lambda i, c: (0, 1, 0, (c[0] * half + t) * tiles + i)),
            (arrived, (2, extent, TILE), lambda i, c: (0, 0, i)),
        ],
        [
            ((2, extent, PART), jnp.float32, (2, extent, TILE), lambda i, c: (0, 0, i)),
            ((extent, PART), jnp.bfloat16, (extent, TILE), lambda i, c: (0, i)),
        ],
    )


def narrow(own, other, pieces, earlier=()):
    count, part, columns = pieces.shape
    half = count // 2
    extent = own[0].shape[0]

    def body(c, *refs):
        xs = refs[:count]
        mine, theirs, *outs = refs[count:]
        total = None
        for j, x in enumerate(xs):
            piece = mm(x[...], (mine if j < half else theirs)[j % half])
            total = piece if total is None else total + piece
        put_rows(total, outs)

    return run(
        body,
        (columns // TILE,),
        [whole(x) for x in own + other]
        + [
            (pieces, (half, part, TILE), lambda n, c: (c[0], 0, n)),
            (pieces, (half, part, TILE), lambda n, c: (1 - c[0], 0, n)),
        ],
        row_outs(extent, columns, TILE),
        earlier,
    )


def narrow_weight(own, other, grads, earlier=()):
    groups = len(grads)
    half = len(own[0])
    extent, part = own[0][0].shape
    columns = grads[0].shape[1]
    order = piece_order(2 * half)
    flat = [x for j in range(2 * half) for x in ([g[j] for g in own] if j < half else [g[j - half] for g in other])]

    def body(c, *refs):
        gs = refs[len(flat) : len(flat) + groups]
        out = refs[-1]
        for j in range(2 * half):

            @pl.when(pl.program_id(0) == j)
            def _(j=j):
                total = None
                for g in range(groups):
                    piece = mm(refs[j * groups + g][...], gs[g][...], TN)
                    total = piece if total is None else total + piece
                out[0] = total.astype(jnp.bfloat16)

    return run(
        body,
        (2 * half,),
        [whole(x) for x in flat] + [whole(g) for g in grads],
        [
            (
                (2 * half, part, columns),
                jnp.bfloat16,
                (1, part, columns),
                lambda i, c: (order(i, c), 0, 0),
            )
        ],
        earlier,
    )[0]


def narrow_back(own, other, parts, far, kept, t, earlier=()):
    count, part, cut = parts[0].shape
    half = count // 2
    extent = own.shape[0]
    tiles = part // TILE

    def body(c, x, y, a_mine, b_mine, a_theirs, b_theirs, saved, out):
        grad = mm(x[:, :cut], a_mine[0], NT) + mm(x[:, cut:], b_mine[0], NT)
        grad = grad + mm(y[:, :cut], a_theirs[0], NT) + mm(y[:, cut:], b_theirs[0], NT)
        gate = saved[0]
        sig = jax.nn.sigmoid(gate)
        out[0] = (grad * saved[1] * sig * (1.0 + gate * (1.0 - sig))).astype(jnp.bfloat16)
        out[1] = (grad * (gate * sig)).astype(jnp.bfloat16)

    return run(
        body,
        (tiles,),
        [whole(own), whole(other)]
        + [
            (block, (1, TILE, block.shape[2]), lambda i, c: (c[0] * half + t, i, 0))
            for block in parts
        ]
        + [(block, (1, TILE, block.shape[2]), lambda i, c: (t, i, 0)) for block in far]
        + [(kept, (2, extent, TILE), lambda i, c: (0, 0, i))],
        [((2, extent, part), jnp.bfloat16, (2, extent, TILE), lambda i, c: (0, 0, i))],
        earlier,
    )[0]


def widen_back(own, other, block, earlier=()):
    n, _, d, width = block.shape
    count = width // PART
    extent = own[0].shape[1]
    group = TILE // d
    order = piece_order(count)

    def body(c, *refs):
        outs = refs[2 * count :]
        total = None
        for x, w in zip(refs[:count], refs[count : 2 * count]):
            for k in range(2):
                piece = mm(x[k], w[:, k].reshape(TILE, PART), NT)
                total = piece if total is None else total + piece
        put_rows(total, outs)

    return run(
        body,
        (n * d // TILE,),
        [whole(x) for x in own + other]
        + [
            (block, (group, 2, d, PART), lambda i, c, j=j: (i, 0, 0, order(j, c)))
            for j in range(count)
        ],
        row_outs(extent, n * d, TILE),
        earlier,
    )


def widen_weight(rows, own, other, shape, earlier=()):
    n, _, d, width = shape
    groups = len(rows)
    half = len(own[0])
    extent, features = rows[0].shape
    group = TILE // d
    order = piece_order(2 * half)
    flat = [x for j in range(2 * half) for x in ([g[j] for g in own] if j < half else [g[j - half] for g in other])]

    def body(c, *refs):
        xs = refs[:groups]
        ys = refs[groups:-1]
        out = refs[-1]
        for j in range(2 * half):

            @pl.when(pl.program_id(1) == j)
            def _(j=j):
                for k in range(2):
                    total = None
                    for g in range(groups):
                        piece = mm(xs[g][...], ys[j * groups + g][k], TN)
                        total = piece if total is None else total + piece
                    out[:, k] = total.astype(jnp.bfloat16).reshape(group, d, PART)

    return run(
        body,
        (features // TILE, 2 * half),
        [(x, (extent, TILE), lambda i, j, c: (0, i)) for x in rows] + [whole(y) for y in flat],
        [
            (
                shape,
                jnp.bfloat16,
                (group, 2, d, PART),
                lambda i, j, c: (i, 0, 0, order(j, c)),
            )
        ],
        earlier,
    )[0]


def project_back(own, other, block, earlier):
    n, _, d, width = block.shape
    half = width // 2
    extent = own.shape[1]
    group = TILE // d

    def body(c, x, y, mine, theirs, *outs):
        total = None
        for a, w in ((x, mine), (y, theirs)):
            for k in range(3):
                piece = mm(a[k], w[:, k].reshape(TILE, half), NT)
                total = piece if total is None else total + piece
        put_rows(total, outs)

    return run(
        body,
        (n * d // TILE,),
        [
            whole(own),
            whole(other),
            (block, (group, 4, d, half), lambda i, c: (i, 0, 0, c[0])),
            (block, (group, 4, d, half), lambda i, c: (i, 0, 0, 1 - c[0])),
        ],
        row_outs(extent, n * d, TILE),
        earlier,
    )


def entry_mixer_weight(rows, own, other, heads, far_heads, grads, shape):
    n, _, d, width = shape
    half = width // 2
    extent, features = rows.shape
    group = TILE // d
    low = jnp.bfloat16
    fine = TILE // 2

    def body(c, x, y, z, a, b, g, first, second):
        for k in range(3):
            out = (first, second)[k // 2]
            mine = mm(x[...], y[k], TN).astype(low).reshape(group, d, half)
            theirs = mm(x[...], z[k], TN).astype(low).reshape(group, d, half)
            for side in range(2):

                @pl.when(c[0] == side)
                def _():
                    out[:, k % 2, :, side * half : (side + 1) * half] = mine
                    out[:, k % 2, :, (1 - side) * half : (2 - side) * half] = theirs

        i = pl.program_id(0)
        for source, first in ((a, c[0] * 2), (b, (1 - c[0]) * 2)):
            for j in range(2):

                @pl.when(i == first + j)
                def _():
                    piece = mm(source[:, j * fine : (j + 1) * fine], g[...], TN).astype(low)
                    for h in range(2):
                        second[:, 1, h * (d // 2) : (h + 1) * (d // 2), :] = piece[
                            :, h * width : (h + 1) * width
                        ].reshape(group, d // 2, width)

    return run(
        body,
        (features // TILE,),
        [(rows, (extent, TILE), lambda i, c: (0, i))]
        + [whole(v) for v in (own, other, heads, far_heads, grads)],
        [((n, 2, d, width), low, (group, 2, d, width), lambda i, c: (i, 0, 0, 0))] * 2,
    )


def take_half(block, axis, which):
    half = block.shape[axis] // 2
    return lax.dynamic_slice_in_dim(block, which * half, half, axis)


def gather_shards(shard):
    return lax.all_gather(shard, "dp", axis=0, tiled=True)


def scatter_shards(values):
    return lax.psum_scatter(values, "dp", scatter_dimension=0, tiled=True)


def adam_values(weight, gradient, moment, square, step_rate):
    moment_new, square_new, updated = adam_step(
        weight, gradient, moment, square, step_rate, WEIGHT_DECAY
    )
    return (gradient, moment_new, square_new, updated)


def adam_call(body, grid, gradients, state, block, where, earlier=()):
    return run(
        body,
        grid,
        gradients + [(array, block, where) for array in state],
        [(state[0].shape, jnp.float32, block, where)] * 4,
        earlier,
    )


def adam_rows(gradient, first, blocks, state, step_rate, earlier=()):
    d = state[0].shape[-2] // (blocks if state[0].ndim == 2 else 1)
    width = state[0].shape[-1]
    lead = (1,) * (state[0].ndim - 2)

    def body(c, g, weight, moment, square, *outs):
        value = g[...].astype(jnp.float32).reshape(weight.shape)
        for out, result in zip(
            outs, adam_values(weight[...], value, moment[...], square[...], step_rate)
        ):
            out[...] = result

    return adam_call(
        body,
        (blocks,),
        [(gradient, (d, width), lambda k, c: (first + k, 0))],
        state,
        lead + (d, width),
        (lambda k, c: (k, 0, 0)) if lead else (lambda k, c: (k, 0)),
        earlier,
    )


def adam_halves(gradient, first, state, step_rate):
    rows, width = state[0].shape
    block = (rows, width // 2)

    def body(c, g, weight, moment, square, *outs):
        value = g[...].astype(jnp.float32)
        for out, result in zip(
            outs, adam_values(weight[...], value, moment[...], square[...], step_rate)
        ):
            out[...] = result

    return adam_call(
        body,
        (2,),
        [(gradient, block, lambda k, c: (first + k, 0))],
        state,
        block,
        lambda k, c: (0, k),
    )


def on_device(
    tokens,
    cotangent,
    seq_lengths,
    gains,
    gain_mean,
    gain_square,
    entry_weight,
    entry_mean,
    entry_square,
    mixer_weight,
    mixer_mean,
    mixer_square,
    expand_weight,
    expand_mean,
    expand_square,
    reduce_weight,
    reduce_mean,
    reduce_square,
):
    low = jnp.bfloat16
    shards = lax.axis_size("dp")
    side = lax.axis_index("col")
    depth, grid_width = entry_weight.shape[1:]
    mixer_rows = mixer_weight.shape[0]
    entry_shard = jnp.concatenate(
        [
            entry_weight.astype(low).reshape(-1, grid_width),
            mixer_weight[:, :grid_width].astype(low),
            mixer_weight[:, grid_width:].astype(low),
        ],
        0,
    )
    if shards > 4:
        entry_block = gather_shards(entry_shard)
    else:
        entry_block = ring_gather([entry_shard[: 2 * depth], entry_shard[2 * depth :]])
    entry_block = entry_block.reshape(shards, 4, depth, grid_width)
    reduce_low = reduce_weight.astype(low)
    expand_low = expand_weight.astype(low)
    expand_block = gather_shards(
        tie(expand_low, entry_block).reshape(-1, expand_low.shape[2])
    )
    expand_block = expand_block.reshape((shards,) + expand_weight.shape)
    cut = reduce_low.shape[1] * 3 // 4
    reduce_first = gather_shards(reduce_low[:, :cut])
    halves = range(2)

    row_size = lax.axis_size("row")
    col_size = lax.axis_size("col")
    local_rows = tokens.shape[0]
    feature_local = tokens.shape[1]
    extent = local_rows * row_size
    row_index = lax.axis_index("row")
    blocks = row_index ^ jnp.arange(row_size, dtype=jnp.int32)
    indices = (
        blocks[:, None] * local_rows + jnp.arange(local_rows, dtype=jnp.int32)[None, :]
    ).reshape(extent)
    segment, positions = layout_info(seq_lengths[0], indices)
    local_valid = (segment[:local_rows] < seq_lengths.shape[1]).astype(jnp.float32)
    head_width = grid_width // col_size
    head_start = (row_index * col_size + lax.axis_index("col")) * head_width
    col_start = lax.axis_index("col") * feature_local
    post_gain = lax.dynamic_slice_in_dim(gains[0:2], col_start, feature_local, 1)
    head_gain = lax.dynamic_slice_in_dim(gains[2:4], head_start, head_width, 1)
    head_count = head_width // HD
    shrink = HD ** (-0.5)
    inputs = tokens.astype(jnp.float32)
    token_rows = gather_rows(tokens)
    projected, projected_far = project(token_rows, entry_block)
    projected = projected + swap_col(projected_far)
    squares = grid_total(jnp.sum(projected[0:2] * projected[0:2], -1))
    query_scale = lax.rsqrt(squares[0] / D + NORM_EPSILON)[:, None]
    key_scale = lax.rsqrt(squares[1] / D + NORM_EPSILON)[:, None]
    query_hat = projected[0] * query_scale
    key_hat = projected[1] * key_scale
    cosine, sine_table = rotary_tables(positions, HD)
    query_rot = rotate(
        (query_hat * head_gain[0]).reshape(extent, head_count, HD), cosine, sine_table
    ).astype(jnp.bfloat16)
    key_rot = rotate(
        (key_hat * head_gain[1]).reshape(extent, head_count, HD), cosine, sine_table
    ).astype(jnp.bfloat16)
    value_rows = projected[2].astype(jnp.bfloat16).reshape(extent, head_count, HD)
    block_rows = min(512, extent)

    def block_scores(offset):
        query_block = query_rot[offset : offset + block_rows]
        scores = (
            jnp.einsum("qhd,khd->hqk", query_block, key_rot, preferred_element_type=jnp.float32)
            * shrink
        )
        rows_here = indices[offset : offset + block_rows]
        allowed = (segment[offset : offset + block_rows][:, None] == segment[None, :]) & (
            indices[None, :] <= rows_here[:, None]
        )
        return (query_block, jnp.where(allowed[None], scores, -1e30))

    outputs = []
    logsums = []
    for offset in range(0, extent, block_rows):
        query_block, masked = block_scores(offset)
        peak = jnp.max(masked, -1, keepdims=True)
        expo = jnp.exp(masked - peak)
        totals = jnp.sum(expo, -1, keepdims=True)
        shares = (expo / totals).astype(jnp.bfloat16)
        outputs.append(
            jnp.einsum("hqk,khd->qhd", shares, value_rows, preferred_element_type=jnp.float32)
        )
        logsums.append(peak + jnp.log(totals))
    attended = jnp.concatenate(outputs, 0).astype(jnp.bfloat16).reshape(extent, head_width)
    attended_other = swap_col(attended)
    branch = scatter_rows(*mix(attended, attended_other, entry_block))
    branch_scale = lax.rsqrt(feature_total(jnp.sum(branch * branch, -1)) / D + NORM_EPSILON)[
        :, None
    ]
    branch_hat = branch * branch_scale
    hidden = inputs + branch_hat * post_gain[0]
    hidden_rows = gather_rows(hidden.astype(jnp.bfloat16))
    sent = [swap_col(widen_send(hidden_rows, expand_block, t)) for t in halves]
    kept, product = zip(*[widen(hidden_rows, expand_block, sent[t], t) for t in halves])
    product = list(product)
    product_other = [swap_col(value) for value in product]
    reduce_second = gather_shards(tie(reduce_low[:, cut:], reduce_first, *product_other))
    reduce_parts = [
        block.reshape(4, -1, block.shape[1]) for block in (reduce_first, reduce_second)
    ]
    main_own, *main_low = narrow(product, product_other, reduce_parts[0])
    main_arrived = [swap(value, "row", k + 1) for k, value in enumerate(main_low)]
    rest = narrow(product, product_other, reduce_parts[1], main_arrived)
    for value in main_arrived:
        main_own = main_own + value.astype(jnp.float32)
    second = jnp.concatenate([main_own, scatter_rows(*rest)], 1)
    upstream = cotangent.astype(jnp.float32) * local_valid[:, None]
    scaled = upstream * post_gain[1]
    totals = feature_total(
        jnp.stack([jnp.sum(second * second, -1), jnp.sum(scaled * second, -1)])
    )
    second_scale = lax.rsqrt(totals[0] / D + NORM_EPSILON)[:, None]
    second_hat = second * second_scale
    layer_output = hidden + second_hat * post_gain[1]
    gain_second_post = jnp.sum(upstream * second_hat, 0)
    inner_sum = totals[1][:, None] * second_scale
    second_grad = (second_scale * (scaled - second_hat * inner_sum / D)).astype(jnp.bfloat16)
    second_rows = gather_rows(second_grad)
    reduce_sum = narrow_weight([product], [product_other], [second_rows])
    second_other = swap_col(second_rows)
    reduce_far = [swap_col(take_half(part, 0, 1 - side)) for part in reduce_parts]
    gated_grad = [
        narrow_back(
            second_rows, second_other, reduce_parts, reduce_far, kept[t], t, [reduce_sum]
        )
        for t in halves
    ]
    gated_other = [swap_col(value) for value in gated_grad]
    hidden_parts = widen_back(gated_grad, gated_other, expand_block)
    hidden_back = scatter_rows(*hidden_parts)
    expand_sum = widen_weight(
        [hidden_rows], [gated_grad], [gated_other], expand_block.shape, [hidden_parts[1]]
    )
    rate = 2.0 * D ** (-0.5)
    reduce_grad = scatter_shards(reduce_sum.reshape(-1, reduce_low.shape[1]))
    expand_grad = scatter_shards(
        tie(expand_sum, reduce_grad).reshape(-1, expand_low.shape[2])
    )
    reduce_outs = adam_rows(
        reduce_grad, 0, 2, [reduce_weight, reduce_mean, reduce_square], 2.0 * FF ** (-0.5)
    )
    hidden_grad = upstream + hidden_back
    gain_first_post = jnp.sum(hidden_grad * branch_hat, 0)
    scaled = hidden_grad * post_gain[0]
    inner_sum = feature_total(jnp.sum(scaled * branch_hat, -1))
    branch_grad = (branch_scale * (scaled - branch_hat * inner_sum[:, None] / D)).astype(
        jnp.bfloat16
    )
    branch_rows = gather_rows(branch_grad)
    branch_other = swap_col(branch_rows)
    mixer_far = swap_col(take_half(entry_block[:, 3:], 0, 1 - side))
    attended_low = mix_back(branch_rows, branch_other, entry_block, mixer_far).reshape(
        extent, head_count, HD
    )
    query_parts = []
    key_accum = jnp.zeros((extent, head_count, HD), jnp.float32)
    value_accum = jnp.zeros((extent, head_count, HD), jnp.float32)
    for number, offset in enumerate(range(0, extent, block_rows)):
        query_block, masked = block_scores(offset)
        shares = jnp.exp(masked - logsums[number])
        grad_block = attended_low[offset : offset + block_rows]
        flow_grad = jnp.einsum(
            "qhd,khd->hqk", grad_block, value_rows, preferred_element_type=jnp.float32
        )
        row_delta = jnp.sum(shares * flow_grad, -1, keepdims=True)
        score_grad = (shares * (flow_grad - row_delta)).astype(jnp.bfloat16)
        query_parts.append(
            jnp.einsum("hqk,khd->qhd", score_grad, key_rot, preferred_element_type=jnp.float32)
            * shrink
        )
        key_accum = (
            key_accum
            + jnp.einsum(
                "hqk,qhd->khd", score_grad, query_block, preferred_element_type=jnp.float32
            )
            * shrink
        )
        value_accum = value_accum + jnp.einsum(
            "hqk,qhd->khd",
            shares.astype(jnp.bfloat16),
            grad_block,
            preferred_element_type=jnp.float32,
        )
    query_grad = rotate_back(jnp.concatenate(query_parts, 0), cosine, sine_table).reshape(
        extent, head_width
    )
    key_grad = rotate_back(key_accum, cosine, sine_table).reshape(extent, head_width)
    gain_query = jnp.sum(query_grad * query_hat, 0)
    gain_key = jnp.sum(key_grad * key_hat, 0)
    query_scaled = query_grad * head_gain[0]
    key_scaled = key_grad * head_gain[1]
    head_dots = grid_total(
        jnp.stack(
            [jnp.sum(query_scaled * query_hat, -1), jnp.sum(key_scaled * key_hat, -1)]
        )
    )
    query_raw = query_scale * (query_scaled - query_hat * head_dots[0][:, None] / D)
    key_raw = key_scale * (key_scaled - key_hat * head_dots[1][:, None] / D)
    value_grad = value_accum.reshape(extent, head_width)
    projected_grad = jnp.stack([query_raw, key_raw, value_grad]).astype(low)
    projected_other = swap_col(projected_grad)
    gain_local = jnp.zeros((4, D), jnp.float32)
    gain_local = lax.dynamic_update_slice(
        gain_local, jnp.stack([gain_first_post, gain_second_post]), (0, col_start)
    )
    gain_local = lax.dynamic_update_slice(
        gain_local, jnp.stack([gain_query, gain_key]), (2, head_start)
    )
    gain_local = axes_total(gain_local, ("dp",))
    entry_sum = entry_mixer_weight(
        token_rows,
        projected_grad,
        projected_other,
        attended,
        attended_other,
        branch_rows,
        entry_block.shape,
    )
    expand_outs = adam_rows(
        expand_grad, 0, 2, [expand_weight, expand_mean, expand_square], rate
    )
    if shards > 4:
        joined = jnp.concatenate(entry_sum, 1)
        entry_out = scatter_shards(tie(joined, expand_grad).reshape(-1, grid_width))
    else:
        entry_out = jnp.concatenate(
            ring_scatter([tie(value, gain_local) for value in entry_sum], expand_outs[0]), 0
        ).reshape(-1, grid_width)
    entry_outs = adam_rows(entry_out, 0, 3, [entry_weight, entry_mean, entry_square], rate)
    mixer_outs = adam_halves(
        entry_out,
        3 * depth // mixer_rows,
        [mixer_weight, mixer_mean, mixer_square],
        rate,
    )
    entry_back = scatter_rows(
        *project_back(projected_grad, projected_other, entry_block, [])
    )
    input_grad = hidden_grad + entry_back
    gain_grad = axes_total(gain_local, ("col", "row"))
    gain_momentum, gain_variance, gain_updated = adam_step(
        gains, gain_grad, gain_mean, gain_square, 1.0, 0.0
    )
    return (
        layer_output,
        input_grad,
        gain_grad,
        gain_momentum,
        gain_variance,
        gain_updated,
        *entry_outs,
        *mixer_outs,
        *expand_outs,
        *reduce_outs,
    )


def solution(mesh):
    placed = (
        P(("dp", "row"), "col"),
        P(("dp", "row"), "col"),
        P("dp", None),
        P(),
        P(),
        P(),
        P(None, ("col", "dp"), "row"),
        P(None, ("col", "dp"), "row"),
        P(None, ("col", "dp"), "row"),
        P(("row", "dp"), "col"),
        P(("row", "dp"), "col"),
        P(("row", "dp"), "col"),
        P(None, ("col", "dp"), "row"),
        P(None, ("col", "dp"), "row"),
        P(None, ("col", "dp"), "row"),
        P(("row", "dp"), "col"),
        P(("row", "dp"), "col"),
        P(("row", "dp"), "col"),
    )
    return jax.shard_map(
        on_device,
        mesh=mesh,
        in_specs=placed,
        out_specs=(
            P(("dp", "row"), "col"),
            P(("dp", "row"), "col"),
            P(),
            P(),
            P(),
            P(),
            P(None, ("col", "dp"), "row"),
            P(None, ("col", "dp"), "row"),
            P(None, ("col", "dp"), "row"),
            P(None, ("col", "dp"), "row"),
            P(("row", "dp"), "col"),
            P(("row", "dp"), "col"),
            P(("row", "dp"), "col"),
            P(("row", "dp"), "col"),
            P(None, ("col", "dp"), "row"),
            P(None, ("col", "dp"), "row"),
            P(None, ("col", "dp"), "row"),
            P(None, ("col", "dp"), "row"),
            P(("row", "dp"), "col"),
            P(("row", "dp"), "col"),
            P(("row", "dp"), "col"),
            P(("row", "dp"), "col"),
        ),
        check_vma=False,
    )
```

```python
import jax
import jax.numpy as jnp
from jax import lax
from jax.experimental import pallas as pl
from jax.experimental.pallas import tpu as pltpu
from jax.sharding import PartitionSpec as P

D = 2048
HD = 128
FF = 8192
STEP = 10


NORM_EPSILON = 1e-06
ROPE_BASE = 500000.0
BETA_FIRST = 0.9
BETA_SECOND = 0.95
ADAM_EPSILON = 1e-08
WEIGHT_DECAY = 0.1


def layout_info(lengths, indices):
    closing = jnp.cumsum(lengths)
    starts = closing - lengths
    segment = jnp.sum((indices[:, None] >= closing[None, :]).astype(jnp.int32), 1)
    member = segment[:, None] == jnp.arange(lengths.shape[0], dtype=jnp.int32)[None, :]
    anchor = jnp.sum(jnp.where(member, starts[None, :], 0), 1)
    anchor = jnp.where(segment >= lengths.shape[0], closing[-1], anchor)
    return (segment, indices - anchor)


def rotary_tables(positions, width):
    half_width = width // 2
    freqs = ROPE_BASE ** (-jnp.arange(half_width, dtype=jnp.float32) * 2.0 / width)
    angles = positions.astype(jnp.float32)[:, None] * freqs[None, :]
    return (jnp.cos(angles), jnp.sin(angles))


def rotate(values, cosine, sine_table):
    half_width = values.shape[-1] // 2
    first = values[..., :half_width]
    second = values[..., half_width:]
    cos_wide = cosine[:, None, :]
    sin_wide = sine_table[:, None, :]
    return jnp.concatenate(
        [first * cos_wide - second * sin_wide, second * cos_wide + first * sin_wide], -1
    )


def rotate_back(values, cosine, sine_table):
    half_width = values.shape[-1] // 2
    first = values[..., :half_width]
    second = values[..., half_width:]
    cos_wide = cosine[:, None, :]
    sin_wide = sine_table[:, None, :]
    return jnp.concatenate(
        [first * cos_wide + second * sin_wide, second * cos_wide - first * sin_wide], -1
    )


def adam_step(weight, gradient, moment, square, step_rate, decay_rate):
    moment_new = BETA_FIRST * moment + (1.0 - BETA_FIRST) * gradient
    square_new = BETA_SECOND * square + (1.0 - BETA_SECOND) * gradient * gradient
    ratio = (
        moment_new
        / (1.0 - BETA_FIRST**STEP)
        / (jnp.sqrt(square_new / (1.0 - BETA_SECOND**STEP)) + ADAM_EPSILON)
    )
    return (moment_new, square_new, weight - step_rate * (ratio + decay_rate * weight))


def swap(values, axis, distance):
    return lax.ppermute(values, axis, [(i, i ^ distance) for i in range(lax.axis_size(axis))])


def swap_col(values):
    return swap(values, "col", 1)


def feature_total(values):
    return values + swap_col(values)


def grid_total(values):
    values = feature_total(values)
    count = lax.axis_size("row")
    blocks = values.reshape(values.shape[0], count, -1)
    total = blocks
    for k in range(1, count):
        part = swap(blocks, "row", k)
        total = total + jnp.stack([part[:, j ^ k] for j in range(count)], 1)
    return total.reshape(values.shape)


def axes_total(values, axes):
    for axis in axes:
        distance = 1
        while distance < lax.axis_size(axis):
            values = values + swap(values, axis, distance)
            distance *= 2
    return values


def gather_rows(block):
    count = lax.axis_size("row")
    if count != 4:
        return jnp.concatenate([block] + [swap(block, "row", k) for k in range(1, count)], 0)
    half = block.shape[0] // 2
    first = swap(block, "row", 1)
    second = swap(block, "row", 2)
    return jnp.concatenate(
        [block, first, second, swap(first[:half], "row", 2), swap(second[half:], "row", 1)], 0
    )


def scatter_rows(own, *lows):
    for k, low in enumerate(lows):
        own = own + swap(low, "row", k + 1).astype(jnp.float32)
    return own


VMEM = 48 * 1024 * 1024
TILE = 256
PART = 512
NN = (((1,), (0,)), ((), ()))
NT = (((1,), (1,)), ((), ()))
TN = (((0,), (0,)), ((), ()))


def mm(left, right, dims=NN):
    return lax.dot_general(left, right, dims, preferred_element_type=jnp.float32)


def run(body, grid, ins, outs, earlier=()):
    place = lax.axis_index("col").astype(jnp.int32).reshape(1)

    def kernel(c, *refs):
        body(c, *refs[: len(ins)], *refs[len(ins) + len(earlier) :])

    return pl.pallas_call(
        kernel,
        grid_spec=pltpu.PrefetchScalarGridSpec(
            num_scalar_prefetch=1,
            grid=grid,
            in_specs=[pl.BlockSpec(block, where) for _, block, where in ins]
            + [pl.BlockSpec(memory_space=pl.ANY)] * len(earlier),
            out_specs=[pl.BlockSpec(block, where) for _, _, block, where in outs],
        ),
        out_shape=[jax.ShapeDtypeStruct(shape, kind) for shape, kind, _, _ in outs],
        compiler_params=pltpu.CompilerParams(vmem_limit_bytes=VMEM),
        cost_estimate=pl.CostEstimate(flops=1, bytes_accessed=1, transcendentals=0),
    )(place, *[array for array, _, _ in ins], *earlier)


def whole(array):
    zeros = (0,) * array.ndim
    return (array, array.shape, lambda *_: zeros)


def tie_body(value, *refs):
    pass


def tie(value, *earlier):
    return pl.pallas_call(
        tie_body,
        in_specs=[pl.BlockSpec(memory_space=pl.ANY)] * (1 + len(earlier)),
        out_specs=pl.BlockSpec(memory_space=pl.ANY),
        out_shape=jax.ShapeDtypeStruct(value.shape, value.dtype),
        input_output_aliases={0: 0},
        cost_estimate=pl.CostEstimate(flops=1, bytes_accessed=1, transcendentals=0),
    )(value, *earlier)


def ring_gather(shards):
    count = lax.axis_size("dp")
    rows = shards[0].shape[0]
    joined = jnp.zeros((count, len(shards)) + shards[0].shape, shards[0].dtype)
    pairs = [(i, (i - 1) % count) for i in range(count)]
    for step in range(count):
        spot = lax.rem(lax.axis_index("dp") + step, count)
        if step:
            shards = [lax.ppermute(shard, "dp", pairs) for shard in shards]
        for j, shard in enumerate(shards):
            joined = lax.dynamic_update_slice(joined, shard[None, None], (spot, j, 0, 0))
    return joined.reshape((count, len(shards) * rows) + joined.shape[3:])


def ring_scatter(values, wait=None):
    count = lax.axis_size("dp")
    pairs = [(i, (i - 1) % count) for i in range(count)]

    def term(value, step):
        spot = lax.rem(lax.axis_index("dp") + step, count)
        return lax.dynamic_index_in_dim(value, spot, 0, keepdims=False)

    totals = [term(value, 1) for value in values]
    for step in range(1, count):
        arrived = [lax.ppermute(total, "dp", pairs) for total in totals]
        if step == 2 and wait is not None:
            arrived[0] = tie(arrived[0], wait)
        totals = [
            (term(value, step + 1).astype(jnp.float32) + part.astype(jnp.float32)).astype(
                value.dtype
            )
            for value, part in zip(values, arrived)
        ]
    return totals


def row_outs(extent, columns, tile):
    count = lax.axis_size("row")
    rows = extent // count
    return [
        ((rows, columns), kind, (rows, tile), lambda n, c: (0, n))
        for kind in [jnp.float32] + [jnp.bfloat16] * (count - 1)
    ]


def put_rows(total, outs):
    rows = outs[0].shape[0]
    for k, out in enumerate(outs):
        out[...] = total[k * rows : (k + 1) * rows].astype(out.dtype)


def project(rows, block):
    n, _, d, width = block.shape
    half = width // 2
    extent = rows.shape[0]

    def body(c, x, mine, theirs, own, far):
        own[0] = mm(x[...], mine[...].reshape(n * d, half))
        far[0] = mm(x[...], theirs[...].reshape(n * d, half))

    return run(
        body,
        (3,),
        [
            whole(rows),
            (block, (n, 1, d, half), lambda k, c: (0, k, 0, c[0])),
            (block, (n, 1, d, half), lambda k, c: (0, k, 0, 1 - c[0])),
        ],
        [
            ((3, extent, half), jnp.float32, (1, extent, half), lambda k, c: (k, 0, 0)),
            ((3, extent, half), jnp.float32, (1, extent, half), lambda k, c: (k, 0, 0)),
        ],
    )


def mix(own, other, block):
    n, _, d, width = block.shape
    extent, half = own.shape

    def body(c, x, y, mine, theirs, *outs):
        parts = []
        a = mine[...].reshape(n // 2, 2, d // 2, width)
        b = theirs[...].reshape(n // 2, 2, d // 2, width)
        for h in range(2):
            parts.append(
                mm(x[...], a[:, h].reshape(half, width)) + mm(y[...], b[:, h].reshape(half, width))
            )
        put_rows(jnp.concatenate(parts, 1), outs)

    return run(
        body,
        (1,),
        [
            whole(own),
            whole(other),
            (block, (n // 2, 1, d, width), lambda n, c: (c[0], 3, 0, 0)),
            (block, (n // 2, 1, d, width), lambda n, c: (1 - c[0], 3, 0, 0)),
        ],
        row_outs(extent, 2 * width, 2 * width),
    )


def mix_back(own, other, block, far):
    n, _, d, width = block.shape
    extent = own.shape[0]
    half = n * d // 4

    def body(c, x, y, mine, theirs, out):
        a = mine[...].reshape(n // 2, 2, d // 2, width)
        b = theirs[...].reshape(n // 2, 2, d // 2, width)
        total = None
        for h in range(2):
            cols = slice(h * width, (h + 1) * width)
            part = mm(x[:, cols], a[:, h].reshape(half, width), NT) + mm(
                y[:, cols], b[:, h].reshape(half, width), NT
            )
            total = part if total is None else total + part
        out[...] = total.astype(jnp.bfloat16)

    return run(
        body,
        (1,),
        [
            whole(own),
            whole(other),
            (block, (n // 2, 1, d, width), lambda n, c: (c[0], 3, 0, 0)),
            whole(far),
        ],
        [((extent, half), jnp.bfloat16, (extent, half), lambda n, c: (0, 0))],
    )[0]


def piece_order(pieces):
    half = pieces // 2
    return lambda j, c: jnp.where(j < half, c[0] * half + j, (1 - c[0]) * half + j - half)


def widen_send(rows, block, t):
    n, _, d, width = block.shape
    half = width // PART // 2
    extent = rows.shape[0]

    def body(c, x, w, out):
        out[0] = mm(x[...], w[...].reshape(n * d, PART)).astype(jnp.bfloat16)

    return run(
        body,
        (2,),
        [
            whole(rows),
            (block, (n, 1, d, PART), lambda k, c: (0, k, 0, (1 - c[0]) * half + t)),
        ],
        [((2, extent, PART), jnp.bfloat16, (1, extent, PART), lambda k, c: (k, 0, 0))],
    )[0]


def widen(rows, block, arrived, t):
    n, _, d, width = block.shape
    half = width // PART // 2
    extent = rows.shape[0]
    tiles = PART // TILE

    def body(c, x, gate, up, far, kept, out):
        g = mm(x[...], gate[...].reshape(n * d, TILE)) + far[0].astype(jnp.float32)
        u = mm(x[...], up[...].reshape(n * d, TILE)) + far[1].astype(jnp.float32)
        kept[0] = g
        kept[1] = u
        out[...] = (g * jax.nn.sigmoid(g) * u).astype(jnp.bfloat16)

    return run(
        body,
        (tiles,),
        [
            whole(rows),
            (block, (n, 1, d, TILE), lambda i, c: (0, 0, 0, (c[0] * half + t) * tiles + i)),
            (block, (n, 1, d, TILE), lambda i, c: (0, 1, 0, (c[0] * half + t) * tiles + i)),
            (arrived, (2, extent, TILE), lambda i, c: (0, 0, i)),
        ],
        [
            ((2, extent, PART), jnp.float32, (2, extent, TILE), lambda i, c: (0, 0, i)),
            ((extent, PART), jnp.bfloat16, (extent, TILE), lambda i, c: (0, i)),
        ],
    )


def narrow(own, other, pieces, earlier=()):
    count, part, columns = pieces.shape
    half = count // 2
    extent = own[0].shape[0]

    def body(c, *refs):
        xs = refs[:count]
        mine, theirs, *outs = refs[count:]
        total = None
        for j, x in enumerate(xs):
            piece = mm(x[...], (mine if j < half else theirs)[j % half])
            total = piece if total is None else total + piece
        put_rows(total, outs)

    return run(
        body,
        (columns // TILE,),
        [whole(x) for x in own + other]
        + [
            (pieces, (half, part, TILE), lambda n, c: (c[0], 0, n)),
            (pieces, (half, part, TILE), lambda n, c: (1 - c[0], 0, n)),
        ],
        row_outs(extent, columns, TILE),
        earlier,
    )


def narrow_weight(own, other, grads, earlier=()):
    groups = len(grads)
    half = len(own[0])
    extent, part = own[0][0].shape
    columns = grads[0].shape[1]
    order = piece_order(2 * half)
    flat = [x for j in range(2 * half) for x in ([g[j] for g in own] if j < half else [g[j - half] for g in other])]

    def body(c, *refs):
        gs = refs[len(flat) : len(flat) + groups]
        out = refs[-1]
        for j in range(2 * half):

            @pl.when(pl.program_id(0) == j)
            def _(j=j):
                total = None
                for g in range(groups):
                    piece = mm(refs[j * groups + g][...], gs[g][...], TN)
                    total = piece if total is None else total + piece
                out[0] = total.astype(jnp.bfloat16)

    return run(
        body,
        (2 * half,),
        [whole(x) for x in flat] + [whole(g) for g in grads],
        [
            (
                (2 * half, part, columns),
                jnp.bfloat16,
                (1, part, columns),
                lambda i, c: (order(i, c), 0, 0),
            )
        ],
        earlier,
    )[0]


def narrow_back(own, other, parts, far, kept, t, earlier=()):
    count, part, cut = parts[0].shape
    half = count // 2
    extent = own.shape[0]
    tiles = part // TILE

    def body(c, x, y, a_mine, b_mine, a_theirs, b_theirs, saved, out):
        grad = mm(x[:, :cut], a_mine[0], NT) + mm(x[:, cut:], b_mine[0], NT)
        grad = grad + mm(y[:, :cut], a_theirs[0], NT) + mm(y[:, cut:], b_theirs[0], NT)
        gate = saved[0]
        sig = jax.nn.sigmoid(gate)
        out[0] = (grad * saved[1] * sig * (1.0 + gate * (1.0 - sig))).astype(jnp.bfloat16)
        out[1] = (grad * (gate * sig)).astype(jnp.bfloat16)

    return run(
        body,
        (tiles,),
        [whole(own), whole(other)]
        + [
            (block, (1, TILE, block.shape[2]), lambda i, c: (c[0] * half + t, i, 0))
            for block in parts
        ]
        + [(block, (1, TILE, block.shape[2]), lambda i, c: (t, i, 0)) for block in far]
        + [(kept, (2, extent, TILE), lambda i, c: (0, 0, i))],
        [((2, extent, part), jnp.bfloat16, (2, extent, TILE), lambda i, c: (0, 0, i))],
        earlier,
    )[0]


def widen_back(own, other, block, earlier=()):
    n, _, d, width = block.shape
    count = width // PART
    extent = own[0].shape[1]
    group = TILE // d
    order = piece_order(count)

    def body(c, *refs):
        outs = refs[2 * count :]
        total = None
        for x, w in zip(refs[:count], refs[count : 2 * count]):
            for k in range(2):
                piece = mm(x[k], w[:, k].reshape(TILE, PART), NT)
                total = piece if total is None else total + piece
        put_rows(total, outs)

    return run(
        body,
        (n * d // TILE,),
        [whole(x) for x in own + other]
        + [
            (block, (group, 2, d, PART), lambda i, c, j=j: (i, 0, 0, order(j, c)))
            for j in range(count)
        ],
        row_outs(extent, n * d, TILE),
        earlier,
    )


def widen_weight(rows, own, other, shape, earlier=()):
    n, _, d, width = shape
    groups = len(rows)
    half = len(own[0])
    extent, features = rows[0].shape
    group = TILE // d
    order = piece_order(2 * half)
    flat = [x for j in range(2 * half) for x in ([g[j] for g in own] if j < half else [g[j - half] for g in other])]

    def body(c, *refs):
        xs = refs[:groups]
        ys = refs[groups:-1]
        out = refs[-1]
        for j in range(2 * half):

            @pl.when(pl.program_id(1) == j)
            def _(j=j):
                for k in range(2):
                    total = None
                    for g in range(groups):
                        piece = mm(xs[g][...], ys[j * groups + g][k], TN)
                        total = piece if total is None else total + piece
                    out[:, k] = total.astype(jnp.bfloat16).reshape(group, d, PART)

    return run(
        body,
        (features // TILE, 2 * half),
        [(x, (extent, TILE), lambda i, j, c: (0, i)) for x in rows] + [whole(y) for y in flat],
        [
            (
                shape,
                jnp.bfloat16,
                (group, 2, d, PART),
                lambda i, j, c: (i, 0, 0, order(j, c)),
            )
        ],
        earlier,
    )[0]


def project_back(own, other, block, earlier):
    n, _, d, width = block.shape
    half = width // 2
    extent = own.shape[1]
    group = TILE // d

    def body(c, x, y, mine, theirs, *outs):
        total = None
        for a, w in ((x, mine), (y, theirs)):
            for k in range(3):
                piece = mm(a[k], w[:, k].reshape(TILE, half), NT)
                total = piece if total is None else total + piece
        put_rows(total, outs)

    return run(
        body,
        (n * d // TILE,),
        [
            whole(own),
            whole(other),
            (block, (group, 4, d, half), lambda i, c: (i, 0, 0, c[0])),
            (block, (group, 4, d, half), lambda i, c: (i, 0, 0, 1 - c[0])),
        ],
        row_outs(extent, n * d, TILE),
        earlier,
    )


def entry_mixer_weight(rows, own, other, heads, far_heads, grads, shape):
    n, _, d, width = shape
    half = width // 2
    extent, features = rows.shape
    group = TILE // d
    low = jnp.bfloat16
    fine = TILE // 2

    def body(c, x, y, z, a, b, g, first, second):
        for k in range(3):
            out = (first, second)[k // 2]
            mine = mm(x[...], y[k], TN).astype(low).reshape(group, d, half)
            theirs = mm(x[...], z[k], TN).astype(low).reshape(group, d, half)
            for side in range(2):

                @pl.when(c[0] == side)
                def _():
                    out[:, k % 2, :, side * half : (side + 1) * half] = mine
                    out[:, k % 2, :, (1 - side) * half : (2 - side) * half] = theirs

        i = pl.program_id(0)
        for source, first in ((a, c[0] * 2), (b, (1 - c[0]) * 2)):
            for j in range(2):

                @pl.when(i == first + j)
                def _():
                    piece = mm(source[:, j * fine : (j + 1) * fine], g[...], TN).astype(low)
                    for h in range(2):
                        second[:, 1, h * (d // 2) : (h + 1) * (d // 2), :] = piece[
                            :, h * width : (h + 1) * width
                        ].reshape(group, d // 2, width)

    return run(
        body,
        (features // TILE,),
        [(rows, (extent, TILE), lambda i, c: (0, i))]
        + [whole(v) for v in (own, other, heads, far_heads, grads)],
        [((n, 2, d, width), low, (group, 2, d, width), lambda i, c: (i, 0, 0, 0))] * 2,
    )


def take_half(block, axis, which):
    half = block.shape[axis] // 2
    return lax.dynamic_slice_in_dim(block, which * half, half, axis)


def gather_shards(shard):
    return lax.all_gather(shard, "dp", axis=0, tiled=True)


def scatter_shards(values):
    return lax.psum_scatter(values, "dp", scatter_dimension=0, tiled=True)


def adam_values(weight, gradient, moment, square, step_rate):
    moment_new, square_new, updated = adam_step(
        weight, gradient, moment, square, step_rate, WEIGHT_DECAY
    )
    return (gradient, moment_new, square_new, updated)


def adam_call(body, grid, gradients, state, block, where, earlier=()):
    return run(
        body,
        grid,
        gradients + [(array, block, where) for array in state],
        [(state[0].shape, jnp.float32, block, where)] * 4,
        earlier,
    )


def adam_rows(gradient, first, blocks, state, step_rate, earlier=()):
    d = state[0].shape[-2] // (blocks if state[0].ndim == 2 else 1)
    width = state[0].shape[-1]
    lead = (1,) * (state[0].ndim - 2)

    def body(c, g, weight, moment, square, *outs):
        value = g[...].astype(jnp.float32).reshape(weight.shape)
        for out, result in zip(
            outs, adam_values(weight[...], value, moment[...], square[...], step_rate)
        ):
            out[...] = result

    return adam_call(
        body,
        (blocks,),
        [(gradient, (d, width), lambda k, c: (first + k, 0))],
        state,
        lead + (d, width),
        (lambda k, c: (k, 0, 0)) if lead else (lambda k, c: (k, 0)),
        earlier,
    )


def adam_halves(gradient, first, state, step_rate):
    rows, width = state[0].shape
    block = (rows, width // 2)

    def body(c, g, weight, moment, square, *outs):
        value = g[...].astype(jnp.float32)
        for out, result in zip(
            outs, adam_values(weight[...], value, moment[...], square[...], step_rate)
        ):
            out[...] = result

    return adam_call(
        body,
        (2,),
        [(gradient, block, lambda k, c: (first + k, 0))],
        state,
        block,
        lambda k, c: (0, k),
    )


def on_device(
    tokens,
    cotangent,
    seq_lengths,
    gains,
    gain_mean,
    gain_square,
    entry_weight,
    entry_mean,
    entry_square,
    mixer_weight,
    mixer_mean,
    mixer_square,
    expand_weight,
    expand_mean,
    expand_square,
    reduce_weight,
    reduce_mean,
    reduce_square,
):
    low = jnp.bfloat16
    shards = lax.axis_size("dp")
    side = lax.axis_index("col")
    depth, grid_width = entry_weight.shape[1:]
    mixer_rows = mixer_weight.shape[0]
    entry_shard = jnp.concatenate(
        [
            entry_weight.astype(low).reshape(-1, grid_width),
            mixer_weight[:, :grid_width].astype(low),
            mixer_weight[:, grid_width:].astype(low),
        ],
        0,
    )
    if shards > 4:
        entry_block = gather_shards(entry_shard)
    else:
        entry_block = ring_gather([entry_shard[: 2 * depth], entry_shard[2 * depth :]])
    entry_block = entry_block.reshape(shards, 4, depth, grid_width)
    reduce_low = reduce_weight.astype(low)
    expand_low = expand_weight.astype(low)
    expand_block = gather_shards(
        tie(expand_low, entry_block).reshape(-1, expand_low.shape[2])
    )
    expand_block = expand_block.reshape((shards,) + expand_weight.shape)
    cut = reduce_low.shape[1] * 3 // 4
    reduce_first = gather_shards(reduce_low[:, :cut])
    halves = range(2)

    row_size = lax.axis_size("row")
    col_size = lax.axis_size("col")
    local_rows = tokens.shape[0]
    feature_local = tokens.shape[1]
    extent = local_rows * row_size
    row_index = lax.axis_index("row")
    blocks = row_index ^ jnp.arange(row_size, dtype=jnp.int32)
    indices = (
        blocks[:, None] * local_rows + jnp.arange(local_rows, dtype=jnp.int32)[None, :]
    ).reshape(extent)
    segment, positions = layout_info(seq_lengths[0], indices)
    local_valid = (segment[:local_rows] < seq_lengths.shape[1]).astype(jnp.float32)
    head_width = grid_width // col_size
    head_start = (row_index * col_size + lax.axis_index("col")) * head_width
    col_start = lax.axis_index("col") * feature_local
    post_gain = lax.dynamic_slice_in_dim(gains[0:2], col_start, feature_local, 1)
    head_gain = lax.dynamic_slice_in_dim(gains[2:4], head_start, head_width, 1)
    head_count = head_width // HD
    shrink = HD ** (-0.5)
    inputs = tokens.astype(jnp.float32)
    token_rows = gather_rows(tokens)
    projected, projected_far = project(token_rows, entry_block)
    projected = projected + swap_col(projected_far)
    squares = grid_total(jnp.sum(projected[0:2] * projected[0:2], -1))
    query_scale = lax.rsqrt(squares[0] / D + NORM_EPSILON)[:, None]
    key_scale = lax.rsqrt(squares[1] / D + NORM_EPSILON)[:, None]
    query_hat = projected[0] * query_scale
    key_hat = projected[1] * key_scale
    cosine, sine_table = rotary_tables(positions, HD)
    query_rot = rotate(
        (query_hat * head_gain[0]).reshape(extent, head_count, HD), cosine, sine_table
    ).astype(jnp.bfloat16)
    key_rot = rotate(
        (key_hat * head_gain[1]).reshape(extent, head_count, HD), cosine, sine_table
    ).astype(jnp.bfloat16)
    value_rows = projected[2].astype(jnp.bfloat16).reshape(extent, head_count, HD)
    block_rows = min(512, extent)

    def block_scores(offset):
        query_block = query_rot[offset : offset + block_rows]
        scores = (
            jnp.einsum("qhd,khd->hqk", query_block, key_rot, preferred_element_type=jnp.float32)
            * shrink
        )
        rows_here = indices[offset : offset + block_rows]
        allowed = (segment[offset : offset + block_rows][:, None] == segment[None, :]) & (
            indices[None, :] <= rows_here[:, None]
        )
        return (query_block, jnp.where(allowed[None], scores, -1e30))

    outputs = []
    logsums = []
    for offset in range(0, extent, block_rows):
        query_block, masked = block_scores(offset)
        peak = jnp.max(masked, -1, keepdims=True)
        expo = jnp.exp(masked - peak)
        totals = jnp.sum(expo, -1, keepdims=True)
        shares = (expo / totals).astype(jnp.bfloat16)
        outputs.append(
            jnp.einsum("hqk,khd->qhd", shares, value_rows, preferred_element_type=jnp.float32)
        )
        logsums.append(peak + jnp.log(totals))
    attended = jnp.concatenate(outputs, 0).astype(jnp.bfloat16).reshape(extent, head_width)
    attended_other = swap_col(attended)
    branch = scatter_rows(*mix(attended, attended_other, entry_block))
    branch_scale = lax.rsqrt(feature_total(jnp.sum(branch * branch, -1)) / D + NORM_EPSILON)[
        :, None
    ]
    branch_hat = branch * branch_scale
    hidden = inputs + branch_hat * post_gain[0]
    hidden_rows = gather_rows(hidden.astype(jnp.bfloat16))
    sent = [swap_col(widen_send(hidden_rows, expand_block, t)) for t in halves]
    kept, product = zip(*[widen(hidden_rows, expand_block, sent[t], t) for t in halves])
    product = list(product)
    product_other = [swap_col(value) for value in product]
    reduce_second = gather_shards(tie(reduce_low[:, cut:], reduce_first, *product_other))
    reduce_parts = [
        block.reshape(4, -1, block.shape[1]) for block in (reduce_first, reduce_second)
    ]
    main_own, *main_low = narrow(product, product_other, reduce_parts[0])
    main_arrived = [swap(value, "row", k + 1) for k, value in enumerate(main_low)]
    rest = narrow(product, product_other, reduce_parts[1], main_arrived[:2])
    for value in main_arrived:
        main_own = main_own + value.astype(jnp.float32)
    second = jnp.concatenate([main_own, scatter_rows(*rest)], 1)
    upstream = cotangent.astype(jnp.float32) * local_valid[:, None]
    scaled = upstream * post_gain[1]
    totals = feature_total(
        jnp.stack([jnp.sum(second * second, -1), jnp.sum(scaled * second, -1)])
    )
    second_scale = lax.rsqrt(totals[0] / D + NORM_EPSILON)[:, None]
    second_hat = second * second_scale
    layer_output = hidden + second_hat * post_gain[1]
    gain_second_post = jnp.sum(upstream * second_hat, 0)
    inner_sum = totals[1][:, None] * second_scale
    second_grad = (second_scale * (scaled - second_hat * inner_sum / D)).astype(jnp.bfloat16)
    second_rows = gather_rows(second_grad)
    reduce_sum = narrow_weight([product], [product_other], [second_rows])
    second_other = swap_col(second_rows)
    reduce_far = [swap_col(take_half(part, 0, 1 - side)) for part in reduce_parts]
    gated_grad = [
        narrow_back(
            second_rows, second_other, reduce_parts, reduce_far, kept[t], t, [reduce_sum]
        )
        for t in halves
    ]
    gated_other = [swap_col(value) for value in gated_grad]
    hidden_parts = widen_back(gated_grad, gated_other, expand_block)
    hidden_back = scatter_rows(*hidden_parts)
    expand_sum = widen_weight(
        [hidden_rows], [gated_grad], [gated_other], expand_block.shape, [hidden_parts[1]]
    )
    rate = 2.0 * D ** (-0.5)
    reduce_grad = scatter_shards(reduce_sum.reshape(-1, reduce_low.shape[1]))
    expand_grad = scatter_shards(
        tie(expand_sum, reduce_grad).reshape(-1, expand_low.shape[2])
    )
    reduce_outs = adam_rows(
        reduce_grad, 0, 2, [reduce_weight, reduce_mean, reduce_square], 2.0 * FF ** (-0.5)
    )
    hidden_grad = upstream + hidden_back
    gain_first_post = jnp.sum(hidden_grad * branch_hat, 0)
    scaled = hidden_grad * post_gain[0]
    inner_sum = feature_total(jnp.sum(scaled * branch_hat, -1))
    branch_grad = (branch_scale * (scaled - branch_hat * inner_sum[:, None] / D)).astype(
        jnp.bfloat16
    )
    branch_rows = gather_rows(branch_grad)
    branch_other = swap_col(branch_rows)
    mixer_far = swap_col(take_half(entry_block[:, 3:], 0, 1 - side))
    attended_low = mix_back(branch_rows, branch_other, entry_block, mixer_far).reshape(
        extent, head_count, HD
    )
    query_parts = []
    key_accum = jnp.zeros((extent, head_count, HD), jnp.float32)
    value_accum = jnp.zeros((extent, head_count, HD), jnp.float32)
    for number, offset in enumerate(range(0, extent, block_rows)):
        query_block, masked = block_scores(offset)
        shares = jnp.exp(masked - logsums[number])
        grad_block = attended_low[offset : offset + block_rows]
        flow_grad = jnp.einsum(
            "qhd,khd->hqk", grad_block, value_rows, preferred_element_type=jnp.float32
        )
        row_delta = jnp.sum(shares * flow_grad, -1, keepdims=True)
        score_grad = (shares * (flow_grad - row_delta)).astype(jnp.bfloat16)
        query_parts.append(
            jnp.einsum("hqk,khd->qhd", score_grad, key_rot, preferred_element_type=jnp.float32)
            * shrink
        )
        key_accum = (
            key_accum
            + jnp.einsum(
                "hqk,qhd->khd", score_grad, query_block, preferred_element_type=jnp.float32
            )
            * shrink
        )
        value_accum = value_accum + jnp.einsum(
            "hqk,qhd->khd",
            shares.astype(jnp.bfloat16),
            grad_block,
            preferred_element_type=jnp.float32,
        )
    query_grad = rotate_back(jnp.concatenate(query_parts, 0), cosine, sine_table).reshape(
        extent, head_width
    )
    key_grad = rotate_back(key_accum, cosine, sine_table).reshape(extent, head_width)
    gain_query = jnp.sum(query_grad * query_hat, 0)
    gain_key = jnp.sum(key_grad * key_hat, 0)
    query_scaled = query_grad * head_gain[0]
    key_scaled = key_grad * head_gain[1]
    head_dots = grid_total(
        jnp.stack(
            [jnp.sum(query_scaled * query_hat, -1), jnp.sum(key_scaled * key_hat, -1)]
        )
    )
    query_raw = query_scale * (query_scaled - query_hat * head_dots[0][:, None] / D)
    key_raw = key_scale * (key_scaled - key_hat * head_dots[1][:, None] / D)
    value_grad = value_accum.reshape(extent, head_width)
    projected_grad = jnp.stack([query_raw, key_raw, value_grad]).astype(low)
    projected_other = swap_col(projected_grad)
    gain_local = jnp.zeros((4, D), jnp.float32)
    gain_local = lax.dynamic_update_slice(
        gain_local, jnp.stack([gain_first_post, gain_second_post]), (0, col_start)
    )
    gain_local = lax.dynamic_update_slice(
        gain_local, jnp.stack([gain_query, gain_key]), (2, head_start)
    )
    gain_local = axes_total(gain_local, ("dp",))
    entry_sum = entry_mixer_weight(
        token_rows,
        projected_grad,
        projected_other,
        attended,
        attended_other,
        branch_rows,
        entry_block.shape,
    )
    expand_outs = adam_rows(
        expand_grad, 0, 2, [expand_weight, expand_mean, expand_square], rate
    )
    if shards > 4:
        joined = jnp.concatenate(entry_sum, 1)
        entry_out = scatter_shards(tie(joined, expand_grad).reshape(-1, grid_width))
    else:
        entry_out = jnp.concatenate(
            ring_scatter([tie(value, gain_local) for value in entry_sum], expand_outs[0]), 0
        ).reshape(-1, grid_width)
    entry_outs = adam_rows(entry_out, 0, 3, [entry_weight, entry_mean, entry_square], rate)
    mixer_outs = adam_halves(
        entry_out,
        3 * depth // mixer_rows,
        [mixer_weight, mixer_mean, mixer_square],
        rate,
    )
    entry_back = scatter_rows(
        *project_back(projected_grad, projected_other, entry_block, [])
    )
    input_grad = hidden_grad + entry_back
    gain_grad = axes_total(gain_local, ("col", "row"))
    gain_momentum, gain_variance, gain_updated = adam_step(
        gains, gain_grad, gain_mean, gain_square, 1.0, 0.0
    )
    return (
        layer_output,
        input_grad,
        gain_grad,
        gain_momentum,
        gain_variance,
        gain_updated,
        *entry_outs,
        *mixer_outs,
        *expand_outs,
        *reduce_outs,
    )


def solution(mesh):
    placed = (
        P(("dp", "row"), "col"),
        P(("dp", "row"), "col"),
        P("dp", None),
        P(),
        P(),
        P(),
        P(None, ("col", "dp"), "row"),
        P(None, ("col", "dp"), "row"),
        P(None, ("col", "dp"), "row"),
        P(("row", "dp"), "col"),
        P(("row", "dp"), "col"),
        P(("row", "dp"), "col"),
        P(None, ("col", "dp"), "row"),
        P(None, ("col", "dp"), "row"),
        P(None, ("col", "dp"), "row"),
        P(("row", "dp"), "col"),
        P(("row", "dp"), "col"),
        P(("row", "dp"), "col"),
    )
    return jax.shard_map(
        on_device,
        mesh=mesh,
        in_specs=placed,
        out_specs=(
            P(("dp", "row"), "col"),
            P(("dp", "row"), "col"),
            P(),
            P(),
            P(),
            P(),
            P(None, ("col", "dp"), "row"),
            P(None, ("col", "dp"), "row"),
            P(None, ("col", "dp"), "row"),
            P(None, ("col", "dp"), "row"),
            P(("row", "dp"), "col"),
            P(("row", "dp"), "col"),
            P(("row", "dp"), "col"),
            P(("row", "dp"), "col"),
            P(None, ("col", "dp"), "row"),
            P(None, ("col", "dp"), "row"),
            P(None, ("col", "dp"), "row"),
            P(None, ("col", "dp"), "row"),
            P(("row", "dp"), "col"),
            P(("row", "dp"), "col"),
            P(("row", "dp"), "col"),
            P(("row", "dp"), "col"),
        ),
        check_vma=False,
    )
```
